32 devices in a mesh: dp: 8 (over z, x), fsdp: 4 (over y, core).
Axes of the slice: x: 2, y: 2, z: 4, core: 2. Of those that a mesh axis runs over, the one named last changes fastest.
Arguments:
- tokens: bfloat16 [32768, 768], P(('dp', 'fsdp')), may hold values from -6 to 6
- lengths: int32 [32], P(('dp', 'fsdp')), may hold values from 256 to 1024, as said below
- ln1_gain: bfloat16 [768], P(('dp', 'fsdp')), may hold values from 0.5 to 1.5
- ln1_shift: bfloat16 [768], P(('dp', 'fsdp')), may hold values from -1.75 to 1.75
- w_qkv: bfloat16 [768, 2304], P(None, ('dp', 'fsdp')), may hold values from -0.21875 to 0.21875
- w_out: bfloat16 [768, 768], P(('dp', 'fsdp')), may hold values from -2.5 to 2.5
- ln2_gain: bfloat16 [768], P(('dp', 'fsdp')), may hold values from 0.5 to 1.5
- ln2_shift: bfloat16 [768], P(('dp', 'fsdp')), may hold values from -1.75 to 1.75
- w_up: bfloat16 [768, 3072], P(None, ('dp', 'fsdp')), may hold values from -0.21875 to 0.21875
- w_down: bfloat16 [3072, 768], P(('dp', 'fsdp')), may hold values from -0.109375 to 0.109375
- cotangent: float32 [32768, 768], P(('dp', 'fsdp')), may hold values from -6 to 6
Outputs:
- output: bfloat16 [32768, 768], P(('dp', 'fsdp'))
- grad_tokens: float32 [32768, 768], P(('dp', 'fsdp'))
- grad_ln1_gain: float32 [768], P(('dp', 'fsdp'))
- grad_ln1_shift: float32 [768], P(('dp', 'fsdp'))
- grad_w_qkv: float32 [768, 2304], P(None, ('dp', 'fsdp'))
- grad_w_out: float32 [768, 768], P(('dp', 'fsdp'))
- grad_ln2_gain: float32 [768], P(('dp', 'fsdp'))
- grad_ln2_shift: float32 [768], P(('dp', 'fsdp'))
- grad_w_up: float32 [768, 3072], P(None, ('dp', 'fsdp'))
- grad_w_down: float32 [3072, 768], P(('dp', 'fsdp'))
The draws below stay inside these ranges and needn't reach their ends.
Inputs may be any that keep to these rules, and one draw needn't show every extreme that they name: Live tokens of a slot are its first lengths positions; the rest is padding. Some slot has 1024 live tokens and some has 256.
All inputs are finite; a program needn't handle non-finite values.
Results may differ from the reference program's by a relative error of at most 0.011.
Values may be sent and summed in bfloat16 or wider, within the bound.
No kernel may reach another device: no remote copies, remote signals or barrier semaphores. Data moves between devices by JAX's collectives and lax.ppermute only.
A program may use at most 192 MiB of HBM per device.

```python
import jax
import jax.numpy as jnp
from jax import lax

D = 768
HEADS = 12
HEAD = 64
FF = 3072
MAXLEN = 1024
QBLOCK = 512
SEQS = 32
TOKENS = 32768


def draw_lengths(key, part):
    first_key = jax.random.fold_in(key, 11)
    second_key = jax.random.fold_in(key, 23)
    lengths_out = jax.random.randint(first_key, (SEQS,), MAXLEN // 4, MAXLEN + 1, dtype=jnp.int32)
    shuffled = jax.random.permutation(second_key, SEQS)
    lengths_out = lengths_out.at[shuffled[0]].set(MAXLEN)
    lengths_out = lengths_out.at[shuffled[1]].set(MAXLEN // 4)
    return lengths_out


def block_scale(rng, dims, pieces, low, top_value):
    gain = 1.0
    for axis_at, blocks in pieces:
        heights = jax.random.uniform(jax.random.fold_in(jax.random.fold_in(rng, 6), axis_at), (blocks,), jnp.float32, low / len(pieces), top_value / len(pieces))
        gain = gain * jnp.repeat(jnp.exp(heights), dims[axis_at] // blocks).reshape((-1,) + (1,) * (len(dims) - 1 - axis_at))
    return gain


def scatter_about(own_key, extent, scale, limit, shards=(), held_as=jnp.bfloat16):
    drawn = scale * jax.random.normal(own_key, extent, jnp.float32)
    if shards:
        drawn = drawn * block_scale(own_key, extent, shards, -0.22, 0.18)
    return jnp.clip(drawn, -limit, limit).astype(held_as)


def setup_inputs(seed: int = 0) -> dict:
    key_of = jax.random.split(jax.random.key(seed), 12)
    tokens = scatter_about(key_of[0], (TOKENS, D), 1.0, 6.0, ((0, 32),))
    lengths = draw_lengths(jax.random.fold_in(key_of[11], 71), 0)
    ln1_gain = jnp.clip(1.0 + 0.1 * jax.random.normal(key_of[2], (D,), jnp.float32), 0.5, 1.5).astype(jnp.bfloat16)
    ln1_shift = scatter_about(key_of[3], (D,), 0.3, 1.75, ((0, 32),))
    w_qkv = scatter_about(key_of[4], (D, 3 * D), D ** -0.5, 0.21875, ((1, 32),))
    w_out = scatter_about(key_of[5], (D, D), (D // 128) ** -0.5, 2.5, ((0, 32),))
    ln2_gain = jnp.clip(1.0 + 0.1 * jax.random.normal(key_of[6], (D,), jnp.float32), 0.5, 1.5).astype(jnp.bfloat16)
    ln2_shift = scatter_about(key_of[7], (D,), 0.3, 1.75, ((0, 32),))
    w_up = scatter_about(key_of[8], (D, FF), D ** -0.5, 0.21875, ((1, 32),))
    w_down = scatter_about(key_of[9], (FF, D), FF ** -0.5, 0.109375, ((0, 32),))
    cotangent = scatter_about(key_of[10], (TOKENS, D), 1.0, 6.0, ((0, 32),), jnp.float32)
    return {"tokens": tokens, "lengths": lengths, "ln1_gain": ln1_gain, "ln1_shift": ln1_shift, "w_qkv": w_qkv, "w_out": w_out, "ln2_gain": ln2_gain, "ln2_shift": ln2_shift, "w_up": w_up, "w_down": w_down, "cotangent": cotangent}


EPSILON = 1e-05
NEGATIVE = -1e+30

@jax.custom_vjp
def low(v):
    return lax.optimization_barrier(v.astype(jnp.bfloat16)).astype(jnp.float32)

@jax.custom_vjp
def low_back(v):
    return v

def low_keep(v):
    return (low(v), None)

def low_pass(kept, grad):
    return (grad,)

def back_keep(v):
    return (v, None)

def back_low(kept, grad):
    return (low(grad),)
low.defvjp(low_keep, low_pass)
low_back.defvjp(back_keep, back_low)

def layer_norm(values, gain_vec, shift_vec):
    average = lax.optimization_barrier(jnp.mean(values, axis=-1, keepdims=True))
    centred = values - average
    variance = lax.optimization_barrier(jnp.mean(centred * centred, axis=-1, keepdims=True))
    return centred * lax.rsqrt(variance + EPSILON) * gain_vec + shift_vec

def block_attend(queries, keys_all, values_all, length, block_start):
    query_rows = lax.dynamic_slice_in_dim(queries, block_start, QBLOCK, 0)
    scores = low_back(jnp.einsum('qhe,khe->hqk', query_rows, keys_all, precision=lax.Precision.HIGHEST) * HEAD ** (-0.5))
    query_pos = block_start + jnp.arange(QBLOCK, dtype=jnp.int32)
    key_pos = jnp.arange(MAXLEN, dtype=jnp.int32)
    allowed = (key_pos[None, :] <= query_pos[:, None]) & (key_pos[None, :] < length)
    magnitude = jnp.where(allowed[None], jnp.sqrt(scores * scores + 1.0), NEGATIVE)
    row_top = lax.optimization_barrier(jnp.max(magnitude, axis=-1, keepdims=True))
    exp_terms = jnp.exp(magnitude - row_top)
    row_total = lax.optimization_barrier(jnp.sum(exp_terms, axis=-1, keepdims=True))
    weights = low(jnp.tanh(scores) * (exp_terms / row_total))
    return jnp.einsum('hqk,khe->qhe', weights, values_all, precision=lax.Precision.HIGHEST)

def seq_forward(inputs, length, params):
    gain_one, shift_one, w_qkv, w_out, gain_two, shift_two, w_up, w_down = params
    normed_one = low(layer_norm(inputs, gain_one, shift_one))
    mixed = low_back(low(jnp.dot(normed_one, w_qkv, precision=lax.Precision.HIGHEST)))
    queries = mixed[:, :D].reshape(MAXLEN, HEADS, HEAD)
    keys_all = mixed[:, D:2 * D].reshape(MAXLEN, HEADS, HEAD)
    values_all = mixed[:, 2 * D:].reshape(MAXLEN, HEADS, HEAD)

    def one_block(block_start):
        return block_attend(queries, keys_all, values_all, length, block_start)
    starts = jnp.arange(MAXLEN // QBLOCK, dtype=jnp.int32) * QBLOCK
    blocks = lax.map(jax.checkpoint(one_block), starts)
    attended = low_back(low(blocks.reshape(MAXLEN, D)))
    projected = low_back(jnp.dot(attended, w_out, precision=lax.Precision.HIGHEST))
    residual = inputs + projected
    normed_two = low(layer_norm(residual, gain_two, shift_two))
    pre_active = low_back(jnp.dot(normed_two, w_up, precision=lax.Precision.HIGHEST))
    active = low(jax.nn.gelu(pre_active))
    branch_out = low_back(jnp.dot(active, w_down, precision=lax.Precision.HIGHEST))
    return residual + branch_out

def reference(tokens, lengths, ln1_gain, ln1_shift, w_qkv, w_out, ln2_gain, ln2_shift, w_up, w_down, cotangent):
    inputs = tokens.astype(jnp.float32)
    params = tuple((weight.astype(jnp.float32) for weight in (ln1_gain, ln1_shift, w_qkv, w_out, ln2_gain, ln2_shift, w_up, w_down)))

    def forward(inputs_all, params_all):
        grouped = inputs_all.reshape(SEQS, MAXLEN, D)

        def run_one(seq_pair):
            return jax.checkpoint(seq_forward)(seq_pair[0], seq_pair[1], params_all)
        return lax.map(run_one, (grouped, lengths)).reshape(TOKENS, D)
    output, pullback = jax.vjp(forward, inputs, params)
    live = (jnp.arange(MAXLEN, dtype=jnp.int32)[None, :] < lengths[:, None]).reshape(TOKENS, 1)
    grad_out = jnp.where(live, cotangent.astype(jnp.float32), jnp.float32(0.0))
    grad_tokens, grad_params = pullback(grad_out)
    return (output.astype(jnp.bfloat16), grad_tokens, grad_params[0], grad_params[1], grad_params[2], grad_params[3], grad_params[4], grad_params[5], grad_params[6], grad_params[7])
```

```python
import functools
import math

import jax
import jax.numpy as jnp
from jax import lax
from jax.experimental import pallas as pl
from jax.experimental.pallas import tpu as pltpu
from jax.sharding import PartitionSpec as P

F32 = jnp.float32
BF16 = jnp.bfloat16
HEAD = 64
PAIR = 2 * HEAD
EPSILON = 1e-05
NEGATIVE = -1e30
TILE = 256
AXES = ("dp", "fsdp")
VMEM_LIMIT = 56 << 20
GELU_A = math.sqrt(2.0 / math.pi)
GELU_B = GELU_A * 0.044715


def mm_nn(left, right):
    return jnp.dot(left, right, preferred_element_type=F32)


def mm_nt(left, right):
    return lax.dot_general(left, right, (((1,), (1,)), ((), ())), preferred_element_type=F32)


def mm_tn(left, right):
    return lax.dot_general(left, right, (((0,), (0,)), ((), ())), preferred_element_type=F32)


def norm_stats(values):
    average = jnp.mean(values, axis=-1, keepdims=True)
    centred = values - average
    variance = jnp.mean(centred * centred, axis=-1, keepdims=True)
    rinv = lax.rsqrt(variance + EPSILON)
    return centred * rinv, rinv


def params(**kw):
    return pltpu.CompilerParams(vmem_limit_bytes=VMEM_LIMIT, **kw)


class Plan:
    def __init__(self, mesh):
        self.n = mesh.shape["dp"] * mesh.shape["fsdp"]
        self.bits = self.n.bit_length() - 1
        self.direct = self.n == 1 << self.bits and 4 <= self.bits <= 5
        self.stages = [tuple(range(3, self.bits)), (1, 2)]

    @staticmethod
    def masks_of(bits):
        found = [0]
        for bit in bits:
            found = found + [m | 1 << bit for m in found]
        return found

    def slot_masks(self):
        masks = [0]
        for stage in self.stages:
            masks = [m ^ k for m in self.masks_of(stage) for k in masks]
        return masks

    def swap(self, value, mask):
        return lax.ppermute(value, AXES, [(i, i ^ mask) for i in range(self.n)])

    def gather(self, piece):
        held = piece[None]
        for stage in self.stages:
            masks = self.masks_of(stage)
            held = jnp.concatenate([held] + [self.swap(held, m) for m in masks[1:]], axis=0)
        return held, self.swap(held, 1)

    def scatter(self, keep, send):
        held = add_low(keep, [self.swap(send, 1)])
        for stage in reversed(self.stages):
            masks = self.masks_of(stage)
            parts = jnp.split(held, len(masks), axis=0)
            held = add_low(parts[0], [self.swap(p, m) for p, m in zip(parts[1:], masks[1:])])
        return held[0]


def add_low(first, others):
    total = first.astype(F32)
    for other in others:
        total = total + other.astype(F32)
    return total.astype(first.dtype)


def slot_of(masks, me, piece_pair):
    wanted = piece_pair ^ lax.div(me, 2)
    slot = jnp.int32(0)
    for s, m in enumerate(masks):
        slot = jnp.where(wanted == m // 2, s, slot)
    return slot


def qkv_kernel(masks, ppr, me_ref, x_ref, own_ref, sib_ref, e_ref, m_ref, mixed_ref, n1_ref, w_ref, vec_ref):
    me = me_ref[0]

    @pl.when(pl.program_id(0) == 0)
    def _():
        core = lax.rem(me, 2)
        for s, m in enumerate(masks):
            pair = lax.div(me, 2) ^ (m // 2)
            at = pl.ds(pl.multiple_of(pair * (2 * ppr), 16), 2 * ppr)

            @pl.when(core == 0)
            def _():
                w_ref[at, :] = jnp.concatenate([own_ref[s, :ppr, :], sib_ref[s, :ppr, :]], axis=0)

            @pl.when(core == 1)
            def _():
                w_ref[at, :] = jnp.concatenate([sib_ref[s, :ppr, :], own_ref[s, :ppr, :]], axis=0)

        packed = jnp.concatenate(
            [own_ref[:, ppr, :128].astype(F32), sib_ref[:, ppr, :128].astype(F32)], axis=0
        )
        for v in range(4):
            spread = jnp.dot(packed, e_ref[v], preferred_element_type=F32, precision=lax.Precision.HIGHEST)
            vec_ref[v : v + 1, :] = jnp.sum(spread * m_ref[...], axis=0, keepdims=True)

    xhat, rinv = norm_stats(x_ref[...].astype(F32))
    n1 = (xhat * vec_ref[0:1, :] + vec_ref[1:2, :]).astype(BF16)
    n1_ref[...] = n1
    mixed_ref[...] = mm_nt(n1, w_ref[...]).astype(BF16)


def qkv_project(plan, me, tokens, own, sib, spread, place, out_cols, rows_block=256):
    rows, width = tokens.shape
    masks = plan.slot_masks()
    full = lambda a: pl.BlockSpec(a.shape, lambda r, *_: (0,) * a.ndim)
    whole = lambda shape: pl.BlockSpec(shape, lambda r, *_: (0,) * len(shape))
    return pl.pallas_call(
        functools.partial(qkv_kernel, masks, out_cols // plan.n),
        grid_spec=pltpu.PrefetchScalarGridSpec(
            num_scalar_prefetch=1,
            grid=(rows // rows_block,),
            in_specs=[
                pl.BlockSpec((rows_block, width), lambda r, *_: (r, 0)),
                full(own), full(sib), full(spread), full(place),
            ],
            out_specs=[
                pl.BlockSpec((rows_block, out_cols), lambda r, *_: (r, 0)),
                pl.BlockSpec((rows_block, width), lambda r, *_: (r, 0)),
                whole((out_cols, width)), whole((8, width)),
            ],
        ),
        out_shape=[
            jax.ShapeDtypeStruct((rows, out_cols), BF16),
            jax.ShapeDtypeStruct((rows, width), BF16),
            jax.ShapeDtypeStruct((out_cols, width), BF16),
            jax.ShapeDtypeStruct((8, width), F32),
        ],
        compiler_params=params(),
        name="qkv_project",
    )(me, tokens, own, sib, spread, place)


def qkv_plain_kernel(x_ref, w_ref, vec_ref, mixed_ref, n1_ref):
    xhat, rinv = norm_stats(x_ref[...].astype(F32))
    n1 = (xhat * vec_ref[0:1, :] + vec_ref[1:2, :]).astype(BF16)
    n1_ref[...] = n1
    mixed_ref[...] = mm_nt(n1, w_ref[...]).astype(BF16)


def qkv_plain(tokens, w_abs, vecs, rows_block=256):
    rows, width = tokens.shape
    out_cols = w_abs.shape[0]
    full = lambda a: pl.BlockSpec(a.shape, lambda r: (0,) * a.ndim)
    return pl.pallas_call(
        qkv_plain_kernel,
        grid=(rows // rows_block,),
        in_specs=[pl.BlockSpec((rows_block, width), lambda r: (r, 0)), full(w_abs), full(vecs)],
        out_specs=[
            pl.BlockSpec((rows_block, out_cols), lambda r: (r, 0)),
            pl.BlockSpec((rows_block, width), lambda r: (r, 0)),
        ],
        out_shape=[
            jax.ShapeDtypeStruct((rows, out_cols), BF16),
            jax.ShapeDtypeStruct((rows, width), BF16),
        ],
        compiler_params=params(),
        name="qkv_plain",
    )(tokens, w_abs, vecs)


def attend_kernel(maxlen, len_ref, q_ref, k_ref, v_ref, att_ref, attT_ref, lse_ref):
    length = len_ref[pl.program_id(0)]
    qT = (q_ref[...].astype(F32) * HEAD**-0.5).T.astype(BF16)
    vT = v_ref[...].astype(F32).T.astype(BF16)
    k = k_ref[...]
    for i in range(maxlen // TILE):
        lo, hi = i * TILE, (i + 1) * TILE
        qpos = lo + lax.broadcasted_iota(jnp.int32, (1, TILE), 1)
        limit = jnp.minimum(qpos, length - 1)
        kpos = lax.broadcasted_iota(jnp.int32, (hi, TILE), 0)
        blank = jnp.zeros((HEAD, TILE), BF16)
        outs = []
        for h in range(2):
            own = qT[h * HEAD : (h + 1) * HEAD, lo:hi]
            own = jnp.concatenate([own, blank] if h == 0 else [blank, own], axis=0)
            s = mm_nn(k[:hi], own)
            t = s * s + 1.0
            magnitude = jnp.where(kpos <= limit, t * lax.rsqrt(t), NEGATIVE)
            top = jnp.max(magnitude, axis=0, keepdims=True)
            e = jnp.exp(magnitude - top)
            total = jnp.sum(e, axis=0, keepdims=True)
            weights = (jnp.tanh(s) * e).astype(BF16)
            outs.append(mm_nn(vT[h * HEAD : (h + 1) * HEAD, :hi], weights) / total)
            lse_ref[0, h : h + 1, lo:hi] = jnp.where(qpos >= length, -NEGATIVE, top + jnp.log(total))
        outT = jnp.concatenate(outs, axis=0)
        attT_ref[:, lo:hi] = outT.astype(BF16)
        att_ref[lo:hi, :] = outT.T.astype(BF16)


def attend_forward(mixed, lengths):
    rows, width = mixed.shape[0], mixed.shape[1] // 3
    seqs = lengths.shape[0]
    maxlen, pairs = rows // seqs, width // PAIR
    col = lambda part: pl.BlockSpec((maxlen, PAIR), lambda s, p, *_: (s, part * pairs + p))
    return pl.pallas_call(
        functools.partial(attend_kernel, maxlen),
        grid_spec=pltpu.PrefetchScalarGridSpec(
            num_scalar_prefetch=1,
            grid=(seqs, pairs),
            in_specs=[col(0), col(1), col(2)],
            out_specs=[
                col(0),
                pl.BlockSpec((PAIR, maxlen), lambda s, p, *_: (p, s)),
                pl.BlockSpec((1, 8, maxlen), lambda s, p, *_: (s * pairs + p, 0, 0)),
            ],
        ),
        out_shape=[
            jax.ShapeDtypeStruct((rows, width), BF16),
            jax.ShapeDtypeStruct((width, rows), BF16),
            jax.ShapeDtypeStruct((seqs * pairs, 8, maxlen), F32),
        ],
        compiler_params=params(),
        name="attend_forward",
    )(lengths, mixed, mixed, mixed)


def attend_back_kernel(maxlen, q_ref, k_ref, v_ref, ga_ref, attT_ref, lse_ref, dq_ref, dk_ref, dv_ref, dqT):
    qs = q_ref[...] * jnp.asarray(HEAD**-0.5, BF16)
    k, v, ga = k_ref[...], v_ref[...], ga_ref[...]
    qT = qs.astype(F32).T.astype(BF16)
    kT = k.astype(F32).T.astype(BF16)
    gaT32 = ga.astype(F32).T
    gaT = gaT32.astype(BF16)
    prod = gaT32 * attT_ref[...].astype(F32)
    lane = lax.broadcasted_iota(jnp.int32, (maxlen, PAIR), 1)
    blank = jnp.zeros((HEAD, maxlen), BF16)
    nil = jnp.zeros((), BF16)
    heads = []
    for h in range(2):
        mine = (lane < HEAD) if h == 0 else (lane >= HEAD)
        at = slice(h * HEAD, (h + 1) * HEAD)
        pad = lambda a: jnp.concatenate([a, blank] if h == 0 else [blank, a], axis=0)
        heads.append(
            (
                jnp.where(mine, ga, nil), jnp.where(mine, qs, nil), pad(qT[at]), pad(gaT[at]), kT[at],
                jnp.sum(prod[at], axis=0, keepdims=True), lse_ref[0, h : h + 1, :],
            )
        )
    for j in range(maxlen // TILE):
        lo, hi = j * TILE, (j + 1) * TILE
        dv = dk = None
        for h in range(2):
            ga_h, q_h, qT_h, gaT_h, kT_h, delta, lse = heads[h]
            s = mm_nn(k[lo:hi], qT_h[:, lo:])
            gw = mm_nn(v[lo:hi], gaT_h[:, lo:])
            t = s * s + 1.0
            r = lax.rsqrt(t)
            p = jnp.exp(t * r - lse[:, lo:])
            kpos = lax.broadcasted_iota(jnp.int32, s.shape, 0)
            qpos = lax.broadcasted_iota(jnp.int32, s.shape, 1)
            p = jnp.where(kpos <= qpos, p, 0.0)
            g = jnp.tanh(s)
            w = g * p
            c = p * (s * r)
            a = p + g * (c - w)
            ds = (gw * a - c * delta[:, lo:]).astype(BF16)
            dv_h = mm_nn(w.astype(BF16), ga_h[lo:])
            dk_h = mm_nn(ds, q_h[lo:])
            dv = dv_h if dv is None else dv + dv_h
            dk = dk_h if dk is None else dk + dk_h
            dq_h = mm_nn(kT_h[:, lo:hi], ds)
            if j == 0:
                dqT[h * HEAD : (h + 1) * HEAD, :] = dq_h
            else:
                dqT[h * HEAD : (h + 1) * HEAD, lo:] += dq_h
        dv_ref[lo:hi, :] = dv.astype(BF16)
        dk_ref[lo:hi, :] = dk.astype(BF16)
    dq_ref[...] = (dqT[...] * HEAD**-0.5).T.astype(BF16)


def attend_backward(mixed, ga, attT, lse, seqs):
    rows, width = mixed.shape[0], mixed.shape[1] // 3
    maxlen, pairs = rows // seqs, width // PAIR
    col = lambda part: pl.BlockSpec((maxlen, PAIR), lambda s, p: (s, part * pairs + p))
    return pl.pallas_call(
        functools.partial(attend_back_kernel, maxlen),
        grid=(seqs, pairs),
        in_specs=[
            col(0), col(1), col(2), col(0),
            pl.BlockSpec((PAIR, maxlen), lambda s, p: (p, s)),
            pl.BlockSpec((1, 8, maxlen), lambda s, p: (s * pairs + p, 0, 0)),
        ],
        out_specs=[col(0)] * 3,
        out_shape=[jax.ShapeDtypeStruct((rows, width), BF16)] * 3,
        scratch_shapes=[pltpu.VMEM((PAIR, maxlen), F32)],
        compiler_params=params(),
        name="attend_backward",
    )(mixed, mixed, mixed, ga, attT, lse)


def project_kernel(att_ref, x_ref, wo_ref, vec_ref, res_ref, n2_ref):
    residual = x_ref[...].astype(F32) + mm_nn(att_ref[...], wo_ref[...])
    res_ref[...] = residual
    xhat, rinv = norm_stats(residual)
    n2_ref[...] = (xhat * vec_ref[2:3, :] + vec_ref[3:4, :]).astype(BF16)


def project_out(att, tokens, wo, vecs, rows_block=256):
    rows, width = tokens.shape
    block = pl.BlockSpec((rows_block, width), lambda r: (r, 0))
    full = lambda a: pl.BlockSpec(a.shape, lambda r: (0,) * a.ndim)
    return pl.pallas_call(
        project_kernel,
        grid=(rows // rows_block,),
        in_specs=[block, block, full(wo), full(vecs)],
        out_specs=[block, block],
        out_shape=[jax.ShapeDtypeStruct((rows, width), F32), jax.ShapeDtypeStruct((rows, width), BF16)],
        compiler_params=params(),
        name="project_out",
    )(att, tokens, wo, vecs)


def live_grad(cot, lengths_ref, maxlen, first_row):
    rows = cot.shape[0]
    at = first_row + lax.broadcasted_iota(jnp.int32, (rows, 1), 0)
    seq = first_row // maxlen
    return jnp.where(at - seq * maxlen < lengths_ref[seq], cot, 0.0)


def mlp_kernel(maxlen, len_ref, n2_ref, res_ref, cot_ref, w_ref, out_ref, gn_ref, gw_ref, gl_s, acc_s):
    step = pl.program_id(0)
    units = w_ref.shape[2]
    rows, width = n2_ref.shape

    @pl.when(step == 0)
    def _():
        for first in range(0, rows, maxlen):
            at = slice(first, first + maxlen)
            gl_s[at, :] = live_grad(cot_ref[at, :], len_ref, maxlen, first).astype(BF16)

    pieces = w_ref.shape[0]
    wu = w_ref[:, 0].reshape(pieces * units, width)
    wd = w_ref[:, 1].reshape(pieces * units, width)
    n2, gl = n2_ref[...], gl_s[...]
    u = mm_nt(n2, wu)
    uu = u * u
    th = jnp.tanh(u * (GELU_A + GELU_B * uu))
    half = 0.5 * u
    act = (half + half * th).astype(BF16)
    slope = 0.5 + 0.5 * th + (half - half * (th * th)) * (GELU_A + (3.0 * GELU_B) * uu)
    gp = (mm_nt(gl, wd) * slope).astype(BF16)
    out = mm_nn(act, wd)
    gn = mm_nn(gp, wu)

    @pl.when(step == 0)
    def _():
        acc_s[...] = out + res_ref[...]
        gn_ref[...] = gn

    @pl.when(step > 0)
    def _():
        acc_s[...] += out
        gn_ref[...] += gn

    gw_ref[:, 0] = mm_tn(gp, n2).astype(BF16).reshape(pieces, units, width)
    gw_ref[:, 1] = mm_tn(act, gl).astype(BF16).reshape(pieces, units, width)

    @pl.when(step == pl.num_programs(0) - 1)
    def _():
        out_ref[...] = acc_s[...].astype(BF16)


def feed_forward(lengths, n2, residual, cot, w):
    rows, width = n2.shape
    pieces, _, units, _ = w.shape
    take = max(1, 768 // units)
    full = lambda: pl.BlockSpec((rows, width), lambda f, *_: (0, 0))
    chunk = pl.BlockSpec((take, 2, units, width), lambda f, *_: (f, 0, 0, 0))
    return pl.pallas_call(
        functools.partial(mlp_kernel, rows // lengths.shape[0]),
        grid_spec=pltpu.PrefetchScalarGridSpec(
            num_scalar_prefetch=1,
            grid=(pieces // take,),
            in_specs=[full(), full(), full(), chunk],
            out_specs=[full(), full(), chunk],
            scratch_shapes=[pltpu.VMEM((rows, width), BF16), pltpu.VMEM((rows, width), F32)],
        ),
        out_shape=[
            jax.ShapeDtypeStruct((rows, width), BF16),
            jax.ShapeDtypeStruct((rows, width), F32),
            jax.ShapeDtypeStruct(w.shape, BF16),
        ],
        compiler_params=params(),
        name="feed_forward",
    )(lengths, n2, residual, cot, w)


def norm_back(grad, xhat, rinv, gain):
    dh = grad * gain
    first = jnp.mean(dh, axis=-1, keepdims=True)
    second = jnp.mean(dh * xhat, axis=-1, keepdims=True)
    return rinv * (dh - first - xhat * second)


def middle_kernel(maxlen, len_ref, gn_ref, res_ref, cot_ref, att_ref, wo_ref, vec_ref, gres_ref, ga_ref, gwo_ref, gvec_ref, acc_s):
    step = pl.program_id(0)
    rows = gn_ref.shape[0]
    gn = gn_ref[...]
    xhat, rinv = norm_stats(res_ref[...])
    gres = live_grad(cot_ref[...], len_ref, maxlen, step * rows) + norm_back(gn, xhat, rinv, vec_ref[2:3, :])
    gres_ref[...] = gres
    low = gres.astype(BF16)
    ga_ref[...] = mm_nt(low, wo_ref[...]).astype(BF16)
    gwo = mm_tn(att_ref[...], low)
    ggain = jnp.sum(gn * xhat, axis=0, keepdims=True)
    gshift = jnp.sum(gn, axis=0, keepdims=True)

    @pl.when(step == 0)
    def _():
        acc_s[...] = gwo
        gvec_ref[...] = jnp.zeros_like(gvec_ref)

    @pl.when(step > 0)
    def _():
        acc_s[...] += gwo

    gvec_ref[0:1, :] += ggain
    gvec_ref[1:2, :] += gshift

    @pl.when(step == pl.num_programs(0) - 1)
    def _():
        gwo_ref[...] = acc_s[...].astype(BF16)


def middle_back(lengths, gn, residual, cot, att, wo, vecs, rows_block=256):
    rows, width = gn.shape
    block = pl.BlockSpec((rows_block, width), lambda r, *_: (r, 0))
    full = lambda shape: pl.BlockSpec(shape, lambda r, *_: (0,) * len(shape))
    return pl.pallas_call(
        functools.partial(middle_kernel, rows // lengths.shape[0]),
        grid_spec=pltpu.PrefetchScalarGridSpec(
            num_scalar_prefetch=1,
            grid=(rows // rows_block,),
            in_specs=[block, block, block, block, full(wo.shape), full(vecs.shape)],
            out_specs=[block, block, full(wo.shape), full((8, width))],
            scratch_shapes=[pltpu.VMEM(wo.shape, F32)],
        ),
        out_shape=[
            jax.ShapeDtypeStruct((rows, width), F32),
            jax.ShapeDtypeStruct((rows, width), BF16),
            jax.ShapeDtypeStruct(wo.shape, BF16),
            jax.ShapeDtypeStruct((8, width), F32),
        ],
        compiler_params=params(),
        name="middle_back",
    )(lengths, gn, residual, cot, att, wo, vecs)


def qkv_grad_kernel(masks, ppr, opr, me_ref, dq_ref, dk_ref, dv_ref, n1_ref, gwo_ref, keep_ref, send_ref, low_s):
    width = n1_ref.shape[1]
    n1 = n1_ref[...]
    for part, ref in enumerate((dq_ref, dk_ref, dv_ref)):
        low_s[part * width : (part + 1) * width, :] = mm_tn(ref[...], n1).astype(BF16)
    me = me_ref[0]
    core = lax.rem(me, 2)
    for pair in range(len(masks)):
        slot = slot_of(masks, me, pair)
        w0 = low_s[2 * pair * ppr : (2 * pair + 1) * ppr, :]
        w1 = low_s[(2 * pair + 1) * ppr : (2 * pair + 2) * ppr, :]
        o0 = gwo_ref[2 * pair * opr : (2 * pair + 1) * opr, :]
        o1 = gwo_ref[(2 * pair + 1) * opr : (2 * pair + 2) * opr, :]
        for side, (own_w, own_o, sib_w, sib_o) in enumerate(((w0, o0, w1, o1), (w1, o1, w0, o0))):

            @pl.when(core == side)
            def _():
                keep_ref[slot] = jnp.concatenate([own_w, own_o], axis=0)
                send_ref[slot] = jnp.concatenate([sib_w, sib_o], axis=0)


def qkv_grad(plan, me, dq, dk, dv, n1, gwo):
    rows, width = n1.shape
    masks = plan.slot_masks()
    ppr, opr = 3 * width // plan.n, width // plan.n
    vm = pl.BlockSpec(memory_space=pltpu.VMEM)
    shape = jax.ShapeDtypeStruct((len(masks), ppr + opr, width), BF16)
    return pl.pallas_call(
        functools.partial(qkv_grad_kernel, masks, ppr, opr),
        in_specs=[pl.BlockSpec(memory_space=pltpu.SMEM)] + [vm] * 5,
        out_specs=[vm, vm],
        out_shape=[shape, shape],
        scratch_shapes=[pltpu.VMEM((3 * width, width), BF16)],
        compiler_params=params(),
        name="qkv_grad",
    )(me, dq, dk, dv, n1, gwo)


def qkv_grad_plain_kernel(d_ref, n1_ref, out_ref):
    out_ref[...] = mm_tn(d_ref[...], n1_ref[...]).astype(BF16)


def qkv_grad_plain(dq, dk, dv, n1):
    rows, width = n1.shape
    vm = pl.BlockSpec(memory_space=pltpu.VMEM)
    call = pl.pallas_call(
        qkv_grad_plain_kernel,
        in_specs=[vm, vm],
        out_specs=vm,
        out_shape=jax.ShapeDtypeStruct((width, width), BF16),
        compiler_params=params(),
        name="qkv_grad_plain",
    )
    return jnp.concatenate([call(d, n1) for d in (dq, dk, dv)], axis=0)


def first_kernel(dq_ref, dk_ref, dv_ref, w_ref, x_ref, gres_ref, vec_ref, gtok_ref, gvec_ref):
    width = x_ref.shape[1]
    gn = mm_nn(dq_ref[...], w_ref[:width, :])
    gn += mm_nn(dk_ref[...], w_ref[width : 2 * width, :])
    gn += mm_nn(dv_ref[...], w_ref[2 * width :, :])
    xhat, rinv = norm_stats(x_ref[...].astype(F32))
    gtok_ref[...] = gres_ref[...] + norm_back(gn, xhat, rinv, vec_ref[0:1, :])

    @pl.when(pl.program_id(0) == 0)
    def _():
        gvec_ref[...] = jnp.zeros_like(gvec_ref)

    gvec_ref[0:1, :] += jnp.sum(gn * xhat, axis=0, keepdims=True)
    gvec_ref[1:2, :] += jnp.sum(gn, axis=0, keepdims=True)


def first_back(dq, dk, dv, w_abs, tokens, gres, vecs, rows_block=256):
    rows, width = tokens.shape
    block = pl.BlockSpec((rows_block, width), lambda r: (r, 0))
    full = lambda shape: pl.BlockSpec(shape, lambda r: (0,) * len(shape))
    return pl.pallas_call(
        first_kernel,
        grid=(rows // rows_block,),
        in_specs=[block, block, block, full(w_abs.shape), block, block, full(vecs.shape)],
        out_specs=[block, full((8, width))],
        out_shape=[jax.ShapeDtypeStruct((rows, width), F32), jax.ShapeDtypeStruct((8, width), F32)],
        compiler_params=params(),
        name="first_back",
    )(dq, dk, dv, w_abs, tokens, gres, vecs)


def body(plan, tokens, lengths, ln1_gain, ln1_shift, w_qkv, w_out, ln2_gain, ln2_shift, w_up, w_down, cot):
    rows, width = tokens.shape
    n = plan.n
    seqs = lengths.shape[0]
    me = lax.axis_index(AXES).astype(jnp.int32)
    me_arr = me[None]
    vec_piece = jnp.stack([ln1_gain, ln1_shift, ln2_gain, ln2_shift])
    per = vec_piece.shape[1]
    qkv_piece = w_qkv.T
    ppr, units = qkv_piece.shape[0], w_down.shape[0]
    ff = units * n

    mlp_piece = jnp.concatenate([w_up.T, w_down, w_out], axis=0)
    mlp_all = lax.all_gather(mlp_piece, AXES, axis=0, tiled=True).reshape(n, -1, width)
    wo = mlp_all[:, 2 * units :].reshape(width, width)
    w_ff = mlp_all[:, : 2 * units].reshape(n, 2, units, width)
    if units % 16 or 768 % units:
        w_ff = w_ff.transpose(1, 0, 2, 3).reshape(2, ff // 768, 768, width).transpose(1, 0, 2, 3)

    if plan.direct:
        flat = jnp.pad(vec_piece.reshape(1, -1), ((0, 7), (0, width - 4 * per)))
        own, sib = plan.gather(jnp.concatenate([qkv_piece, flat], axis=0))
        slots = jnp.array(plan.slot_masks() + [m ^ 1 for m in plan.slot_masks()], jnp.int32)
        column = jnp.arange(width, dtype=jnp.int32)
        place = ((slots ^ me)[:, None] == (column // per)[None]).astype(F32)
        lane = jnp.arange(128, dtype=jnp.int32)
        spread = jnp.stack([(lane[:, None] == v * per + (column % per)[None]).astype(F32) for v in range(4)])
        mixed, n1, w_abs, vecs = qkv_project(plan, me_arr, tokens, own, sib, spread, place, ppr * n)
    else:
        w_abs = lax.all_gather(qkv_piece, AXES, axis=0, tiled=True)
        vecs = lax.all_gather(vec_piece, AXES, axis=1, tiled=True).astype(F32)
        vecs = jnp.pad(vecs, ((0, 4), (0, 0)))
        mixed, n1 = qkv_plain(tokens, w_abs, vecs)

    att, attT, lse = attend_forward(mixed, lengths)
    residual, n2 = project_out(att, tokens, wo, vecs)
    output, gn2, gw_ff = feed_forward(lengths, n2, residual, cot, w_ff)
    if units % 16 or 768 % units:
        gw_ff = gw_ff.transpose(1, 0, 2, 3).reshape(2, n, units, width).transpose(1, 0, 2, 3)
    g_ff = lax.psum_scatter(gw_ff.reshape(n * 2 * units, width), AXES, scatter_dimension=0, tiled=True)
    gres, ga, gwo, gvec2 = middle_back(lengths, gn2, residual, cot, att, wo, vecs)
    dq, dk, dv = attend_backward(mixed, ga, attT, lse, seqs)
    if plan.direct:
        keep, send = qkv_grad(plan, me_arr, dq, dk, dv, n1, gwo)
        g_attn = plan.scatter(keep, send).astype(F32)
        g_qkv, g_out = g_attn[:ppr], g_attn[ppr:]
    else:
        g_qkv = lax.psum_scatter(qkv_grad_plain(dq, dk, dv, n1), AXES, scatter_dimension=0, tiled=True)
        g_out = lax.psum_scatter(gwo, AXES, scatter_dimension=0, tiled=True)
    gtok, gvec1 = first_back(dq, dk, dv, w_abs, tokens, gres, vecs)
    gvec = jnp.concatenate([gvec1[:2], gvec2[:2]], axis=0)
    if plan.direct:
        by_piece = gvec.reshape(4, n, per).transpose(1, 0, 2)
        by_slot = by_piece[slots ^ me]
        half = n // 2
        g_vec = plan.scatter(by_slot[:half], by_slot[half:])
    else:
        g_vec = lax.psum_scatter(gvec, AXES, scatter_dimension=1, tiled=True)
    g_ff = g_ff.astype(F32)
    return (
        output, gtok, g_vec[0], g_vec[1], g_qkv.astype(F32).T, g_out.astype(F32), g_vec[2], g_vec[3],
        g_ff[:units].T, g_ff[units:],
    )


def solution(mesh):
    both = AXES
    rows2, vec, cols2 = P(both, None), P(both), P(None, both)
    in_specs = (rows2, vec, vec, vec, cols2, rows2, vec, vec, cols2, rows2, rows2)
    out_specs = (rows2, rows2, vec, vec, cols2, rows2, vec, vec, cols2, rows2)
    return jax.shard_map(
        functools.partial(body, Plan(mesh)), mesh=mesh, in_specs=in_specs, out_specs=out_specs, check_vma=False
    )
```

```python
import functools
import math

import jax
import jax.numpy as jnp
from jax import lax
from jax.experimental import pallas as pl
from jax.experimental.pallas import tpu as pltpu
from jax.sharding import PartitionSpec as P

F32 = jnp.float32
BF16 = jnp.bfloat16
HEAD = 64
PAIR = 2 * HEAD
EPSILON = 1e-05
NEGATIVE = -1e30
TILE = 256
AXES = ("dp", "fsdp")
VMEM_LIMIT = 56 << 20
GELU_A = math.sqrt(2.0 / math.pi)
GELU_B = GELU_A * 0.044715


def mm_nn(left, right):
    return jnp.dot(left, right, preferred_element_type=F32)


def mm_nt(left, right):
    return lax.dot_general(left, right, (((1,), (1,)), ((), ())), preferred_element_type=F32)


def mm_tn(left, right):
    return lax.dot_general(left, right, (((0,), (0,)), ((), ())), preferred_element_type=F32)


def norm_stats(values):
    average = jnp.mean(values, axis=-1, keepdims=True)
    centred = values - average
    variance = jnp.mean(centred * centred, axis=-1, keepdims=True)
    rinv = lax.rsqrt(variance + EPSILON)
    return centred * rinv, rinv


def params(**kw):
    return pltpu.CompilerParams(vmem_limit_bytes=VMEM_LIMIT, **kw)


def cost(flops, moved):
    return pl.CostEstimate(flops=int(flops), bytes_accessed=int(moved), transcendentals=0)


class Plan:
    def __init__(self, mesh):
        self.n = mesh.shape["dp"] * mesh.shape["fsdp"]
        self.bits = self.n.bit_length() - 1
        self.direct = self.n == 1 << self.bits and self.bits == 5 and mesh.shape["fsdp"] == 4
        self.along = (3, 4)
        self.across = (1, 2)

    @staticmethod
    def masks_of(bits):
        found = [0]
        for bit in bits:
            found = found + [m | 1 << bit for m in found]
        return found

    def slot_masks(self):
        return [m ^ k for m in self.masks_of(self.across) for k in self.masks_of(self.along)]

    def swap(self, value, mask):
        return lax.ppermute(value, AXES, [(i, i ^ mask) for i in range(self.n)])

    def spread_stage(self, held, bits):
        return jnp.concatenate([held] + [self.swap(held, m) for m in self.masks_of(bits)[1:]], axis=0)

    def gather(self, piece):
        held = self.spread_stage(self.spread_stage(piece[None], self.along), self.across)
        return held, self.swap(held, 1)

    def scatter_first(self, keep, send, cut):
        got = self.swap(send, 1)
        outer, inner = len(self.masks_of(self.across)), len(self.masks_of(self.along))
        grid = (outer, inner) + keep.shape[1:]
        keep, got = keep.reshape(grid), got.reshape(grid)
        pair = lambda at: add_low(keep[at], [got[at]])
        head, tail = slice(None, cut), slice(cut, None)
        first = [pair((slice(None), z, head)) for z in range(inner)]
        second = [pair((x, slice(None), tail)) for x in range(outer)]
        return first, second

    def scatter_rest(self, first, second):
        outer, inner = self.masks_of(self.across), self.masks_of(self.along)
        second = add_low(second[0], [self.swap(v, m) for v, m in zip(second[1:], outer[1:])])
        first = add_low(first[0], [self.swap(v, m) for v, m in zip(first[1:], inner[1:])])
        second = add_low(second[0], [self.swap(second[z], m) for z, m in list(enumerate(inner))[1:]])
        first = add_low(first[0], [self.swap(first[x], m) for x, m in list(enumerate(outer))[1:]])
        return jnp.concatenate([first, second], axis=0)

    def view(self, held):
        pieces, rows, width = held.shape
        return held.reshape(pieces // 4, 2, 2, 2, rows // 2, width)

    def first_away(self, keep, got):
        k, g = self.view(keep), self.view(got)
        return add_low(k[:, :, 1, 0], [g[:, :, 1, 0]]), add_low(k[:, 1, :, 1], [g[:, 1, :, 1]])

    def second_away(self, keep, got, back):
        k, g = self.view(keep), self.view(got)
        return (
            add_low(k[:, 1, 0, 0], [g[:, 1, 0, 0], back[0][:, 1]]),
            add_low(k[:, 0, 1, 1], [g[:, 0, 1, 1], back[1][:, 1]]),
        )

    def last_sum(self, keep, got, back, again):
        k, g = self.view(keep), self.view(got)
        both = [
            add_low(k[:, 0, 0, half], [g[:, 0, 0, half], back[half][:, 0], again[half]]) for half in range(2)
        ]
        whole = jnp.concatenate(both, axis=1)
        line = [[r + 8 * z for z in range(self.n // 8)] for r in range(8)]
        whole = whole.reshape(-1, whole.shape[-1])
        return lax.psum_scatter(whole, AXES, scatter_dimension=0, tiled=True, axis_index_groups=line)


def add_low(first, others):
    total = first.astype(F32)
    for other in others:
        total = total + other.astype(F32)
    return total.astype(first.dtype)


def slot_of(masks, me, piece_pair):
    wanted = piece_pair ^ lax.div(me, 2)
    slot = jnp.int32(0)
    for s, m in enumerate(masks):
        slot = jnp.where(wanted == m // 2, s, slot)
    return slot


def qkv_kernel(masks, ppr, me_ref, x_ref, own_ref, sib_ref, e_ref, m_ref, mixed_ref, n1_ref, w_ref, vec_ref):
    me = me_ref[0]

    @pl.when(pl.program_id(0) == 0)
    def _():
        core = lax.rem(me, 2)
        for s, m in enumerate(masks):
            pair = lax.div(me, 2) ^ (m // 2)
            at = pl.ds(pl.multiple_of(pair * (2 * ppr), 16), 2 * ppr)
            both = [own_ref[s, :ppr, :], sib_ref[s, :ppr, :]]
            for side in range(2):

                @pl.when(core == side)
                def _():
                    w_ref[at, :] = jnp.concatenate([both[side], both[1 - side]], axis=0)

        packed = jnp.concatenate([own_ref[:, ppr, :128], sib_ref[:, ppr, :128]], axis=0)
        for v in range(4):
            vec_ref[v : v + 1, :] = jnp.sum(mm_nn(packed, e_ref[v]) * m_ref[...], axis=0, keepdims=True)

    xhat, rinv = norm_stats(x_ref[...].astype(F32))
    n1 = (xhat * vec_ref[0:1, :] + vec_ref[1:2, :]).astype(BF16)
    n1_ref[...] = n1
    mixed_ref[...] = mm_nt(n1, w_ref[...]).astype(BF16)


def qkv_project(plan, me, tokens, gathered, spread, place, out_cols, rows_block=256):
    rows, width = tokens.shape
    masks = plan.slot_masks()
    full = lambda a: pl.BlockSpec(a.shape, lambda r, *_: (0,) * a.ndim)
    whole = lambda shape: pl.BlockSpec(shape, lambda r, *_: (0,) * len(shape))
    return pl.pallas_call(
        functools.partial(qkv_kernel, masks, out_cols // plan.n),
        grid_spec=pltpu.PrefetchScalarGridSpec(
            num_scalar_prefetch=1,
            grid=(rows // rows_block,),
            in_specs=[
                pl.BlockSpec((rows_block, width), lambda r, *_: (r, 0)),
            ]
            + [full(a) for a in (*gathered, spread, place)],
            out_specs=[
                pl.BlockSpec((rows_block, out_cols), lambda r, *_: (r, 0)),
                pl.BlockSpec((rows_block, width), lambda r, *_: (r, 0)),
                whole((out_cols, width)), whole((8, width)),
            ],
        ),
        out_shape=[
            jax.ShapeDtypeStruct((rows, out_cols), BF16),
            jax.ShapeDtypeStruct((rows, width), BF16),
            jax.ShapeDtypeStruct((out_cols, width), BF16),
            jax.ShapeDtypeStruct((8, width), F32),
        ],
        compiler_params=params(),
        cost_estimate=cost(2 * rows * width * out_cols, 20e6),
        name="qkv_project",
    )(me, tokens, *gathered, spread, place)


def qkv_plain_kernel(x_ref, w_ref, vec_ref, mixed_ref, n1_ref):
    xhat, rinv = norm_stats(x_ref[...].astype(F32))
    n1 = (xhat * vec_ref[0:1, :] + vec_ref[1:2, :]).astype(BF16)
    n1_ref[...] = n1
    mixed_ref[...] = mm_nt(n1, w_ref[...]).astype(BF16)


def qkv_plain(tokens, w_abs, vecs, rows_block=256):
    rows, width = tokens.shape
    out_cols = w_abs.shape[0]
    full = lambda a: pl.BlockSpec(a.shape, lambda r: (0,) * a.ndim)
    return pl.pallas_call(
        qkv_plain_kernel,
        grid=(rows // rows_block,),
        in_specs=[pl.BlockSpec((rows_block, width), lambda r: (r, 0)), full(w_abs), full(vecs)],
        out_specs=[
            pl.BlockSpec((rows_block, out_cols), lambda r: (r, 0)),
            pl.BlockSpec((rows_block, width), lambda r: (r, 0)),
        ],
        out_shape=[
            jax.ShapeDtypeStruct((rows, out_cols), BF16),
            jax.ShapeDtypeStruct((rows, width), BF16),
        ],
        compiler_params=params(),
        name="qkv_plain",
    )(tokens, w_abs, vecs)


def attend_kernel(maxlen, len_ref, q_ref, k_ref, v_ref, att_ref, attT_ref, lse_ref):
    length = len_ref[pl.program_id(0)]
    qT = (q_ref[...].astype(F32) * HEAD**-0.5).T.astype(BF16)
    vT = v_ref[...].astype(F32).T.astype(BF16)
    k = k_ref[...]
    for i in range(maxlen // TILE):
        lo, hi = i * TILE, (i + 1) * TILE
        qpos = lo + lax.broadcasted_iota(jnp.int32, (1, TILE), 1)
        limit = jnp.minimum(qpos, length - 1)
        kpos = lax.broadcasted_iota(jnp.int32, (hi, TILE), 0)
        blank = jnp.zeros((HEAD, TILE), BF16)
        outs = []
        for h in range(2):
            own = qT[h * HEAD : (h + 1) * HEAD, lo:hi]
            own = jnp.concatenate([own, blank] if h == 0 else [blank, own], axis=0)
            s = mm_nn(k[:hi], own)
            t = s * s + 1.0
            magnitude = jnp.where(kpos <= limit, t * lax.rsqrt(t), NEGATIVE)
            top = jnp.max(magnitude, axis=0, keepdims=True)
            e = jnp.exp(magnitude - top)
            total = jnp.sum(e, axis=0, keepdims=True)
            weights = (jnp.tanh(s) * e).astype(BF16)
            outs.append(mm_nn(vT[h * HEAD : (h + 1) * HEAD, :hi], weights) / total)
            lse_ref[0, h : h + 1, lo:hi] = jnp.where(qpos >= length, -NEGATIVE, top + jnp.log(total))
        outT = jnp.concatenate(outs, axis=0)
        attT_ref[:, lo:hi] = outT.astype(BF16)
        att_ref[lo:hi, :] = outT.T.astype(BF16)


def attend_forward(mixed, lengths):
    rows, width = mixed.shape[0], mixed.shape[1] // 3
    seqs = lengths.shape[0]
    maxlen, pairs = rows // seqs, width // PAIR
    col = lambda part: pl.BlockSpec((maxlen, PAIR), lambda s, p, *_: (s, part * pairs + p))
    return pl.pallas_call(
        functools.partial(attend_kernel, maxlen),
        grid_spec=pltpu.PrefetchScalarGridSpec(
            num_scalar_prefetch=1,
            grid=(seqs, pairs),
            in_specs=[col(0), col(1), col(2)],
            out_specs=[
                col(0),
                pl.BlockSpec((PAIR, maxlen), lambda s, p, *_: (p, s)),
                pl.BlockSpec((1, 8, maxlen), lambda s, p, *_: (s * pairs + p, 0, 0)),
            ],
        ),
        out_shape=[
            jax.ShapeDtypeStruct((rows, width), BF16),
            jax.ShapeDtypeStruct((width, rows), BF16),
            jax.ShapeDtypeStruct((seqs * pairs, 8, maxlen), F32),
        ],
        compiler_params=params(),
        cost_estimate=cost(20e9, 10e6),
        name="attend_forward",
    )(lengths, mixed, mixed, mixed)


def attend_back_kernel(maxlen, q_ref, k_ref, v_ref, ga_ref, attT_ref, lse_ref, d_ref, sum_ref, dqT):
    qs = q_ref[...] * jnp.asarray(HEAD**-0.5, BF16)
    k, v, ga = k_ref[...], v_ref[...], ga_ref[...]
    qT = qs.astype(F32).T.astype(BF16)
    kT = k.astype(F32).T.astype(BF16)
    gaT32 = ga.astype(F32).T
    gaT = gaT32.astype(BF16)
    prod = gaT32 * attT_ref[...].astype(F32)
    lane = lax.broadcasted_iota(jnp.int32, (maxlen, PAIR), 1)
    blank = jnp.zeros((HEAD, maxlen), BF16)
    nil = jnp.zeros((), BF16)
    heads = []
    for h in range(2):
        mine = (lane < HEAD) if h == 0 else (lane >= HEAD)
        at = slice(h * HEAD, (h + 1) * HEAD)
        pad = lambda a: jnp.concatenate([a, blank] if h == 0 else [blank, a], axis=0)
        heads.append(
            (
                jnp.where(mine, ga, nil), jnp.where(mine, qs, nil), pad(qT[at]), pad(gaT[at]), kT[at],
                jnp.sum(prod[at], axis=0, keepdims=True), lse_ref[0, h : h + 1, :],
            )
        )
    for j in range(maxlen // TILE):
        lo, hi = j * TILE, (j + 1) * TILE
        dv = dk = None
        for h in range(2):
            ga_h, q_h, qT_h, gaT_h, kT_h, delta, lse = heads[h]
            s = mm_nn(k[lo:hi], qT_h[:, lo:])
            gw = mm_nn(v[lo:hi], gaT_h[:, lo:])
            t = s * s + 1.0
            r = lax.rsqrt(t)
            p = jnp.exp(t * r - lse[:, lo:])
            kpos = lax.broadcasted_iota(jnp.int32, s.shape, 0)
            qpos = lax.broadcasted_iota(jnp.int32, s.shape, 1)
            p = jnp.where(kpos <= qpos, p, 0.0)
            g = jnp.tanh(s)
            w = g * p
            c = p * (s * r)
            a = p + g * (c - w)
            ds = (gw * a - c * delta[:, lo:]).astype(BF16)
            dv_h = mm_nn(w.astype(BF16), ga_h[lo:])
            dk_h = mm_nn(ds, q_h[lo:])
            dv = dv_h if dv is None else dv + dv_h
            dk = dk_h if dk is None else dk + dk_h
            dq_h = mm_nn(kT_h[:, lo:hi], ds)
            if j == 0:
                dqT[h * HEAD : (h + 1) * HEAD, :] = dq_h
            else:
                dqT[h * HEAD : (h + 1) * HEAD, lo:] += dq_h
        d_ref[2, lo:hi, :] = dv.astype(BF16)
        d_ref[1, lo:hi, :] = dk.astype(BF16)
        sums = [jnp.sum(d, axis=0, keepdims=True) for d in (dk, dv)]
        total = sums if j == 0 else [t + d for t, d in zip(total, sums)]
    dq = (dqT[...] * HEAD**-0.5).T
    d_ref[0] = dq.astype(BF16)
    total = [jnp.sum(dq, axis=0, keepdims=True)] + total
    sum_ref[0] = jnp.concatenate(total + [jnp.zeros((5, PAIR), F32)], axis=0)


def attend_backward(mixed, ga, attT, lse, seqs, first, count):
    rows, width = mixed.shape[0], mixed.shape[1] // 3
    maxlen, pairs = rows // seqs, width // PAIR
    col = lambda part: pl.BlockSpec((maxlen, PAIR), lambda s, p: (s, part * pairs + p + first))
    return pl.pallas_call(
        functools.partial(attend_back_kernel, maxlen),
        grid=(seqs, count),
        in_specs=[
            col(0), col(1), col(2), col(0),
            pl.BlockSpec((PAIR, maxlen), lambda s, p: (p + first, s)),
            pl.BlockSpec((1, 8, maxlen), lambda s, p: (s * pairs + p + first, 0, 0)),
        ],
        out_specs=[
            pl.BlockSpec((3, maxlen, PAIR), lambda s, p: (0, s, p)),
            pl.BlockSpec((1, 8, PAIR), lambda s, p: (s, 0, p)),
        ],
        out_shape=[
            jax.ShapeDtypeStruct((3, rows, count * PAIR), BF16),
            jax.ShapeDtypeStruct((seqs, 8, count * PAIR), F32),
        ],
        scratch_shapes=[pltpu.VMEM((PAIR, maxlen), F32)],
        compiler_params=params(),
        cost_estimate=cost(5e9 * count, 2e6 * count),
        name="attend_backward",
    )(mixed, mixed, mixed, ga, attT, lse)


def project_kernel(att_ref, x_ref, wp_ref, vec_ref, res_ref, n2_ref, wo_ref):
    pieces, per, _ = wp_ref.shape

    @pl.when(pl.program_id(0) == 0)
    def _():
        for p in range(pieces):
            wo_ref[p * per : (p + 1) * per, :] = wp_ref[p]

    residual = x_ref[...].astype(F32) + mm_nn(att_ref[...], wo_ref[...])
    res_ref[...] = residual
    xhat, rinv = norm_stats(residual)
    n2_ref[...] = (xhat * vec_ref[2:3, :] + vec_ref[3:4, :]).astype(BF16)


def project_out(att, tokens, wo_pieces, at, vecs, rows_block=256):
    rows, width = tokens.shape
    pieces = wo_pieces.shape[0]
    block = pl.BlockSpec((rows_block, width), lambda r: (r, 0))
    full = lambda a: pl.BlockSpec(a.shape, lambda r: (0,) * a.ndim)
    return pl.pallas_call(
        project_kernel,
        grid=(rows // rows_block,),
        in_specs=[
            block, block, pl.BlockSpec((pieces, width // pieces, width), lambda r: (0, at, 0)), full(vecs),
        ],
        out_specs=[block, block, pl.BlockSpec((width, width), lambda r: (0, 0))],
        out_shape=[
            jax.ShapeDtypeStruct((rows, width), F32),
            jax.ShapeDtypeStruct((rows, width), BF16),
            jax.ShapeDtypeStruct((width, width), BF16),
        ],
        compiler_params=params(),
        cost_estimate=cost(2 * rows * width * width, 10e6),
        name="project_out",
    )(att, tokens, wo_pieces, vecs)


def live_grad(cot, lengths_ref, maxlen, first_row):
    rows = cot.shape[0]
    at = first_row + lax.broadcasted_iota(jnp.int32, (rows, 1), 0)
    seq = first_row // maxlen
    return jnp.where(at - seq * maxlen < lengths_ref[seq], cot, 0.0)


def mlp_kernel(maxlen, units, len_ref, me_ref, n2_ref, res_ref, cot_ref, w_ref, out_ref, gn_ref, *rest):
    *gw_refs, gl_s, acc_s = rest
    step = pl.program_id(0)
    rows, width = n2_ref.shape

    @pl.when(step == 0)
    def _():
        for first in range(0, rows, maxlen):
            at = slice(first, first + maxlen)
            gl_s[at, :] = live_grad(cot_ref[at, :], len_ref, maxlen, first).astype(BF16)

    pieces = w_ref.shape[0]
    wu = w_ref[:, :units, :].reshape(pieces * units, width)
    wd = w_ref[:, units : 2 * units, :].reshape(pieces * units, width)
    n2, gl = n2_ref[...], gl_s[...]
    u = mm_nt(n2, wu)
    uu = u * u
    th = jnp.tanh(u * (GELU_A + GELU_B * uu))
    half = 0.5 * u
    act = (half + half * th).astype(BF16)
    slope = 0.5 + 0.5 * th + (half - half * (th * th)) * (GELU_A + (3.0 * GELU_B) * uu)
    gp = (mm_nt(gl, wd) * slope).astype(BF16)
    out = mm_nn(act, wd)
    gn = mm_nn(gp, wu)

    @pl.when(step == 0)
    def _():
        acc_s[...] = out + res_ref[...]
        gn_ref[...] = gn

    @pl.when(step > 0)
    def _():
        acc_s[...] += out
        gn_ref[...] += gn

    for at, grad in ((0, mm_tn(gp, n2)), (units, mm_tn(act, gl))):
        grad = grad.astype(BF16)
        if len(gw_refs) == 1:
            gw_refs[0][:, at : at + units, :] = grad.reshape(pieces, units, width)
            continue
        grad = grad.reshape(pieces // 2, 2, units, width)
        core = lax.rem(me_ref[0], 2)
        near = lax.rem(lax.div(me_ref[0], 2), 4)
        for side in range(2):

            @pl.when(core == side)
            def _():
                for place in range(pieces // 2):
                    slot = (place // 4) * 4 + ((place % 4) ^ near)
                    gw_refs[0][slot, at : at + units, :] = grad[place, side]
                    gw_refs[1][slot, at : at + units, :] = grad[place, 1 - side]

    @pl.when(step == pl.num_programs(0) - 1)
    def _():
        out_ref[...] = acc_s[...].astype(BF16)


def feed_forward(lengths, me, n2, residual, cot, w, units, split):
    rows, width = n2.shape
    pieces, held, _ = w.shape
    take = max(1, 768 // units)
    full = lambda: pl.BlockSpec((rows, width), lambda f, *_: (0, 0))
    outs = 2 if split else 1
    grads = [pl.BlockSpec((take // outs, 2 * units, width), lambda f, *_: (f, 0, 0))] * outs
    return pl.pallas_call(
        functools.partial(mlp_kernel, rows // lengths.shape[0], units),
        grid_spec=pltpu.PrefetchScalarGridSpec(
            num_scalar_prefetch=2,
            grid=(pieces // take,),
            in_specs=[full(), full(), full(), pl.BlockSpec((take, held, width), lambda f, *_: (f, 0, 0))],
            out_specs=[full(), full()] + grads,
            scratch_shapes=[pltpu.VMEM((rows, width), BF16), pltpu.VMEM((rows, width), F32)],
        ),
        out_shape=[jax.ShapeDtypeStruct((rows, width), BF16), jax.ShapeDtypeStruct((rows, width), F32)]
        + [jax.ShapeDtypeStruct((pieces // outs, 2 * units, width), BF16)] * outs,
        compiler_params=params(),
        cost_estimate=cost(12 * rows * width * pieces * units, 40e6),
        name="feed_forward",
    )(lengths, me, n2, residual, cot, w)


def norm_back(grad, xhat, rinv, gain):
    dh = grad * gain
    first = jnp.mean(dh, axis=-1, keepdims=True)
    second = jnp.mean(dh * xhat, axis=-1, keepdims=True)
    return rinv * (dh - first - xhat * second)


def middle_kernel(maxlen, len_ref, gn_ref, res_ref, cot_ref, att_ref, wo_ref, vec_ref, gres_ref, ga_ref, gwo_ref, gvec_ref, low_s):
    step = pl.program_id(0)
    rows = gn_ref.shape[0]
    gn = gn_ref[...]
    xhat, rinv = norm_stats(res_ref[...])
    gres = live_grad(cot_ref[...], len_ref, maxlen, step * rows) + norm_back(gn, xhat, rinv, vec_ref[2:3, :])
    gres_ref[...] = gres
    low = gres.astype(BF16)
    low_s[pl.ds(pl.multiple_of(step * rows, rows), rows), :] = low
    ga_ref[...] = mm_nt(low, wo_ref[...]).astype(BF16)

    @pl.when(step == 0)
    def _():
        gvec_ref[...] = jnp.zeros_like(gvec_ref)

    gvec_ref[0:1, :] += jnp.sum(gn * xhat, axis=0, keepdims=True)
    gvec_ref[1:2, :] += jnp.sum(gn, axis=0, keepdims=True)

    @pl.when(step == pl.num_programs(0) - 1)
    def _():
        gwo_ref[...] = mm_tn(att_ref[...], low_s[...]).astype(BF16)


def middle_back(lengths, gn, residual, cot, att, wo, vecs, rows_block=256):
    rows, width = gn.shape
    block = pl.BlockSpec((rows_block, width), lambda r, *_: (r, 0))
    full = lambda shape: pl.BlockSpec(shape, lambda r, *_: (0,) * len(shape))
    return pl.pallas_call(
        functools.partial(middle_kernel, rows // lengths.shape[0]),
        grid_spec=pltpu.PrefetchScalarGridSpec(
            num_scalar_prefetch=1,
            grid=(rows // rows_block,),
            in_specs=[block, block, block, full(att.shape), full(wo.shape), full(vecs.shape)],
            out_specs=[block, block, full(wo.shape), full((8, width))],
            scratch_shapes=[pltpu.VMEM((rows, width), BF16)],
        ),
        out_shape=[
            jax.ShapeDtypeStruct((rows, width), F32),
            jax.ShapeDtypeStruct((rows, width), BF16),
            jax.ShapeDtypeStruct(wo.shape, BF16),
            jax.ShapeDtypeStruct((8, width), F32),
        ],
        compiler_params=params(),
        cost_estimate=cost(4 * rows * width * width, 30e6),
        name="middle_back",
    )(lengths, gn, residual, cot, att, wo, vecs)


def qkv_grad_kernel(masks, ppr, opr, me_ref, *refs):
    d1_ref, d2_ref, sum1_ref, sum2_ref, n1_ref, w_ref, gwo_ref, vec_ref, gvec2_ref, e_ref, keep_ref, send_ref, low_s, acc_s = refs
    rows, width = n1_ref.shape
    part = pl.program_id(0)
    n1 = n1_ref[...]
    paired, gshift, at = jnp.zeros((1, width), F32), jnp.zeros((8, width), F32), 0
    for d_ref, sum_ref in ((d1_ref, sum1_ref), (d2_ref, sum2_ref)):
        cols = d_ref.shape[2]
        gw = mm_tn(d_ref[0], n1)
        low_s[pl.ds(pl.multiple_of(part * width + at, PAIR), cols), :] = gw.astype(BF16)
        w = w_ref[at : at + cols, :]
        paired += jnp.sum(gw * w.astype(F32), axis=0, keepdims=True)
        total = jnp.sum(sum_ref[...], axis=0)
        pick = lax.broadcasted_iota(jnp.int32, (8, 1), 0) == part
        total = jnp.sum(jnp.where(pick, total, 0.0), axis=0, keepdims=True)
        high = total.astype(BF16).astype(F32)
        low = jnp.concatenate([high, total - high, jnp.zeros((6, cols), F32)], axis=0)
        gshift += mm_nn(low.astype(BF16), w)
        at += cols

    @pl.when(part == 0)
    def _():
        acc_s[...] = jnp.zeros_like(acc_s)

    acc_s[0:1, :] += paired
    acc_s[1:2, :] += gshift[0:1, :] + gshift[1:2, :]

    @pl.when(part == 2)
    def _():
        qkv_grad_pieces(masks, ppr, opr, me_ref, acc_s, gwo_ref, vec_ref, gvec2_ref, e_ref, keep_ref, send_ref, low_s)


def qkv_grad_pieces(masks, ppr, opr, me_ref, acc_s, gwo_ref, vec_ref, gvec2_ref, e_ref, keep_ref, send_ref, low_s):
    width = acc_s.shape[1]
    paired, gshift = acc_s[0:1, :], acc_s[1:2, :]
    ggain = (paired - vec_ref[1:2, :] * gshift) / vec_ref[0:1, :]
    n = 2 * len(masks)
    owner = lax.broadcasted_iota(jnp.int32, (n, width), 1) // opr == lax.broadcasted_iota(jnp.int32, (n, width), 0)
    packed = jnp.zeros((n, 128), F32)
    for v, row in enumerate((ggain, gshift, gvec2_ref[0:1, :], gvec2_ref[1:2, :])):
        packed += mm_nt(jnp.where(owner, row, 0.0).astype(BF16), e_ref[v])
    me = me_ref[0]
    core = lax.rem(me, 2)
    for pair in range(len(masks)):
        slot = slot_of(masks, me, pair)
        sides = []
        for j in (2 * pair, 2 * pair + 1):
            extra = jnp.concatenate([packed[j : j + 1, :], jnp.zeros((1, width - 128), F32)], axis=1)
            extra = jnp.concatenate([extra, jnp.zeros((7, width), F32)], axis=0)
            sides.append((low_s[j * ppr : (j + 1) * ppr, :], gwo_ref[j * opr : (j + 1) * opr, :], extra.astype(BF16)))
        for side in range(2):

            @pl.when(core == side)
            def _():
                for out, part in ((keep_ref, sides[side]), (send_ref, sides[1 - side])):
                    out[slot] = jnp.concatenate(part, axis=0)


def qkv_grad(plan, me, grads, sums, n1, w_abs, gwo, vecs, gvec2, spread):
    rows, width = n1.shape
    masks = plan.slot_masks()
    ppr, opr = 3 * width // plan.n, width // plan.n
    full = lambda a: pl.BlockSpec(a.shape, lambda p, *_: (0,) * len(a.shape))
    shape = jax.ShapeDtypeStruct((len(masks), ppr + opr + 8, width), BF16)
    return pl.pallas_call(
        functools.partial(qkv_grad_kernel, masks, ppr, opr),
        grid_spec=pltpu.PrefetchScalarGridSpec(
            num_scalar_prefetch=1,
            grid=(3,),
            in_specs=[pl.BlockSpec((1, rows, d.shape[2]), lambda p, *_: (p, 0, 0)) for d in grads]
            + [full(a) for a in (*sums, n1)]
            + [pl.BlockSpec((width, width), lambda p, *_: (p, 0))]
            + [full(a) for a in (gwo, vecs, gvec2, spread)],
            out_specs=[full(shape), full(shape)],
            scratch_shapes=[pltpu.VMEM((3 * width, width), BF16), pltpu.VMEM((8, width), F32)],
        ),
        out_shape=[shape, shape],
        compiler_params=params(),
        cost_estimate=cost(6 * rows * width * width, 25e6),
        name="qkv_grad",
    )(me, *grads, *sums, n1, w_abs, gwo, vecs, gvec2, spread)


def qkv_grad_plain_kernel(d_ref, n1_ref, out_ref):
    out_ref[...] = mm_tn(d_ref[...], n1_ref[...]).astype(BF16)


def qkv_grad_plain(grads, n1):
    rows, width = n1.shape
    vm = pl.BlockSpec(memory_space=pltpu.VMEM)
    found = []
    for part in range(3):
        for d in grads:
            call = pl.pallas_call(
                qkv_grad_plain_kernel,
                in_specs=[vm, vm],
                out_specs=vm,
                out_shape=jax.ShapeDtypeStruct((d.shape[2], width), BF16),
                compiler_params=params(),
                name="qkv_grad_plain",
            )
            found.append(call(d[part], n1))
    return jnp.concatenate(found, axis=0)


def first_kernel(d1_ref, d2_ref, w_ref, x_ref, gres_ref, vec_ref, gtok_ref, gvec_ref):
    width = x_ref.shape[1]
    gn = jnp.zeros(x_ref.shape, F32)
    for part in range(3):
        at = part * width
        for ref in (d1_ref, d2_ref):
            gn += mm_nn(ref[part], w_ref[at : at + ref.shape[2], :])
            at += ref.shape[2]
    xhat, rinv = norm_stats(x_ref[...].astype(F32))
    gtok_ref[...] = gres_ref[...] + norm_back(gn, xhat, rinv, vec_ref[0:1, :])

    @pl.when(pl.program_id(0) == 0)
    def _():
        gvec_ref[...] = jnp.zeros_like(gvec_ref)

    gvec_ref[0:1, :] += jnp.sum(gn * xhat, axis=0, keepdims=True)
    gvec_ref[1:2, :] += jnp.sum(gn, axis=0, keepdims=True)


def first_back(grads, w_abs, tokens, gres, vecs, rows_block=256):
    rows, width = tokens.shape
    block = pl.BlockSpec((rows_block, width), lambda r: (r, 0))
    full = lambda shape: pl.BlockSpec(shape, lambda r: (0,) * len(shape))
    return pl.pallas_call(
        first_kernel,
        grid=(rows // rows_block,),
        in_specs=[pl.BlockSpec((3, rows_block, d.shape[2]), lambda r: (0, r, 0)) for d in grads]
        + [full(w_abs.shape), block, block, full(vecs.shape)],
        out_specs=[block, full((8, width))],
        out_shape=[jax.ShapeDtypeStruct((rows, width), F32), jax.ShapeDtypeStruct((8, width), F32)],
        compiler_params=params(),
        cost_estimate=cost(6 * rows * width * width, 25e6),
        name="first_back",
    )(*grads, w_abs, tokens, gres, vecs)


def body(plan, tokens, lengths, ln1_gain, ln1_shift, w_qkv, w_out, ln2_gain, ln2_shift, w_up, w_down, cot):
    rows, width = tokens.shape
    n = plan.n
    seqs = lengths.shape[0]
    me = lax.axis_index(AXES).astype(jnp.int32)
    me_arr = me[None]
    vec_piece = jnp.stack([ln1_gain, ln1_shift, ln2_gain, ln2_shift])
    per = vec_piece.shape[1]
    qkv_piece = w_qkv.T
    ppr, units = qkv_piece.shape[0], w_down.shape[0]
    ff = units * n

    mlp_piece = jnp.concatenate([w_up.T, w_down, w_out], axis=0)
    mlp_all = lax.all_gather(mlp_piece, AXES, axis=0, tiled=True).reshape(n, -1, width)
    if plan.direct:
        w_ff, ff_units, wo_pieces, wo_at = mlp_all, units, mlp_all, 2 * units // per
    else:
        ff_units = 768
        wo_pieces, wo_at = mlp_all[:, 2 * units :].reshape(1, width, width), 0
        w_ff = mlp_all[:, : 2 * units].reshape(n, 2, units, width).transpose(1, 0, 2, 3)
        w_ff = w_ff.reshape(2, ff // 768, 768, width).transpose(1, 0, 2, 3).reshape(ff // 768, 2 * 768, width)

    if plan.direct:
        flat = jnp.pad(vec_piece.reshape(1, -1), ((0, 7), (0, width - 4 * per)))
        gathered = plan.gather(jnp.concatenate([qkv_piece, flat], axis=0))
        slots = jnp.array(plan.slot_masks() + [m ^ 1 for m in plan.slot_masks()], jnp.int32)
        column = jnp.arange(width, dtype=jnp.int32)
        place = ((slots ^ me)[:, None] == (column // per)[None]).astype(F32)
        lane = jnp.arange(128, dtype=jnp.int32)
        spread = jnp.stack([(lane[:, None] == v * per + (column % per)[None]).astype(BF16) for v in range(4)])
        mixed, n1, w_abs, vecs = qkv_project(plan, me_arr, tokens, gathered, spread, place, ppr * n)
    else:
        w_abs = lax.all_gather(qkv_piece, AXES, axis=0, tiled=True)
        vecs = lax.all_gather(vec_piece, AXES, axis=1, tiled=True).astype(F32)
        vecs = jnp.pad(vecs, ((0, 4), (0, 0)))
        mixed, n1 = qkv_plain(tokens, w_abs, vecs)

    att, attT, lse = attend_forward(mixed, lengths)
    residual, n2, wo = project_out(att, tokens, wo_pieces, wo_at, vecs)
    output, gn2, *gw_ff = feed_forward(lengths, me_arr, n2, residual, cot, w_ff, ff_units, plan.direct)
    if plan.direct:
        got = plan.swap(gw_ff[1], 1)
    else:
        gw_ff = gw_ff[0].reshape(ff // 768, 2, 768, width).transpose(1, 0, 2, 3)
        gw_ff = gw_ff.reshape(2, n, units, width).transpose(1, 0, 2, 3).reshape(-1, width)
        g_ff = lax.psum_scatter(gw_ff, AXES, scatter_dimension=0, tiled=True)
    gres, ga, gwo, gvec2 = middle_back(lengths, gn2, residual, cot, att, wo, vecs)
    pairs = width // PAIR
    late = pairs // 3
    if plan.direct:
        ga, got, keep = lax.optimization_barrier((ga, got, gw_ff[0]))
        away = plan.first_away(keep, got)
        back = (plan.swap(away[0], 2), plan.swap(away[1], 4))
        ga, away = lax.optimization_barrier((ga, away))
    grads, sums = attend_backward(mixed, ga, attT, lse, seqs, 0, pairs - late)
    if plan.direct:
        back, grads, ga, sums = lax.optimization_barrier((back, grads, ga, sums))
        away = plan.second_away(keep, got, back)
        again = (plan.swap(away[0], 4), plan.swap(away[1], 2))
        ga, away = lax.optimization_barrier((ga, away))
    more, late_sums = attend_backward(mixed, ga, attT, lse, seqs, pairs - late, late)
    if plan.direct:
        again, more, n1 = lax.optimization_barrier((again, more, n1))
        g_ff = plan.last_sum(keep, got, back, again)
    grads, sums = [grads, more], [sums, late_sums]
    if plan.direct:
        keep, send = qkv_grad(plan, me_arr, grads, sums, n1, w_abs, gwo, vecs, gvec2, spread)
        summed = plan.scatter_first(keep, send, 32)
        gres, summed = lax.optimization_barrier((gres, summed))
        g_attn = plan.scatter_rest(*summed)
        g_attn, g_ff = lax.optimization_barrier((g_attn, g_ff))
        g_attn = g_attn.astype(F32)
        g_qkv, g_out = g_attn[:ppr], g_attn[ppr : ppr + per]
        g_vec = g_attn[ppr + per, : 4 * per].reshape(4, per)
    else:
        g_qkv = lax.psum_scatter(qkv_grad_plain(grads, n1), AXES, scatter_dimension=0, tiled=True)
        g_out = lax.psum_scatter(gwo, AXES, scatter_dimension=0, tiled=True)
    gtok, gvec1 = first_back(grads, w_abs, tokens, gres, vecs)
    if not plan.direct:
        gvec = jnp.concatenate([gvec1[:2], gvec2[:2]], axis=0)
        g_vec = lax.psum_scatter(gvec, AXES, scatter_dimension=1, tiled=True)
    g_ff = g_ff.astype(F32)
    return (
        output, gtok, g_vec[0], g_vec[1], g_qkv.astype(F32).T, g_out.astype(F32), g_vec[2], g_vec[3],
        g_ff[:units].T, g_ff[units:],
    )


def solution(mesh):
    both = AXES
    rows2, vec, cols2 = P(both, None), P(both), P(None, both)
    in_specs = (rows2, vec, vec, vec, cols2, rows2, vec, vec, cols2, rows2, rows2)
    out_specs = (rows2, rows2, vec, vec, cols2, rows2, vec, vec, cols2, rows2)
    return jax.shard_map(
        functools.partial(body, Plan(mesh)), mesh=mesh, in_specs=in_specs, out_specs=out_specs, check_vma=False
    )
```

```python
import functools
import math

import jax
import jax.numpy as jnp
from jax import lax
from jax.experimental import pallas as pl
from jax.experimental.pallas import tpu as pltpu
from jax.sharding import PartitionSpec as P

F32 = jnp.float32
BF16 = jnp.bfloat16
HEAD = 64
PAIR = 2 * HEAD
EPSILON = 1e-05
NEGATIVE = -1e30
TILE = 256
CHUNK = 32
AXES = ("dp", "fsdp")
VMEM_LIMIT = 56 << 20
GELU_A = math.sqrt(2.0 / math.pi)
GELU_B = GELU_A * 0.044715


def mm_nn(left, right):
    return jnp.dot(left, right, preferred_element_type=F32)


def mm_nt(left, right):
    return lax.dot_general(left, right, (((1,), (1,)), ((), ())), preferred_element_type=F32)


def mm_tn(left, right):
    return lax.dot_general(left, right, (((0,), (0,)), ((), ())), preferred_element_type=F32)


def norm_stats(values):
    average = jnp.mean(values, axis=-1, keepdims=True)
    centred = values - average
    variance = jnp.mean(centred * centred, axis=-1, keepdims=True)
    rinv = lax.rsqrt(variance + EPSILON)
    return centred * rinv, rinv


def params(**kw):
    return pltpu.CompilerParams(vmem_limit_bytes=VMEM_LIMIT, **kw)


def cost(flops, moved):
    return pl.CostEstimate(flops=int(flops), bytes_accessed=int(moved), transcendentals=0)


class Plan:
    def __init__(self, mesh):
        self.n = mesh.shape["dp"] * mesh.shape["fsdp"]
        self.bits = self.n.bit_length() - 1
        self.direct = self.n == 1 << self.bits and self.bits == 5 and mesh.shape["fsdp"] == 4
        self.along = (3, 4)
        self.across = (1, 2)

    @staticmethod
    def masks_of(bits):
        found = [0]
        for bit in bits:
            found = found + [m | 1 << bit for m in found]
        return found

    def slot_masks(self):
        return [m ^ k for m in self.masks_of(self.across) for k in self.masks_of(self.along)]

    def swap(self, value, mask):
        return lax.ppermute(value, AXES, [(i, i ^ mask) for i in range(self.n)])

    def spread_stage(self, held, bits):
        return jnp.concatenate([held] + [self.swap(held, m) for m in self.masks_of(bits)[1:]], axis=0)

    def gather(self, piece):
        held = self.spread_stage(self.spread_stage(piece[None], self.along), self.across)
        return held, self.swap(held, 1)

    def scatter_first(self, keep, send):
        got = self.swap(send, 1)
        grid = (len(self.masks_of(self.across)), -1) + keep.shape[1:]
        keep, got = keep.reshape(grid), got.reshape(grid)
        return [add_low(keep[x], [got[x]]) for x in range(grid[0])]

    def scatter_rest(self, held, beside):
        outer, inner = self.masks_of(self.across), self.masks_of(self.along)
        held = add_low(held[0], [self.swap(v, m) for v, m in zip(held[1:], outer[1:])])
        held, beside = lax.optimization_barrier((held, beside))
        return add_low(held[0], [self.swap(held[z], m) for z, m in list(enumerate(inner))[1:]]), beside

    def view(self, held):
        pieces, rows, width = held.shape
        return held.reshape(pieces // 4, 2, 2, 2, rows // 2, width)

    def first_away(self, keep, got):
        k, g = self.view(keep), self.view(got)
        return add_low(k[:, :, 1, 0], [g[:, :, 1, 0]]), add_low(k[:, 1, :, 1], [g[:, 1, :, 1]])

    def second_away(self, keep, got, back):
        k, g = self.view(keep), self.view(got)
        return (
            add_low(k[:, 1, 0, 0], [g[:, 1, 0, 0], back[0][:, 1]]),
            add_low(k[:, 0, 1, 1], [g[:, 0, 1, 1], back[1][:, 1]]),
        )

    def last_sum(self, keep, got, back, again):
        k, g = self.view(keep), self.view(got)
        both = [
            add_low(k[:, 0, 0, half], [g[:, 0, 0, half], back[half][:, 0], again[half]]) for half in range(2)
        ]
        whole = jnp.concatenate(both, axis=1)
        return whole.reshape(-1, whole.shape[-1])

    def along_sum(self, whole):
        line = [[r + 8 * z for z in range(self.n // 8)] for r in range(8)]
        return lax.psum_scatter(whole, AXES, scatter_dimension=0, tiled=True, axis_index_groups=line)


def add_low(first, others):
    total = first.astype(F32)
    for other in others:
        total = total + other.astype(F32)
    return total.astype(first.dtype)


def slot_of(masks, me, piece_pair):
    wanted = piece_pair ^ lax.div(me, 2)
    slot = jnp.int32(0)
    for s, m in enumerate(masks):
        slot = jnp.where(wanted == m // 2, s, slot)
    return slot


def qkv_kernel(masks, ppr, me_ref, x_ref, own_ref, sib_ref, e_ref, m_ref, mixed_ref, n1_ref, w_ref, vec_ref):
    me = me_ref[0]

    @pl.when(pl.program_id(0) == 0)
    def _():
        core = lax.rem(me, 2)
        for s, m in enumerate(masks):
            pair = lax.div(me, 2) ^ (m // 2)
            at = pl.ds(pl.multiple_of(pair * (2 * ppr), 16), 2 * ppr)
            both = [own_ref[s, :ppr, :], sib_ref[s, :ppr, :]]
            for side in range(2):

                @pl.when(core == side)
                def _():
                    w_ref[at, :] = jnp.concatenate([both[side], both[1 - side]], axis=0)

        packed = jnp.concatenate([own_ref[:, ppr, :128], sib_ref[:, ppr, :128]], axis=0)
        for v in range(4):
            vec_ref[v : v + 1, :] = jnp.sum(mm_nn(packed, e_ref[v]) * m_ref[...], axis=0, keepdims=True)

    xhat, rinv = norm_stats(x_ref[...].astype(F32))
    n1 = (xhat * vec_ref[0:1, :] + vec_ref[1:2, :]).astype(BF16)
    n1_ref[...] = n1
    mixed_ref[...] = mm_nt(n1, w_ref[...]).astype(BF16)


def qkv_project(plan, me, tokens, gathered, spread, place, out_cols, rows_block=256):
    rows, width = tokens.shape
    masks = plan.slot_masks()
    full = lambda a: pl.BlockSpec(a.shape, lambda r, *_: (0,) * a.ndim)
    whole = lambda shape: pl.BlockSpec(shape, lambda r, *_: (0,) * len(shape))
    return pl.pallas_call(
        functools.partial(qkv_kernel, masks, out_cols // plan.n),
        grid_spec=pltpu.PrefetchScalarGridSpec(
            num_scalar_prefetch=1,
            grid=(rows // rows_block,),
            in_specs=[
                pl.BlockSpec((rows_block, width), lambda r, *_: (r, 0)),
            ]
            + [full(a) for a in (*gathered, spread, place)],
            out_specs=[
                pl.BlockSpec((rows_block, out_cols), lambda r, *_: (r, 0)),
                pl.BlockSpec((rows_block, width), lambda r, *_: (r, 0)),
                whole((out_cols, width)), whole((8, width)),
            ],
        ),
        out_shape=[
            jax.ShapeDtypeStruct((rows, out_cols), BF16),
            jax.ShapeDtypeStruct((rows, width), BF16),
            jax.ShapeDtypeStruct((out_cols, width), BF16),
            jax.ShapeDtypeStruct((8, width), F32),
        ],
        compiler_params=params(),
        cost_estimate=cost(2 * rows * width * out_cols, 20e6),
        name="qkv_project",
    )(me, tokens, *gathered, spread, place)


def qkv_plain_kernel(x_ref, w_ref, vec_ref, mixed_ref, n1_ref):
    xhat, rinv = norm_stats(x_ref[...].astype(F32))
    n1 = (xhat * vec_ref[0:1, :] + vec_ref[1:2, :]).astype(BF16)
    n1_ref[...] = n1
    mixed_ref[...] = mm_nt(n1, w_ref[...]).astype(BF16)


def qkv_plain(tokens, w_abs, vecs, rows_block=256):
    rows, width = tokens.shape
    out_cols = w_abs.shape[0]
    full = lambda a: pl.BlockSpec(a.shape, lambda r: (0,) * a.ndim)
    return pl.pallas_call(
        qkv_plain_kernel,
        grid=(rows // rows_block,),
        in_specs=[pl.BlockSpec((rows_block, width), lambda r: (r, 0)), full(w_abs), full(vecs)],
        out_specs=[
            pl.BlockSpec((rows_block, out_cols), lambda r: (r, 0)),
            pl.BlockSpec((rows_block, width), lambda r: (r, 0)),
        ],
        out_shape=[
            jax.ShapeDtypeStruct((rows, out_cols), BF16),
            jax.ShapeDtypeStruct((rows, width), BF16),
        ],
        compiler_params=params(),
        name="qkv_plain",
    )(tokens, w_abs, vecs)


def tile_at(i, j):
    return i * (i + 1) // 2 + j

def attend_kernel(maxlen, len_ref, q_ref, k_ref, v_ref, att_ref, attT_ref, inv_ref, keep_ref):
    length = len_ref[pl.program_id(0)]
    q, k = q_ref[...], k_ref[...]
    qT = (q.astype(F32) * HEAD**-0.5).T.astype(BF16)
    vT = v_ref[...].astype(F32).T.astype(BF16)
    same = lax.broadcasted_iota(jnp.int32, (PAIR, PAIR), 0) // HEAD == lax.broadcasted_iota(jnp.int32, (PAIR, PAIR), 1) // HEAD
    same = jnp.where(same, 1.0, 0.0).astype(BF16)
    square = lambda a: jnp.max(mm_nn((a.astype(F32) * a.astype(F32)).astype(BF16), same))
    small = square(q) * square(k) * (1.03 / HEAD) < 70.0**2

    def block(i, plain):
        lo, hi = i * TILE, (i + 1) * TILE
        qpos = lo + lax.broadcasted_iota(jnp.int32, (1, TILE), 1)
        limit = jnp.minimum(qpos, length - 1)
        blank = jnp.zeros((HEAD, TILE), BF16)
        outs = []
        for h in range(2):
            own = qT[h * HEAD : (h + 1) * HEAD, lo:hi]
            own = jnp.concatenate([own, blank] if h == 0 else [blank, own], axis=0)

            def piece(at):
                s = mm_nn(k[at : at + CHUNK], own)
                t = s * s + 1.0
                r = lax.rsqrt(t)
                kpos = at + lax.broadcasted_iota(jnp.int32, (CHUNK, TILE), 0)
                return s, r, t * r, (kpos <= limit if at >= lo else kpos < length)

            top = None
            if not plain:
                for at in range(0, hi, CHUNK):
                    s, r, smooth, allowed = piece(at)
                    here = jnp.max(jnp.where(allowed, smooth, NEGATIVE), axis=0, keepdims=True)
                    top = here if top is None else jnp.maximum(top, here)
            total, weights = None, []
            for at in range(0, hi, CHUNK):
                s, r, smooth, allowed = piece(at)
                e = jnp.exp(smooth) if plain else jnp.exp(jnp.minimum(smooth - top, 0.0))
                e = jnp.where(allowed, e, 0.0)
                part = e.reshape(CHUNK // 8, 8, TILE).sum(axis=0)
                total = part if total is None else total + part
                g = jnp.tanh(s)
                w = g * e
                c = e * (s * r)
                a = e + g * (c - w)
                w = w.astype(BF16)
                weights.append(w)
                tile, row = tile_at(i, at // TILE), at % TILE
                keep_ref[0, h, 0, tile, row : row + CHUNK, :] = w
                keep_ref[0, h, 1, tile, row : row + CHUNK, :] = a.astype(BF16)
                keep_ref[0, h, 2, tile, row : row + CHUNK, :] = c.astype(BF16)
            inv = 1.0 / jnp.sum(total, axis=0, keepdims=True)
            inv_ref[0, h : h + 1, lo:hi] = inv
            outs.append(mm_nn(vT[h * HEAD : (h + 1) * HEAD, :hi], jnp.concatenate(weights, axis=0)) * inv)
        outT = jnp.concatenate(outs, axis=0)
        attT_ref[:, lo:hi] = outT.astype(BF16)
        att_ref[lo:hi, :] = outT.T.astype(BF16)

    @pl.when(small)
    def _():
        for i in range(maxlen // TILE):
            block(i, True)

    @pl.when(jnp.logical_not(small))
    def _():
        for i in range(maxlen // TILE):
            block(i, False)


def attend_forward(mixed, lengths):
    rows, width = mixed.shape[0], mixed.shape[1] // 3
    seqs = lengths.shape[0]
    maxlen, pairs = rows // seqs, width // PAIR
    tiles = tile_at(maxlen // TILE, 0)
    col = lambda part: pl.BlockSpec((maxlen, PAIR), lambda s, p, *_: (s, part * pairs + p))
    return pl.pallas_call(
        functools.partial(attend_kernel, maxlen),
        grid_spec=pltpu.PrefetchScalarGridSpec(
            num_scalar_prefetch=1,
            grid=(seqs, pairs),
            in_specs=[col(0), col(1), col(2)],
            out_specs=[
                col(0),
                pl.BlockSpec((PAIR, maxlen), lambda s, p, *_: (p, s)),
                pl.BlockSpec((1, 8, maxlen), lambda s, p, *_: (s * pairs + p, 0, 0)),
                pl.BlockSpec((1, 2, 3, tiles, TILE, TILE), lambda s, p, *_: (s * pairs + p, 0, 0, 0, 0, 0)),
            ],
        ),
        out_shape=[
            jax.ShapeDtypeStruct((rows, width), BF16),
            jax.ShapeDtypeStruct((width, rows), BF16),
            jax.ShapeDtypeStruct((seqs * pairs, 8, maxlen), F32),
            jax.ShapeDtypeStruct((seqs * pairs, 2, 3, tiles, TILE, TILE), BF16),
        ],
        compiler_params=params(),
        cost_estimate=cost(20e9, 60e6),
        name="attend_forward",
    )(lengths, mixed, mixed, mixed)


def attend_back_kernel(maxlen, q_ref, k_ref, v_ref, ga_ref, attT_ref, inv_ref, keep_ref, d_ref, sum_ref, dqT):
    qs = q_ref[...] * jnp.asarray(HEAD**-0.5, BF16)
    v = v_ref[...]
    kT = k_ref[...].astype(F32).T.astype(BF16)
    gaT = ga_ref[...].astype(F32).T
    prod = gaT * attT_ref[...].astype(F32)
    half = lambda h: slice(h * HEAD, (h + 1) * HEAD)
    inv = [inv_ref[0, h : h + 1, :] for h in range(2)]
    gaT = jnp.concatenate([gaT[half(h)] * inv[h] for h in range(2)], axis=0)
    ga = gaT.T.astype(BF16)
    gaT = gaT.astype(BF16)
    lane = lax.broadcasted_iota(jnp.int32, (maxlen, PAIR), 1)
    blank = jnp.zeros((HEAD, maxlen), BF16)
    nil = jnp.zeros((), BF16)
    heads = []
    for h in range(2):
        mine = (lane < HEAD) if h == 0 else (lane >= HEAD)
        own = gaT[half(h)]
        heads.append(
            (
                jnp.where(mine, ga, nil), jnp.where(mine, qs, nil),
                jnp.concatenate([own, blank] if h == 0 else [blank, own], axis=0), kT[half(h)],
                jnp.sum(prod[half(h)], axis=0, keepdims=True) * inv[h],
            )
        )
    blocks = maxlen // TILE
    for j in range(blocks):
        lo, hi = j * TILE, (j + 1) * TILE
        dv = dk = None
        for h in range(2):
            ga_h, q_h, gaT_h, kT_h, delta = heads[h]
            side = lambda part: jnp.concatenate([keep_ref[0, h, part, tile_at(i, j)] for i in range(j, blocks)], axis=1)
            gw = mm_nn(v[lo:hi], gaT_h[:, lo:])
            ds = (gw * side(1).astype(F32) - side(2).astype(F32) * delta[:, lo:]).astype(BF16)
            dv_h = mm_nn(side(0), ga_h[lo:])
            dk_h = mm_nn(ds, q_h[lo:])
            dv = dv_h if dv is None else dv + dv_h
            dk = dk_h if dk is None else dk + dk_h
            dq_h = mm_nn(kT_h[:, lo:hi], ds)
            if j == 0:
                dqT[half(h), :] = dq_h
            else:
                dqT[half(h), lo:] += dq_h
        d_ref[2, lo:hi, :] = dv.astype(BF16)
        d_ref[1, lo:hi, :] = dk.astype(BF16)
        sums = [jnp.sum(d, axis=0, keepdims=True) for d in (dk, dv)]
        total = sums if j == 0 else [t + d for t, d in zip(total, sums)]
    dq = (dqT[...] * HEAD**-0.5).T
    d_ref[0] = dq.astype(BF16)
    total = [jnp.sum(dq, axis=0, keepdims=True)] + total
    sum_ref[0] = jnp.concatenate(total + [jnp.zeros((5, PAIR), F32)], axis=0)


def attend_backward(mixed, ga, attT, inv, keep, seqs, first, count):
    rows, width = mixed.shape[0], mixed.shape[1] // 3
    maxlen, pairs = rows // seqs, width // PAIR
    col = lambda part: pl.BlockSpec((maxlen, PAIR), lambda s, p: (s, part * pairs + p + first))
    return pl.pallas_call(
        functools.partial(attend_back_kernel, maxlen),
        grid=(seqs, count),
        in_specs=[
            col(0), col(1), col(2), col(0),
            pl.BlockSpec((PAIR, maxlen), lambda s, p: (p + first, s)),
            pl.BlockSpec((1, 8, maxlen), lambda s, p: (s * pairs + p + first, 0, 0)),
            pl.BlockSpec((1,) + keep.shape[1:], lambda s, p: (s * pairs + p + first, 0, 0, 0, 0, 0)),
        ],
        out_specs=[
            pl.BlockSpec((3, maxlen, PAIR), lambda s, p: (0, s, p)),
            pl.BlockSpec((1, 8, PAIR), lambda s, p: (s, 0, p)),
        ],
        out_shape=[
            jax.ShapeDtypeStruct((3, rows, count * PAIR), BF16),
            jax.ShapeDtypeStruct((seqs, 8, count * PAIR), F32),
        ],
        scratch_shapes=[pltpu.VMEM((PAIR, maxlen), F32)],
        compiler_params=params(),
        cost_estimate=cost(5e9 * count, 10e6 * count),
        name="attend_backward",
    )(mixed, mixed, mixed, ga, attT, inv, keep)


def project_kernel(att_ref, x_ref, wp_ref, vec_ref, res_ref, n2_ref, wo_ref):
    pieces, per, _ = wp_ref.shape

    @pl.when(pl.program_id(0) == 0)
    def _():
        for p in range(pieces):
            wo_ref[p * per : (p + 1) * per, :] = wp_ref[p]

    residual = x_ref[...].astype(F32) + mm_nn(att_ref[...], wo_ref[...])
    res_ref[...] = residual
    xhat, rinv = norm_stats(residual)
    n2_ref[...] = (xhat * vec_ref[2:3, :] + vec_ref[3:4, :]).astype(BF16)


def project_out(att, tokens, wo_pieces, at, vecs, rows_block=256):
    rows, width = tokens.shape
    pieces = wo_pieces.shape[0]
    block = pl.BlockSpec((rows_block, width), lambda r: (r, 0))
    full = lambda a: pl.BlockSpec(a.shape, lambda r: (0,) * a.ndim)
    return pl.pallas_call(
        project_kernel,
        grid=(rows // rows_block,),
        in_specs=[
            block, block, pl.BlockSpec((pieces, width // pieces, width), lambda r: (0, at, 0)), full(vecs),
        ],
        out_specs=[block, block, pl.BlockSpec((width, width), lambda r: (0, 0))],
        out_shape=[
            jax.ShapeDtypeStruct((rows, width), F32),
            jax.ShapeDtypeStruct((rows, width), BF16),
            jax.ShapeDtypeStruct((width, width), BF16),
        ],
        compiler_params=params(),
        cost_estimate=cost(2 * rows * width * width, 10e6),
        name="project_out",
    )(att, tokens, wo_pieces, vecs)


def live_grad(cot, lengths_ref, maxlen, first_row):
    rows = cot.shape[0]
    at = first_row + lax.broadcasted_iota(jnp.int32, (rows, 1), 0)
    seq = first_row // maxlen
    return jnp.where(at - seq * maxlen < lengths_ref[seq], cot, 0.0)


def mlp_kernel(maxlen, units, len_ref, me_ref, n2_ref, res_ref, cot_ref, w_ref, out_ref, gn_ref, *rest):
    *gw_refs, gl_s, acc_s = rest
    step = pl.program_id(0)
    rows, width = n2_ref.shape

    @pl.when(step == 0)
    def _():
        for first in range(0, rows, maxlen):
            at = slice(first, first + maxlen)
            gl_s[at, :] = live_grad(cot_ref[at, :], len_ref, maxlen, first).astype(BF16)

    pieces = w_ref.shape[0]
    wu = w_ref[:, :units, :].reshape(pieces * units, width)
    wd = w_ref[:, units : 2 * units, :].reshape(pieces * units, width)
    n2, gl = n2_ref[...], gl_s[...]
    u = mm_nt(n2, wu)
    uu = u * u
    th = jnp.tanh(u * (GELU_A + GELU_B * uu))
    half = 0.5 * u
    act = (half + half * th).astype(BF16)
    slope = 0.5 + 0.5 * th + (half - half * (th * th)) * (GELU_A + (3.0 * GELU_B) * uu)
    gp = (mm_nt(gl, wd) * slope).astype(BF16)
    out = mm_nn(act, wd)
    gn = mm_nn(gp, wu)

    @pl.when(step == 0)
    def _():
        acc_s[...] = out + res_ref[...]
        gn_ref[...] = gn

    @pl.when(step > 0)
    def _():
        acc_s[...] += out
        gn_ref[...] += gn

    for at, grad in ((0, mm_tn(gp, n2)), (units, mm_tn(act, gl))):
        grad = grad.astype(BF16)
        if len(gw_refs) == 1:
            gw_refs[0][:, at : at + units, :] = grad.reshape(pieces, units, width)
            continue
        grad = grad.reshape(pieces // 2, 2, units, width)
        core = lax.rem(me_ref[0], 2)
        near = lax.rem(lax.div(me_ref[0], 2), 4)
        for side in range(2):

            @pl.when(core == side)
            def _():
                for place in range(pieces // 2):
                    slot = (place // 4) * 4 + ((place % 4) ^ near)
                    gw_refs[0][slot, at : at + units, :] = grad[place, side]
                    gw_refs[1][slot, at : at + units, :] = grad[place, 1 - side]

    @pl.when(step == pl.num_programs(0) - 1)
    def _():
        out_ref[...] = acc_s[...].astype(BF16)


def feed_forward(lengths, me, n2, residual, cot, w, units, split):
    rows, width = n2.shape
    pieces, held, _ = w.shape
    take = max(1, 768 // units)
    full = lambda: pl.BlockSpec((rows, width), lambda f, *_: (0, 0))
    outs = 2 if split else 1
    grads = [pl.BlockSpec((take // outs, 2 * units, width), lambda f, *_: (f, 0, 0))] * outs
    return pl.pallas_call(
        functools.partial(mlp_kernel, rows // lengths.shape[0], units),
        grid_spec=pltpu.PrefetchScalarGridSpec(
            num_scalar_prefetch=2,
            grid=(pieces // take,),
            in_specs=[full(), full(), full(), pl.BlockSpec((take, held, width), lambda f, *_: (f, 0, 0))],
            out_specs=[full(), full()] + grads,
            scratch_shapes=[pltpu.VMEM((rows, width), BF16), pltpu.VMEM((rows, width), F32)],
        ),
        out_shape=[jax.ShapeDtypeStruct((rows, width), BF16), jax.ShapeDtypeStruct((rows, width), F32)]
        + [jax.ShapeDtypeStruct((pieces // outs, 2 * units, width), BF16)] * outs,
        compiler_params=params(),
        cost_estimate=cost(12 * rows * width * pieces * units, 40e6),
        name="feed_forward",
    )(lengths, me, n2, residual, cot, w)


def norm_back(grad, xhat, rinv, gain):
    dh = grad * gain
    first = jnp.mean(dh, axis=-1, keepdims=True)
    second = jnp.mean(dh * xhat, axis=-1, keepdims=True)
    return rinv * (dh - first - xhat * second)


def middle_kernel(maxlen, len_ref, gn_ref, res_ref, cot_ref, att_ref, wo_ref, vec_ref, gres_ref, ga_ref, gwo_ref, gvec_ref, low_s):
    step = pl.program_id(0)
    rows = gn_ref.shape[0]
    gn = gn_ref[...]
    xhat, rinv = norm_stats(res_ref[...])
    gres = live_grad(cot_ref[...], len_ref, maxlen, step * rows) + norm_back(gn, xhat, rinv, vec_ref[2:3, :])
    gres_ref[...] = gres
    low = gres.astype(BF16)
    low_s[pl.ds(pl.multiple_of(step * rows, rows), rows), :] = low
    ga_ref[...] = mm_nt(low, wo_ref[...]).astype(BF16)

    @pl.when(step == 0)
    def _():
        gvec_ref[...] = jnp.zeros_like(gvec_ref)

    gvec_ref[0:1, :] += jnp.sum(gn * xhat, axis=0, keepdims=True)
    gvec_ref[1:2, :] += jnp.sum(gn, axis=0, keepdims=True)

    @pl.when(step == pl.num_programs(0) - 1)
    def _():
        gwo_ref[...] = mm_tn(att_ref[...], low_s[...]).astype(BF16)


def middle_back(lengths, gn, residual, cot, att, wo, vecs, rows_block=256):
    rows, width = gn.shape
    block = pl.BlockSpec((rows_block, width), lambda r, *_: (r, 0))
    full = lambda shape: pl.BlockSpec(shape, lambda r, *_: (0,) * len(shape))
    return pl.pallas_call(
        functools.partial(middle_kernel, rows // lengths.shape[0]),
        grid_spec=pltpu.PrefetchScalarGridSpec(
            num_scalar_prefetch=1,
            grid=(rows // rows_block,),
            in_specs=[block, block, block, full(att.shape), full(wo.shape), full(vecs.shape)],
            out_specs=[block, block, full(wo.shape), full((8, width))],
            scratch_shapes=[pltpu.VMEM((rows, width), BF16)],
        ),
        out_shape=[
            jax.ShapeDtypeStruct((rows, width), F32),
            jax.ShapeDtypeStruct((rows, width), BF16),
            jax.ShapeDtypeStruct(wo.shape, BF16),
            jax.ShapeDtypeStruct((8, width), F32),
        ],
        compiler_params=params(),
        cost_estimate=cost(4 * rows * width * width, 30e6),
        name="middle_back",
    )(lengths, gn, residual, cot, att, wo, vecs)


def qkv_grad_kernel(masks, ppr, opr, me_ref, *refs):
    d1_ref, d2_ref, sum1_ref, sum2_ref, n1_ref, w_ref, gwo_ref, vec_ref, gvec2_ref, e_ref, keep_ref, send_ref, low_s, acc_s = refs
    rows, width = n1_ref.shape
    part = pl.program_id(0)
    n1 = n1_ref[...]
    paired, gshift, at = jnp.zeros((1, width), F32), jnp.zeros((8, width), F32), 0
    for d_ref, sum_ref in ((d1_ref, sum1_ref), (d2_ref, sum2_ref)):
        cols = d_ref.shape[2]
        gw = mm_tn(d_ref[0], n1)
        low_s[pl.ds(pl.multiple_of(part * width + at, PAIR), cols), :] = gw.astype(BF16)
        w = w_ref[at : at + cols, :]
        paired += jnp.sum(gw * w.astype(F32), axis=0, keepdims=True)
        total = jnp.sum(sum_ref[...], axis=0)
        pick = lax.broadcasted_iota(jnp.int32, (8, 1), 0) == part
        total = jnp.sum(jnp.where(pick, total, 0.0), axis=0, keepdims=True)
        high = total.astype(BF16).astype(F32)
        low = jnp.concatenate([high, total - high, jnp.zeros((6, cols), F32)], axis=0)
        gshift += mm_nn(low.astype(BF16), w)
        at += cols

    @pl.when(part == 0)
    def _():
        acc_s[...] = jnp.zeros_like(acc_s)

    acc_s[0:1, :] += paired
    acc_s[1:2, :] += gshift[0:1, :] + gshift[1:2, :]

    @pl.when(part == 2)
    def _():
        qkv_grad_pieces(masks, ppr, opr, me_ref, acc_s, gwo_ref, vec_ref, gvec2_ref, e_ref, keep_ref, send_ref, low_s)


def qkv_grad_pieces(masks, ppr, opr, me_ref, acc_s, gwo_ref, vec_ref, gvec2_ref, e_ref, keep_ref, send_ref, low_s):
    width = acc_s.shape[1]
    paired, gshift = acc_s[0:1, :], acc_s[1:2, :]
    ggain = (paired - vec_ref[1:2, :] * gshift) / vec_ref[0:1, :]
    n = 2 * len(masks)
    owner = lax.broadcasted_iota(jnp.int32, (n, width), 1) // opr == lax.broadcasted_iota(jnp.int32, (n, width), 0)
    packed = jnp.zeros((n, 128), F32)
    for v, row in enumerate((ggain, gshift, gvec2_ref[0:1, :], gvec2_ref[1:2, :])):
        packed += mm_nt(jnp.where(owner, row, 0.0).astype(BF16), e_ref[v])
    me = me_ref[0]
    core = lax.rem(me, 2)
    for pair in range(len(masks)):
        slot = slot_of(masks, me, pair)
        sides = []
        for j in (2 * pair, 2 * pair + 1):
            extra = jnp.concatenate([packed[j : j + 1, :], jnp.zeros((1, width - 128), F32)], axis=1)
            extra = jnp.concatenate([extra, jnp.zeros((7, width), F32)], axis=0)
            sides.append((low_s[j * ppr : (j + 1) * ppr, :], gwo_ref[j * opr : (j + 1) * opr, :], extra.astype(BF16)))
        for side in range(2):

            @pl.when(core == side)
            def _():
                for out, part in ((keep_ref, sides[side]), (send_ref, sides[1 - side])):
                    out[slot] = jnp.concatenate(part, axis=0)


def qkv_grad(plan, me, grads, sums, n1, w_abs, gwo, vecs, gvec2, spread):
    rows, width = n1.shape
    masks = plan.slot_masks()
    ppr, opr = 3 * width // plan.n, width // plan.n
    full = lambda a: pl.BlockSpec(a.shape, lambda p, *_: (0,) * len(a.shape))
    shape = jax.ShapeDtypeStruct((len(masks), ppr + opr + 8, width), BF16)
    return pl.pallas_call(
        functools.partial(qkv_grad_kernel, masks, ppr, opr),
        grid_spec=pltpu.PrefetchScalarGridSpec(
            num_scalar_prefetch=1,
            grid=(3,),
            in_specs=[pl.BlockSpec((1, rows, d.shape[2]), lambda p, *_: (p, 0, 0)) for d in grads]
            + [full(a) for a in (*sums, n1)]
            + [pl.BlockSpec((width, width), lambda p, *_: (p, 0))]
            + [full(a) for a in (gwo, vecs, gvec2, spread)],
            out_specs=[full(shape), full(shape)],
            scratch_shapes=[pltpu.VMEM((3 * width, width), BF16), pltpu.VMEM((8, width), F32)],
        ),
        out_shape=[shape, shape],
        compiler_params=params(),
        cost_estimate=cost(6 * rows * width * width, 25e6),
        name="qkv_grad",
    )(me, *grads, *sums, n1, w_abs, gwo, vecs, gvec2, spread)


def qkv_grad_plain_kernel(d_ref, n1_ref, out_ref):
    out_ref[...] = mm_tn(d_ref[...], n1_ref[...]).astype(BF16)


def qkv_grad_plain(grads, n1):
    rows, width = n1.shape
    vm = pl.BlockSpec(memory_space=pltpu.VMEM)
    found = []
    for part in range(3):
        for d in grads:
            call = pl.pallas_call(
                qkv_grad_plain_kernel,
                in_specs=[vm, vm],
                out_specs=vm,
                out_shape=jax.ShapeDtypeStruct((d.shape[2], width), BF16),
                compiler_params=params(),
                name="qkv_grad_plain",
            )
            found.append(call(d[part], n1))
    return jnp.concatenate(found, axis=0)


def first_kernel(d1_ref, d2_ref, w_ref, x_ref, gres_ref, vec_ref, gtok_ref, gvec_ref):
    width = x_ref.shape[1]
    gn = jnp.zeros(x_ref.shape, F32)
    for part in range(3):
        at = part * width
        for ref in (d1_ref, d2_ref):
            gn += mm_nn(ref[part], w_ref[at : at + ref.shape[2], :])
            at += ref.shape[2]
    xhat, rinv = norm_stats(x_ref[...].astype(F32))
    gtok_ref[...] = gres_ref[...] + norm_back(gn, xhat, rinv, vec_ref[0:1, :])

    @pl.when(pl.program_id(0) == 0)
    def _():
        gvec_ref[...] = jnp.zeros_like(gvec_ref)

    gvec_ref[0:1, :] += jnp.sum(gn * xhat, axis=0, keepdims=True)
    gvec_ref[1:2, :] += jnp.sum(gn, axis=0, keepdims=True)


def first_back(grads, w_abs, tokens, gres, vecs, rows_block=256):
    rows, width = tokens.shape
    block = pl.BlockSpec((rows_block, width), lambda r: (r, 0))
    full = lambda shape: pl.BlockSpec(shape, lambda r: (0,) * len(shape))
    return pl.pallas_call(
        first_kernel,
        grid=(rows // rows_block,),
        in_specs=[pl.BlockSpec((3, rows_block, d.shape[2]), lambda r: (0, r, 0)) for d in grads]
        + [full(w_abs.shape), block, block, full(vecs.shape)],
        out_specs=[block, full((8, width))],
        out_shape=[jax.ShapeDtypeStruct((rows, width), F32), jax.ShapeDtypeStruct((8, width), F32)],
        compiler_params=params(),
        cost_estimate=cost(6 * rows * width * width, 25e6),
        name="first_back",
    )(*grads, w_abs, tokens, gres, vecs)


def body(plan, tokens, lengths, ln1_gain, ln1_shift, w_qkv, w_out, ln2_gain, ln2_shift, w_up, w_down, cot):
    rows, width = tokens.shape
    n = plan.n
    seqs = lengths.shape[0]
    me = lax.axis_index(AXES).astype(jnp.int32)
    me_arr = me[None]
    vec_piece = jnp.stack([ln1_gain, ln1_shift, ln2_gain, ln2_shift])
    per = vec_piece.shape[1]
    qkv_piece = w_qkv.T
    ppr, units = qkv_piece.shape[0], w_down.shape[0]
    ff = units * n

    mlp_piece = jnp.concatenate([w_up.T, w_down, w_out], axis=0)
    mlp_all = lax.all_gather(mlp_piece, AXES, axis=0, tiled=True).reshape(n, -1, width)
    if plan.direct:
        w_ff, ff_units, wo_pieces, wo_at = mlp_all, units, mlp_all, 2 * units // per
    else:
        ff_units = 768
        wo_pieces, wo_at = mlp_all[:, 2 * units :].reshape(1, width, width), 0
        w_ff = mlp_all[:, : 2 * units].reshape(n, 2, units, width).transpose(1, 0, 2, 3)
        w_ff = w_ff.reshape(2, ff // 768, 768, width).transpose(1, 0, 2, 3).reshape(ff // 768, 2 * 768, width)

    if plan.direct:
        flat = jnp.pad(vec_piece.reshape(1, -1), ((0, 7), (0, width - 4 * per)))
        gathered = plan.gather(jnp.concatenate([qkv_piece, flat], axis=0))
        slots = jnp.array(plan.slot_masks() + [m ^ 1 for m in plan.slot_masks()], jnp.int32)
        column = jnp.arange(width, dtype=jnp.int32)
        place = ((slots ^ me)[:, None] == (column // per)[None]).astype(F32)
        lane = jnp.arange(128, dtype=jnp.int32)
        spread = jnp.stack([(lane[:, None] == v * per + (column % per)[None]).astype(BF16) for v in range(4)])
        mixed, n1, w_abs, vecs = qkv_project(plan, me_arr, tokens, gathered, spread, place, ppr * n)
    else:
        w_abs = lax.all_gather(qkv_piece, AXES, axis=0, tiled=True)
        vecs = lax.all_gather(vec_piece, AXES, axis=1, tiled=True).astype(F32)
        vecs = jnp.pad(vecs, ((0, 4), (0, 0)))
        mixed, n1 = qkv_plain(tokens, w_abs, vecs)

    att, attT, inv, kept = attend_forward(mixed, lengths)
    residual, n2, wo = project_out(att, tokens, wo_pieces, wo_at, vecs)
    output, gn2, *gw_ff = feed_forward(lengths, me_arr, n2, residual, cot, w_ff, ff_units, plan.direct)
    if plan.direct:
        got = plan.swap(gw_ff[1], 1)
    else:
        gw_ff = gw_ff[0].reshape(ff // 768, 2, 768, width).transpose(1, 0, 2, 3)
        gw_ff = gw_ff.reshape(2, n, units, width).transpose(1, 0, 2, 3).reshape(-1, width)
        g_ff = lax.psum_scatter(gw_ff, AXES, scatter_dimension=0, tiled=True)
    gres, ga, gwo, gvec2 = middle_back(lengths, gn2, residual, cot, att, wo, vecs)
    pairs = width // PAIR
    late = pairs // 6
    if plan.direct:
        ga, got, keep = lax.optimization_barrier((ga, got, gw_ff[0]))
        away = plan.first_away(keep, got)
        back = (plan.swap(away[0], 2), plan.swap(away[1], 4))
        ga, away = lax.optimization_barrier((ga, away))
    grads, sums = attend_backward(mixed, ga, attT, inv, kept, seqs, 0, pairs - late)
    if plan.direct:
        back, grads, ga, sums = lax.optimization_barrier((back, grads, ga, sums))
        away = plan.second_away(keep, got, back)
        again = (plan.swap(away[0], 4), plan.swap(away[1], 2))
        ga, away = lax.optimization_barrier((ga, away))
    more, late_sums = attend_backward(mixed, ga, attT, inv, kept, seqs, pairs - late, late)
    grads, sums = [grads, more], [sums, late_sums]
    if plan.direct:
        q_keep, q_send = qkv_grad(plan, me_arr, grads, sums, n1, w_abs, gwo, vecs, gvec2, spread)
        again, q_keep, q_send = lax.optimization_barrier((again, q_keep, q_send))
        whole, q_keep = lax.optimization_barrier((plan.last_sum(keep, got, back, again), q_keep))
        g_ff = plan.along_sum(whole)
        summed = plan.scatter_first(q_keep, q_send)
        gres, summed = lax.optimization_barrier((gres, summed))
        g_attn, g_ff = plan.scatter_rest(summed, g_ff)
        g_attn = g_attn.astype(F32)
        g_qkv, g_out = g_attn[:ppr], g_attn[ppr : ppr + per]
        g_vec = g_attn[ppr + per, : 4 * per].reshape(4, per)
    else:
        g_qkv = lax.psum_scatter(qkv_grad_plain(grads, n1), AXES, scatter_dimension=0, tiled=True)
        g_out = lax.psum_scatter(gwo, AXES, scatter_dimension=0, tiled=True)
    gtok, gvec1 = first_back(grads, w_abs, tokens, gres, vecs)
    if not plan.direct:
        gvec = jnp.concatenate([gvec1[:2], gvec2[:2]], axis=0)
        g_vec = lax.psum_scatter(gvec, AXES, scatter_dimension=1, tiled=True)
    g_ff = g_ff.astype(F32)
    return (
        output, gtok, g_vec[0], g_vec[1], g_qkv.astype(F32).T, g_out.astype(F32), g_vec[2], g_vec[3],
        g_ff[:units].T, g_ff[units:],
    )


def solution(mesh):
    both = AXES
    rows2, vec, cols2 = P(both, None), P(both), P(None, both)
    in_specs = (rows2, vec, vec, vec, cols2, rows2, vec, vec, cols2, rows2, rows2)
    out_specs = (rows2, rows2, vec, vec, cols2, rows2, vec, vec, cols2, rows2)
    return jax.shard_map(
        functools.partial(body, Plan(mesh)), mesh=mesh, in_specs=in_specs, out_specs=out_specs, check_vma=False
    )
```

```python
import functools
import math

import jax
import jax.numpy as jnp
from jax import lax
from jax.experimental import pallas as pl
from jax.experimental.pallas import tpu as pltpu
from jax.sharding import PartitionSpec as P

F32 = jnp.float32
BF16 = jnp.bfloat16
HEAD = 64
PAIR = 2 * HEAD
EPSILON = 1e-05
NEGATIVE = -1e30
TILE = 256
CHUNK = 32
AXES = ("dp", "fsdp")
VMEM_LIMIT = 56 << 20
GELU_A = math.sqrt(2.0 / math.pi)
GELU_B = GELU_A * 0.044715


def mm_nn(left, right):
    return jnp.dot(left, right, preferred_element_type=F32)


def mm_nt(left, right):
    return lax.dot_general(left, right, (((1,), (1,)), ((), ())), preferred_element_type=F32)


def mm_tn(left, right):
    return lax.dot_general(left, right, (((0,), (0,)), ((), ())), preferred_element_type=F32)


def norm_stats(values):
    average = jnp.mean(values, axis=-1, keepdims=True)
    centred = values - average
    variance = jnp.mean(centred * centred, axis=-1, keepdims=True)
    rinv = lax.rsqrt(variance + EPSILON)
    return centred * rinv, rinv


def params(**kw):
    return pltpu.CompilerParams(vmem_limit_bytes=VMEM_LIMIT, **kw)


def cost(flops, moved):
    return pl.CostEstimate(flops=int(flops), bytes_accessed=int(moved), transcendentals=0)


class Plan:
    def __init__(self, mesh):
        self.n = mesh.shape["dp"] * mesh.shape["fsdp"]
        self.bits = self.n.bit_length() - 1
        self.direct = self.n == 1 << self.bits and self.bits == 5 and mesh.shape["fsdp"] == 4
        self.along = (3, 4)
        self.across = (1, 2)

    @staticmethod
    def masks_of(bits):
        found = [0]
        for bit in bits:
            found = found + [m | 1 << bit for m in found]
        return found

    def slot_masks(self):
        return [m ^ k for m in self.masks_of(self.across) for k in self.masks_of(self.along)]

    def swap(self, value, mask):
        return lax.ppermute(value, AXES, [(i, i ^ mask) for i in range(self.n)])

    def spread_stage(self, held, bits):
        return jnp.concatenate([held] + [self.swap(held, m) for m in self.masks_of(bits)[1:]], axis=0)

    def gather(self, piece):
        held = self.spread_stage(self.spread_stage(piece[None], self.along), self.across)
        return held, self.swap(held, 1)

    def scatter_first(self, keep, send, cut):
        got = self.swap(send, 1)
        grid = (2, 2, -1) + keep.shape[1:]
        keep, got = keep.reshape(grid), got.reshape(grid)
        pair = lambda at: add_low(keep[at], [got[at]])
        every, head, tail = slice(None), slice(None, cut), slice(cut, None)
        one = [pair((every, y, every, head)) for y in range(2)]
        two = [pair((x, every, every, tail)) for x in range(2)]
        return one, two

    def scatter_rest(self, one, two, beside):
        inner = self.masks_of(self.along)
        arriving = self.swap(one[1], 2), self.swap(two[1], 4)
        stay = [add_low(own[0][0], [got[0]]) for own, got in ((one, arriving[0]), (two, arriving[1]))]
        goes = [add_low(own[0][1], [got[1]]) for own, got in ((one, arriving[0]), (two, arriving[1]))]
        got = self.swap(goes[0], 4), self.swap(goes[1], 2)
        held = jnp.concatenate([add_low(stay[0], [got[0]]), add_low(stay[1], [got[1]])], axis=1)
        arriving = [self.swap(held[z], m) for z, m in list(enumerate(inner))[1:]]
        arriving[0], beside = lax.optimization_barrier((arriving[0], beside))
        return add_low(held[0], arriving), beside

    def view(self, held):
        pieces, rows, width = held.shape
        return held.reshape(pieces // 4, 2, 2, 2, rows // 2, width)

    def first_away(self, keep, got):
        k, g = self.view(keep), self.view(got)
        return add_low(k[:, :, 1, 0], [g[:, :, 1, 0]]), add_low(k[:, 1, :, 1], [g[:, 1, :, 1]])

    def second_away(self, keep, got, back):
        k, g = self.view(keep), self.view(got)
        return (
            add_low(k[:, 1, 0, 0], [g[:, 1, 0, 0], back[0][:, 1]]),
            add_low(k[:, 0, 1, 1], [g[:, 0, 1, 1], back[1][:, 1]]),
        )

    def last_sum(self, keep, got, back, again):
        k, g = self.view(keep), self.view(got)
        both = [
            add_low(k[:, 0, 0, half], [g[:, 0, 0, half], back[half][:, 0], again[half]]) for half in range(2)
        ]
        whole = jnp.concatenate(both, axis=1)
        return whole.reshape(-1, whole.shape[-1])

    def along_sum(self, whole):
        line = [[r + 8 * z for z in range(self.n // 8)] for r in range(8)]
        return lax.psum_scatter(whole, AXES, scatter_dimension=0, tiled=True, axis_index_groups=line)


def add_low(first, others):
    total = first.astype(F32)
    for other in others:
        total = total + other.astype(F32)
    return total.astype(first.dtype)


def slot_of(masks, me, piece_pair):
    wanted = piece_pair ^ lax.div(me, 2)
    slot = jnp.int32(0)
    for s, m in enumerate(masks):
        slot = jnp.where(wanted == m // 2, s, slot)
    return slot


def qkv_kernel(masks, ppr, me_ref, x_ref, own_ref, sib_ref, e_ref, m_ref, mixed_ref, n1_ref, w_ref, vec_ref):
    me = me_ref[0]

    @pl.when(pl.program_id(0) == 0)
    def _():
        core = lax.rem(me, 2)
        for s, m in enumerate(masks):
            pair = lax.div(me, 2) ^ (m // 2)
            at = pl.ds(pl.multiple_of(pair * (2 * ppr), 16), 2 * ppr)
            both = [own_ref[s, :ppr, :], sib_ref[s, :ppr, :]]
            for side in range(2):

                @pl.when(core == side)
                def _():
                    w_ref[at, :] = jnp.concatenate([both[side], both[1 - side]], axis=0)

        packed = jnp.concatenate([own_ref[:, ppr, :128], sib_ref[:, ppr, :128]], axis=0)
        for v in range(4):
            vec_ref[v : v + 1, :] = jnp.sum(mm_nn(packed, e_ref[v]) * m_ref[...], axis=0, keepdims=True)

    xhat, rinv = norm_stats(x_ref[...].astype(F32))
    n1 = (xhat * vec_ref[0:1, :] + vec_ref[1:2, :]).astype(BF16)
    n1_ref[...] = n1
    mixed_ref[...] = mm_nt(n1, w_ref[...]).astype(BF16)


def qkv_project(plan, me, tokens, gathered, spread, place, out_cols, rows_block=256):
    rows, width = tokens.shape
    masks = plan.slot_masks()
    full = lambda a: pl.BlockSpec(a.shape, lambda r, *_: (0,) * a.ndim)
    whole = lambda shape: pl.BlockSpec(shape, lambda r, *_: (0,) * len(shape))
    return pl.pallas_call(
        functools.partial(qkv_kernel, masks, out_cols // plan.n),
        grid_spec=pltpu.PrefetchScalarGridSpec(
            num_scalar_prefetch=1,
            grid=(rows // rows_block,),
            in_specs=[
                pl.BlockSpec((rows_block, width), lambda r, *_: (r, 0)),
            ]
            + [full(a) for a in (*gathered, spread, place)],
            out_specs=[
                pl.BlockSpec((rows_block, out_cols), lambda r, *_: (r, 0)),
                pl.BlockSpec((rows_block, width), lambda r, *_: (r, 0)),
                whole((out_cols, width)), whole((8, width)),
            ],
        ),
        out_shape=[
            jax.ShapeDtypeStruct((rows, out_cols), BF16),
            jax.ShapeDtypeStruct((rows, width), BF16),
            jax.ShapeDtypeStruct((out_cols, width), BF16),
            jax.ShapeDtypeStruct((8, width), F32),
        ],
        compiler_params=params(),
        cost_estimate=cost(2 * rows * width * out_cols, 20e6),
        name="qkv_project",
    )(me, tokens, *gathered, spread, place)


def qkv_plain_kernel(x_ref, w_ref, vec_ref, mixed_ref, n1_ref):
    xhat, rinv = norm_stats(x_ref[...].astype(F32))
    n1 = (xhat * vec_ref[0:1, :] + vec_ref[1:2, :]).astype(BF16)
    n1_ref[...] = n1
    mixed_ref[...] = mm_nt(n1, w_ref[...]).astype(BF16)


def qkv_plain(tokens, w_abs, vecs, rows_block=256):
    rows, width = tokens.shape
    out_cols = w_abs.shape[0]
    full = lambda a: pl.BlockSpec(a.shape, lambda r: (0,) * a.ndim)
    return pl.pallas_call(
        qkv_plain_kernel,
        grid=(rows // rows_block,),
        in_specs=[pl.BlockSpec((rows_block, width), lambda r: (r, 0)), full(w_abs), full(vecs)],
        out_specs=[
            pl.BlockSpec((rows_block, out_cols), lambda r: (r, 0)),
            pl.BlockSpec((rows_block, width), lambda r: (r, 0)),
        ],
        out_shape=[
            jax.ShapeDtypeStruct((rows, out_cols), BF16),
            jax.ShapeDtypeStruct((rows, width), BF16),
        ],
        compiler_params=params(),
        name="qkv_plain",
    )(tokens, w_abs, vecs)


def tile_at(i, j):
    return i * (i + 1) // 2 + j

def attend_kernel(maxlen, len_ref, q_ref, k_ref, v_ref, att_ref, attT_ref, inv_ref, keep_ref):
    length = len_ref[pl.program_id(0)]
    q, k = q_ref[...], k_ref[...]
    qT = (q.astype(F32) * HEAD**-0.5).T.astype(BF16)
    vT = v_ref[...].astype(F32).T.astype(BF16)
    same = lax.broadcasted_iota(jnp.int32, (PAIR, PAIR), 0) // HEAD == lax.broadcasted_iota(jnp.int32, (PAIR, PAIR), 1) // HEAD
    same = jnp.where(same, 1.0, 0.0).astype(BF16)
    square = lambda a: jnp.max(mm_nn((a.astype(F32) * a.astype(F32)).astype(BF16), same))
    small = square(q) * square(k) * (1.03 / HEAD) < 70.0**2

    def block(i, plain):
        lo, hi = i * TILE, (i + 1) * TILE
        qpos = lo + lax.broadcasted_iota(jnp.int32, (1, TILE), 1)
        limit = jnp.minimum(qpos, length - 1)
        blank = jnp.zeros((HEAD, TILE), BF16)
        outs = []
        for h in range(2):
            own = qT[h * HEAD : (h + 1) * HEAD, lo:hi]
            own = jnp.concatenate([own, blank] if h == 0 else [blank, own], axis=0)

            def piece(at):
                s = mm_nn(k[at : at + CHUNK], own)
                t = s * s + 1.0
                r = lax.rsqrt(t)
                kpos = at + lax.broadcasted_iota(jnp.int32, (CHUNK, TILE), 0)
                return s, r, t * r, (kpos <= limit if at >= lo else kpos < length)

            top = None
            if not plain:
                for at in range(0, hi, CHUNK):
                    s, r, smooth, allowed = piece(at)
                    here = jnp.max(jnp.where(allowed, smooth, NEGATIVE), axis=0, keepdims=True)
                    top = here if top is None else jnp.maximum(top, here)
            total, weights = None, []
            for at in range(0, hi, CHUNK):
                s, r, smooth, allowed = piece(at)
                e = jnp.exp(smooth) if plain else jnp.exp(jnp.minimum(smooth - top, 0.0))
                e = jnp.where(allowed, e, 0.0)
                part = e.reshape(CHUNK // 8, 8, TILE).sum(axis=0)
                total = part if total is None else total + part
                g = jnp.tanh(s)
                w = g * e
                c = e * (s * r)
                a = e + g * (c - w)
                w = w.astype(BF16)
                weights.append(w)
                tile, row = tile_at(i, at // TILE), at % TILE
                keep_ref[0, h, 0, tile, row : row + CHUNK, :] = w
                keep_ref[0, h, 1, tile, row : row + CHUNK, :] = a.astype(BF16)
                keep_ref[0, h, 2, tile, row : row + CHUNK, :] = c.astype(BF16)
            inv = 1.0 / jnp.sum(total, axis=0, keepdims=True)
            inv_ref[0, h : h + 1, lo:hi] = inv
            outs.append(mm_nn(vT[h * HEAD : (h + 1) * HEAD, :hi], jnp.concatenate(weights, axis=0)) * inv)
        outT = jnp.concatenate(outs, axis=0)
        attT_ref[:, lo:hi] = outT.astype(BF16)
        att_ref[lo:hi, :] = outT.T.astype(BF16)

    @pl.when(small)
    def _():
        for i in range(maxlen // TILE):
            block(i, True)

    @pl.when(jnp.logical_not(small))
    def _():
        for i in range(maxlen // TILE):
            block(i, False)


def attend_forward(mixed, lengths):
    rows, width = mixed.shape[0], mixed.shape[1] // 3
    seqs = lengths.shape[0]
    maxlen, pairs = rows // seqs, width // PAIR
    tiles = tile_at(maxlen // TILE, 0)
    col = lambda part: pl.BlockSpec((maxlen, PAIR), lambda s, p, *_: (s, part * pairs + p))
    return pl.pallas_call(
        functools.partial(attend_kernel, maxlen),
        grid_spec=pltpu.PrefetchScalarGridSpec(
            num_scalar_prefetch=1,
            grid=(seqs, pairs),
            in_specs=[col(0), col(1), col(2)],
            out_specs=[
                col(0),
                pl.BlockSpec((PAIR, maxlen), lambda s, p, *_: (p, s)),
                pl.BlockSpec((1, 8, maxlen), lambda s, p, *_: (s * pairs + p, 0, 0)),
                pl.BlockSpec((1, 2, 3, tiles, TILE, TILE), lambda s, p, *_: (s * pairs + p, 0, 0, 0, 0, 0)),
            ],
        ),
        out_shape=[
            jax.ShapeDtypeStruct((rows, width), BF16),
            jax.ShapeDtypeStruct((width, rows), BF16),
            jax.ShapeDtypeStruct((seqs * pairs, 8, maxlen), F32),
            jax.ShapeDtypeStruct((seqs * pairs, 2, 3, tiles, TILE, TILE), BF16),
        ],
        compiler_params=params(),
        cost_estimate=cost(20e9, 60e6),
        name="attend_forward",
    )(lengths, mixed, mixed, mixed)


def attend_back_kernel(maxlen, q_ref, k_ref, v_ref, ga_ref, attT_ref, inv_ref, keep_ref, d_ref, sum_ref, dqT):
    qs = q_ref[...] * jnp.asarray(HEAD**-0.5, BF16)
    v = v_ref[...]
    kT = k_ref[...].astype(F32).T.astype(BF16)
    gaT = ga_ref[...].astype(F32).T
    prod = gaT * attT_ref[...].astype(F32)
    half = lambda h: slice(h * HEAD, (h + 1) * HEAD)
    inv = [inv_ref[0, h : h + 1, :] for h in range(2)]
    gaT = jnp.concatenate([gaT[half(h)] * inv[h] for h in range(2)], axis=0)
    ga = gaT.T.astype(BF16)
    gaT = gaT.astype(BF16)
    lane = lax.broadcasted_iota(jnp.int32, (maxlen, PAIR), 1)
    blank = jnp.zeros((HEAD, maxlen), BF16)
    nil = jnp.zeros((), BF16)
    heads = []
    for h in range(2):
        mine = (lane < HEAD) if h == 0 else (lane >= HEAD)
        own = gaT[half(h)]
        heads.append(
            (
                jnp.where(mine, ga, nil), jnp.where(mine, qs, nil),
                jnp.concatenate([own, blank] if h == 0 else [blank, own], axis=0), kT[half(h)],
                jnp.sum(prod[half(h)], axis=0, keepdims=True) * inv[h],
            )
        )
    blocks = maxlen // TILE
    for j in range(blocks):
        lo, hi = j * TILE, (j + 1) * TILE
        dv = dk = None
        for h in range(2):
            ga_h, q_h, gaT_h, kT_h, delta = heads[h]
            side = lambda part: jnp.concatenate([keep_ref[0, h, part, tile_at(i, j)] for i in range(j, blocks)], axis=1)
            gw = mm_nn(v[lo:hi], gaT_h[:, lo:])
            ds = (gw * side(1).astype(F32) - side(2).astype(F32) * delta[:, lo:]).astype(BF16)
            dv_h = mm_nn(side(0), ga_h[lo:])
            dk_h = mm_nn(ds, q_h[lo:])
            dv = dv_h if dv is None else dv + dv_h
            dk = dk_h if dk is None else dk + dk_h
            dq_h = mm_nn(kT_h[:, lo:hi], ds)
            if j == 0:
                dqT[half(h), :] = dq_h
            else:
                dqT[half(h), lo:] += dq_h
        d_ref[2, lo:hi, :] = dv.astype(BF16)
        d_ref[1, lo:hi, :] = dk.astype(BF16)
        sums = [jnp.sum(d, axis=0, keepdims=True) for d in (dk, dv)]
        total = sums if j == 0 else [t + d for t, d in zip(total, sums)]
    dq = (dqT[...] * HEAD**-0.5).T
    d_ref[0] = dq.astype(BF16)
    total = [jnp.sum(dq, axis=0, keepdims=True)] + total
    sum_ref[0] = jnp.concatenate(total + [jnp.zeros((5, PAIR), F32)], axis=0)


def attend_backward(mixed, ga, attT, inv, keep, seqs, first, count):
    rows, width = mixed.shape[0], mixed.shape[1] // 3
    maxlen, pairs = rows // seqs, width // PAIR
    col = lambda part: pl.BlockSpec((maxlen, PAIR), lambda s, p: (s, part * pairs + p + first))
    return pl.pallas_call(
        functools.partial(attend_back_kernel, maxlen),
        grid=(seqs, count),
        in_specs=[
            col(0), col(1), col(2), col(0),
            pl.BlockSpec((PAIR, maxlen), lambda s, p: (p + first, s)),
            pl.BlockSpec((1, 8, maxlen), lambda s, p: (s * pairs + p + first, 0, 0)),
            pl.BlockSpec((1,) + keep.shape[1:], lambda s, p: (s * pairs + p + first, 0, 0, 0, 0, 0)),
        ],
        out_specs=[
            pl.BlockSpec((3, maxlen, PAIR), lambda s, p: (0, s, p)),
            pl.BlockSpec((1, 8, PAIR), lambda s, p: (s, 0, p)),
        ],
        out_shape=[
            jax.ShapeDtypeStruct((3, rows, count * PAIR), BF16),
            jax.ShapeDtypeStruct((seqs, 8, count * PAIR), F32),
        ],
        scratch_shapes=[pltpu.VMEM((PAIR, maxlen), F32)],
        compiler_params=params(),
        cost_estimate=cost(5e9 * count, 10e6 * count),
        name="attend_backward",
    )(mixed, mixed, mixed, ga, attT, inv, keep)


def project_kernel(att_ref, x_ref, wp_ref, vec_ref, res_ref, n2_ref, wo_ref):
    pieces, per, _ = wp_ref.shape

    @pl.when(pl.program_id(0) == 0)
    def _():
        for p in range(pieces):
            wo_ref[p * per : (p + 1) * per, :] = wp_ref[p]

    residual = x_ref[...].astype(F32) + mm_nn(att_ref[...], wo_ref[...])
    res_ref[...] = residual
    xhat, rinv = norm_stats(residual)
    n2_ref[...] = (xhat * vec_ref[2:3, :] + vec_ref[3:4, :]).astype(BF16)


def project_out(att, tokens, wo_pieces, at, vecs, rows_block=512):
    rows, width = tokens.shape
    pieces = wo_pieces.shape[0]
    block = pl.BlockSpec((rows_block, width), lambda r: (r, 0))
    full = lambda a: pl.BlockSpec(a.shape, lambda r: (0,) * a.ndim)
    return pl.pallas_call(
        project_kernel,
        grid=(rows // rows_block,),
        in_specs=[
            block, block, pl.BlockSpec((pieces, width // pieces, width), lambda r: (0, at, 0)), full(vecs),
        ],
        out_specs=[block, block, pl.BlockSpec((width, width), lambda r: (0, 0))],
        out_shape=[
            jax.ShapeDtypeStruct((rows, width), F32),
            jax.ShapeDtypeStruct((rows, width), BF16),
            jax.ShapeDtypeStruct((width, width), BF16),
        ],
        compiler_params=params(),
        cost_estimate=cost(2 * rows * width * width, 10e6),
        name="project_out",
    )(att, tokens, wo_pieces, vecs)


def live_grad(cot, lengths_ref, maxlen, first_row):
    rows = cot.shape[0]
    at = first_row + lax.broadcasted_iota(jnp.int32, (rows, 1), 0)
    seq = first_row // maxlen
    return jnp.where(at - seq * maxlen < lengths_ref[seq], cot, 0.0)


def mlp_kernel(units, me_ref, n2_ref, gl_ref, w_ref, res_ref, out_ref, gn_ref, *rest):
    *gw_refs, acc_s, res_s, sem = rest
    step = pl.program_id(0)
    rows, width = n2_ref.shape

    @pl.when(step == 0)
    def _():
        pltpu.make_async_copy(res_ref, res_s, sem).start()

    pieces = w_ref.shape[0]
    wu = w_ref[:, :units, :].reshape(pieces * units, width)
    wd = w_ref[:, units : 2 * units, :].reshape(pieces * units, width)
    n2, gl = n2_ref[...], gl_ref[...]
    u = mm_nt(n2, wu)
    uu = u * u
    th = jnp.tanh(u * (GELU_A + GELU_B * uu))
    half = 0.5 * u
    act = (half + half * th).astype(BF16)
    slope = 0.5 + 0.5 * th + (half - half * (th * th)) * (GELU_A + (3.0 * GELU_B) * uu)
    gp = (mm_nt(gl, wd) * slope).astype(BF16)
    out = mm_nn(act, wd)
    gn = mm_nn(gp, wu)

    @pl.when(step == 0)
    def _():
        acc_s[...] = out
        gn_ref[...] = gn

    @pl.when(step > 0)
    def _():
        acc_s[...] += out
        gn_ref[...] += gn

    for at, grad in ((0, mm_tn(gp, n2)), (units, mm_tn(act, gl))):
        grad = grad.astype(BF16)
        if len(gw_refs) == 1:
            gw_refs[0][:, at : at + units, :] = grad.reshape(pieces, units, width)
            continue
        grad = grad.reshape(pieces // 2, 2, units, width)
        core = lax.rem(me_ref[0], 2)
        near = lax.rem(lax.div(me_ref[0], 2), 4)
        for side in range(2):

            @pl.when(core == side)
            def _():
                for place in range(pieces // 2):
                    slot = (place // 4) * 4 + ((place % 4) ^ near)
                    gw_refs[0][slot, at : at + units, :] = grad[place, side]
                    gw_refs[1][slot, at : at + units, :] = grad[place, 1 - side]

    @pl.when(step == pl.num_programs(0) - 1)
    def _():
        pltpu.make_async_copy(res_ref, res_s, sem).wait()
        out_ref[...] = (acc_s[...] + res_s[...]).astype(BF16)


def feed_forward(me, n2, residual, gl, w, units, split):
    rows, width = n2.shape
    pieces, held, _ = w.shape
    take = max(1, 768 // units)
    full = lambda: pl.BlockSpec((rows, width), lambda f, *_: (0, 0))
    outs = 2 if split else 1
    grads = [pl.BlockSpec((take // outs, 2 * units, width), lambda f, *_: (f, 0, 0))] * outs
    return pl.pallas_call(
        functools.partial(mlp_kernel, units),
        grid_spec=pltpu.PrefetchScalarGridSpec(
            num_scalar_prefetch=1,
            grid=(pieces // take,),
            in_specs=[
                full(), full(), pl.BlockSpec((take, held, width), lambda f, *_: (f, 0, 0)),
                pl.BlockSpec(memory_space=pl.ANY),
            ],
            out_specs=[full(), full()] + grads,
            scratch_shapes=[pltpu.VMEM((rows, width), F32)] * 2 + [pltpu.SemaphoreType.DMA],
        ),
        out_shape=[jax.ShapeDtypeStruct((rows, width), BF16), jax.ShapeDtypeStruct((rows, width), F32)]
        + [jax.ShapeDtypeStruct((pieces // outs, 2 * units, width), BF16)] * outs,
        compiler_params=params(),
        cost_estimate=cost(12 * rows * width * pieces * units, 40e6),
        name="feed_forward",
    )(me, n2, gl, w, residual)


def norm_back(grad, xhat, rinv, gain):
    dh = grad * gain
    first = jnp.mean(dh, axis=-1, keepdims=True)
    second = jnp.mean(dh * xhat, axis=-1, keepdims=True)
    return rinv * (dh - first - xhat * second)


def middle_kernel(maxlen, len_ref, gn_ref, res_ref, cot_ref, att_ref, wo_ref, vec_ref, gres_ref, ga_ref, gwo_ref, gvec_ref, low_s):
    step = pl.program_id(0)
    rows = gn_ref.shape[0]
    gn = gn_ref[...]
    xhat, rinv = norm_stats(res_ref[...])
    gres = live_grad(cot_ref[...], len_ref, maxlen, step * rows) + norm_back(gn, xhat, rinv, vec_ref[2:3, :])
    gres_ref[...] = gres
    low = gres.astype(BF16)
    low_s[pl.ds(pl.multiple_of(step * rows, rows), rows), :] = low
    ga_ref[...] = mm_nt(low, wo_ref[...]).astype(BF16)

    @pl.when(step == 0)
    def _():
        gvec_ref[...] = jnp.zeros_like(gvec_ref)

    gvec_ref[0:1, :] += jnp.sum(gn * xhat, axis=0, keepdims=True)
    gvec_ref[1:2, :] += jnp.sum(gn, axis=0, keepdims=True)

    @pl.when(step == pl.num_programs(0) - 1)
    def _():
        gwo_ref[...] = mm_tn(att_ref[...], low_s[...]).astype(BF16)


def middle_back(lengths, gn, residual, cot, att, wo, vecs):
    rows, width = gn.shape
    rows_block = rows // lengths.shape[0]
    block = pl.BlockSpec((rows_block, width), lambda r, *_: (r, 0))
    full = lambda shape: pl.BlockSpec(shape, lambda r, *_: (0,) * len(shape))
    return pl.pallas_call(
        functools.partial(middle_kernel, rows // lengths.shape[0]),
        grid_spec=pltpu.PrefetchScalarGridSpec(
            num_scalar_prefetch=1,
            grid=(rows // rows_block,),
            in_specs=[block, block, block, full(att.shape), full(wo.shape), full(vecs.shape)],
            out_specs=[block, block, full(wo.shape), full((8, width))],
            scratch_shapes=[pltpu.VMEM((rows, width), BF16)],
        ),
        out_shape=[
            jax.ShapeDtypeStruct((rows, width), F32),
            jax.ShapeDtypeStruct((rows, width), BF16),
            jax.ShapeDtypeStruct(wo.shape, BF16),
            jax.ShapeDtypeStruct((8, width), F32),
        ],
        compiler_params=params(),
        cost_estimate=cost(4 * rows * width * width, 30e6),
        name="middle_back",
    )(lengths, gn, residual, cot, att, wo, vecs)


def qkv_grad_kernel(masks, ppr, opr, me_ref, *refs):
    d1_ref, d2_ref, sum1_ref, sum2_ref, n1_ref, w_ref, gwo_ref, vec_ref, gvec2_ref, e_ref, keep_ref, send_ref, low_s, acc_s = refs
    rows, width = n1_ref.shape
    part = pl.program_id(0)
    n1 = n1_ref[...]
    paired, gshift, at = jnp.zeros((1, width), F32), jnp.zeros((8, width), F32), 0
    for d_ref, sum_ref in ((d1_ref, sum1_ref), (d2_ref, sum2_ref)):
        cols = d_ref.shape[2]
        gw = mm_tn(d_ref[0], n1)
        low_s[pl.ds(pl.multiple_of(part * width + at, PAIR), cols), :] = gw.astype(BF16)
        w = w_ref[at : at + cols, :]
        paired += jnp.sum(gw * w.astype(F32), axis=0, keepdims=True)
        total = jnp.sum(sum_ref[...], axis=0)
        pick = lax.broadcasted_iota(jnp.int32, (8, 1), 0) == part
        total = jnp.sum(jnp.where(pick, total, 0.0), axis=0, keepdims=True)
        high = total.astype(BF16).astype(F32)
        low = jnp.concatenate([high, total - high, jnp.zeros((6, cols), F32)], axis=0)
        gshift += mm_nn(low.astype(BF16), w)
        at += cols

    @pl.when(part == 0)
    def _():
        acc_s[...] = jnp.zeros_like(acc_s)

    acc_s[0:1, :] += paired
    acc_s[1:2, :] += gshift[0:1, :] + gshift[1:2, :]

    @pl.when(part == 2)
    def _():
        qkv_grad_pieces(masks, ppr, opr, me_ref, acc_s, gwo_ref, vec_ref, gvec2_ref, e_ref, keep_ref, send_ref, low_s)


def qkv_grad_pieces(masks, ppr, opr, me_ref, acc_s, gwo_ref, vec_ref, gvec2_ref, e_ref, keep_ref, send_ref, low_s):
    width = acc_s.shape[1]
    paired, gshift = acc_s[0:1, :], acc_s[1:2, :]
    ggain = (paired - vec_ref[1:2, :] * gshift) / vec_ref[0:1, :]
    n = 2 * len(masks)
    owner = lax.broadcasted_iota(jnp.int32, (n, width), 1) // opr == lax.broadcasted_iota(jnp.int32, (n, width), 0)
    packed = jnp.zeros((n, 128), F32)
    for v, row in enumerate((ggain, gshift, gvec2_ref[0:1, :], gvec2_ref[1:2, :])):
        packed += mm_nt(jnp.where(owner, row, 0.0).astype(BF16), e_ref[v])
    me = me_ref[0]
    core = lax.rem(me, 2)
    for pair in range(len(masks)):
        slot = slot_of(masks, me, pair)
        sides = []
        for j in (2 * pair, 2 * pair + 1):
            extra = jnp.concatenate([packed[j : j + 1, :], jnp.zeros((1, width - 128), F32)], axis=1)
            extra = jnp.concatenate([extra, jnp.zeros((7, width), F32)], axis=0)
            sides.append((low_s[j * ppr : (j + 1) * ppr, :], gwo_ref[j * opr : (j + 1) * opr, :], extra.astype(BF16)))
        for side in range(2):

            @pl.when(core == side)
            def _():
                for out, part in ((keep_ref, sides[side]), (send_ref, sides[1 - side])):
                    out[slot] = jnp.concatenate(part, axis=0)


def qkv_grad(plan, me, grads, sums, n1, w_abs, gwo, vecs, gvec2, spread):
    rows, width = n1.shape
    masks = plan.slot_masks()
    ppr, opr = 3 * width // plan.n, width // plan.n
    full = lambda a: pl.BlockSpec(a.shape, lambda p, *_: (0,) * len(a.shape))
    shape = jax.ShapeDtypeStruct((len(masks), ppr + opr + 8, width), BF16)
    return pl.pallas_call(
        functools.partial(qkv_grad_kernel, masks, ppr, opr),
        grid_spec=pltpu.PrefetchScalarGridSpec(
            num_scalar_prefetch=1,
            grid=(3,),
            in_specs=[pl.BlockSpec((1, rows, d.shape[2]), lambda p, *_: (p, 0, 0)) for d in grads]
            + [full(a) for a in (*sums, n1)]
            + [pl.BlockSpec((width, width), lambda p, *_: (p, 0))]
            + [full(a) for a in (gwo, vecs, gvec2, spread)],
            out_specs=[full(shape), full(shape)],
            scratch_shapes=[pltpu.VMEM((3 * width, width), BF16), pltpu.VMEM((8, width), F32)],
        ),
        out_shape=[shape, shape],
        compiler_params=params(),
        cost_estimate=cost(6 * rows * width * width, 25e6),
        name="qkv_grad",
    )(me, *grads, *sums, n1, w_abs, gwo, vecs, gvec2, spread)


def qkv_grad_plain_kernel(d_ref, n1_ref, out_ref):
    out_ref[...] = mm_tn(d_ref[...], n1_ref[...]).astype(BF16)


def qkv_grad_plain(grads, n1):
    rows, width = n1.shape
    vm = pl.BlockSpec(memory_space=pltpu.VMEM)
    found = []
    for part in range(3):
        for d in grads:
            call = pl.pallas_call(
                qkv_grad_plain_kernel,
                in_specs=[vm, vm],
                out_specs=vm,
                out_shape=jax.ShapeDtypeStruct((d.shape[2], width), BF16),
                compiler_params=params(),
                name="qkv_grad_plain",
            )
            found.append(call(d[part], n1))
    return jnp.concatenate(found, axis=0)


def first_kernel(d1_ref, d2_ref, w_ref, x_ref, gres_ref, vec_ref, gtok_ref, gvec_ref):
    width = x_ref.shape[1]
    gn = jnp.zeros(x_ref.shape, F32)
    for part in range(3):
        at = part * width
        for ref in (d1_ref, d2_ref):
            gn += mm_nn(ref[part], w_ref[at : at + ref.shape[2], :])
            at += ref.shape[2]
    xhat, rinv = norm_stats(x_ref[...].astype(F32))
    gtok_ref[...] = gres_ref[...] + norm_back(gn, xhat, rinv, vec_ref[0:1, :])

    @pl.when(pl.program_id(0) == 0)
    def _():
        gvec_ref[...] = jnp.zeros_like(gvec_ref)

    gvec_ref[0:1, :] += jnp.sum(gn * xhat, axis=0, keepdims=True)
    gvec_ref[1:2, :] += jnp.sum(gn, axis=0, keepdims=True)


def first_back(grads, w_abs, tokens, gres, vecs, rows_block=256):
    rows, width = tokens.shape
    block = pl.BlockSpec((rows_block, width), lambda r: (r, 0))
    full = lambda shape: pl.BlockSpec(shape, lambda r: (0,) * len(shape))
    return pl.pallas_call(
        first_kernel,
        grid=(rows // rows_block,),
        in_specs=[pl.BlockSpec((3, rows_block, d.shape[2]), lambda r: (0, r, 0)) for d in grads]
        + [full(w_abs.shape), block, block, full(vecs.shape)],
        out_specs=[block, full((8, width))],
        out_shape=[jax.ShapeDtypeStruct((rows, width), F32), jax.ShapeDtypeStruct((8, width), F32)],
        compiler_params=params(),
        cost_estimate=cost(6 * rows * width * width, 25e6),
        name="first_back",
    )(*grads, w_abs, tokens, gres, vecs)


def body(plan, tokens, lengths, ln1_gain, ln1_shift, w_qkv, w_out, ln2_gain, ln2_shift, w_up, w_down, cot):
    rows, width = tokens.shape
    n = plan.n
    seqs = lengths.shape[0]
    me = lax.axis_index(AXES).astype(jnp.int32)
    me_arr = me[None]
    vec_piece = jnp.stack([ln1_gain, ln1_shift, ln2_gain, ln2_shift])
    per = vec_piece.shape[1]
    qkv_piece = w_qkv.T
    ppr, units = qkv_piece.shape[0], w_down.shape[0]
    ff = units * n

    mlp_piece = jnp.concatenate([w_up.T, w_down, w_out], axis=0)
    mlp_all = lax.all_gather(mlp_piece, AXES, axis=0, tiled=True).reshape(n, -1, width)
    if plan.direct:
        w_ff, ff_units, wo_pieces, wo_at = mlp_all, units, mlp_all, 2 * units // per
    else:
        ff_units = 768
        wo_pieces, wo_at = mlp_all[:, 2 * units :].reshape(1, width, width), 0
        w_ff = mlp_all[:, : 2 * units].reshape(n, 2, units, width).transpose(1, 0, 2, 3)
        w_ff = w_ff.reshape(2, ff // 768, 768, width).transpose(1, 0, 2, 3).reshape(ff // 768, 2 * 768, width)

    maxlen = rows // seqs
    live = (lax.iota(jnp.int32, maxlen)[None, :] < lengths[:, None]).reshape(rows, 1)
    grad_low = jnp.where(live, cot, 0.0).astype(BF16)
    if plan.direct:
        flat = jnp.pad(vec_piece.reshape(1, -1), ((0, 7), (0, width - 4 * per)))
        gathered = plan.gather(jnp.concatenate([qkv_piece, flat], axis=0))
        gathered, grad_low = lax.optimization_barrier((gathered, grad_low))
        slots = jnp.array(plan.slot_masks() + [m ^ 1 for m in plan.slot_masks()], jnp.int32)
        column = jnp.arange(width, dtype=jnp.int32)
        place = ((slots ^ me)[:, None] == (column // per)[None]).astype(F32)
        lane = jnp.arange(128, dtype=jnp.int32)
        spread = jnp.stack([(lane[:, None] == v * per + (column % per)[None]).astype(BF16) for v in range(4)])
        mixed, n1, w_abs, vecs = qkv_project(plan, me_arr, tokens, gathered, spread, place, ppr * n)
    else:
        w_abs = lax.all_gather(qkv_piece, AXES, axis=0, tiled=True)
        vecs = lax.all_gather(vec_piece, AXES, axis=1, tiled=True).astype(F32)
        vecs = jnp.pad(vecs, ((0, 4), (0, 0)))
        mixed, n1 = qkv_plain(tokens, w_abs, vecs)

    att, attT, inv, kept = attend_forward(mixed, lengths)
    residual, n2, wo = project_out(att, tokens, wo_pieces, wo_at, vecs)
    output, gn2, *gw_ff = feed_forward(me_arr, n2, residual, grad_low, w_ff, ff_units, plan.direct)
    if plan.direct:
        got = plan.swap(gw_ff[1], 1)
    else:
        gw_ff = gw_ff[0].reshape(ff // 768, 2, 768, width).transpose(1, 0, 2, 3)
        gw_ff = gw_ff.reshape(2, n, units, width).transpose(1, 0, 2, 3).reshape(-1, width)
        g_ff = lax.psum_scatter(gw_ff, AXES, scatter_dimension=0, tiled=True)
    gres, ga, gwo, gvec2 = middle_back(lengths, gn2, residual, cot, att, wo, vecs)
    pairs = width // PAIR
    late = pairs // 6
    if plan.direct:
        ga, got, keep = lax.optimization_barrier((ga, got, gw_ff[0]))
        away = plan.first_away(keep, got)
        back = (plan.swap(away[0], 2), plan.swap(away[1], 4))
        ga, away = lax.optimization_barrier((ga, away))
    grads, sums = attend_backward(mixed, ga, attT, inv, kept, seqs, 0, pairs - late)
    if plan.direct:
        back, grads, ga, sums = lax.optimization_barrier((back, grads, ga, sums))
        away = plan.second_away(keep, got, back)
        again = (plan.swap(away[0], 4), plan.swap(away[1], 2))
        ga, away = lax.optimization_barrier((ga, away))
    more, late_sums = attend_backward(mixed, ga, attT, inv, kept, seqs, pairs - late, late)
    grads, sums = [grads, more], [sums, late_sums]
    if plan.direct:
        q_keep, q_send = qkv_grad(plan, me_arr, grads, sums, n1, w_abs, gwo, vecs, gvec2, spread)
        again, q_keep, q_send = lax.optimization_barrier((again, q_keep, q_send))
        whole, q_keep = lax.optimization_barrier((plan.last_sum(keep, got, back, again), q_keep))
        g_ff = plan.along_sum(whole)
        summed = plan.scatter_first(q_keep, q_send, 48)
        gres, summed = lax.optimization_barrier((gres, summed))
        g_attn, g_ff = plan.scatter_rest(*summed, g_ff)
        g_attn = g_attn.astype(F32)
        g_qkv, g_out = g_attn[:ppr], g_attn[ppr : ppr + per]
        g_vec = g_attn[ppr + per, : 4 * per].reshape(4, per)
    else:
        g_qkv = lax.psum_scatter(qkv_grad_plain(grads, n1), AXES, scatter_dimension=0, tiled=True)
        g_out = lax.psum_scatter(gwo, AXES, scatter_dimension=0, tiled=True)
    gtok, gvec1 = first_back(grads, w_abs, tokens, gres, vecs)
    if not plan.direct:
        gvec = jnp.concatenate([gvec1[:2], gvec2[:2]], axis=0)
        g_vec = lax.psum_scatter(gvec, AXES, scatter_dimension=1, tiled=True)
    g_ff = g_ff.astype(F32)
    return (
        output, gtok, g_vec[0], g_vec[1], g_qkv.astype(F32).T, g_out.astype(F32), g_vec[2], g_vec[3],
        g_ff[:units].T, g_ff[units:],
    )


def solution(mesh):
    both = AXES
    rows2, vec, cols2 = P(both, None), P(both), P(None, both)
    in_specs = (rows2, vec, vec, vec, cols2, rows2, vec, vec, cols2, rows2, rows2)
    out_specs = (rows2, rows2, vec, vec, cols2, rows2, vec, vec, cols2, rows2)
    return jax.shard_map(
        functools.partial(body, Plan(mesh)), mesh=mesh, in_specs=in_specs, out_specs=out_specs, check_vma=False
    )
```

```python
import functools
import math

import jax
import jax.numpy as jnp
from jax import lax
from jax.experimental import pallas as pl
from jax.experimental.pallas import tpu as pltpu
from jax.sharding import PartitionSpec as P

F32 = jnp.float32
BF16 = jnp.bfloat16
HEAD = 64
PAIR = 2 * HEAD
EPSILON = 1e-05
NEGATIVE = -1e30
TILE = 256
CHUNK = 32
AXES = ("dp", "fsdp")
VMEM_LIMIT = 56 << 20
GELU_A = math.sqrt(2.0 / math.pi)
GELU_B = GELU_A * 0.044715


def mm_nn(left, right):
    return jnp.dot(left, right, preferred_element_type=F32)


def mm_nt(left, right):
    return lax.dot_general(left, right, (((1,), (1,)), ((), ())), preferred_element_type=F32)


def mm_tn(left, right):
    return lax.dot_general(left, right, (((0,), (0,)), ((), ())), preferred_element_type=F32)


def norm_stats(values):
    average = jnp.mean(values, axis=-1, keepdims=True)
    centred = values - average
    variance = jnp.mean(centred * centred, axis=-1, keepdims=True)
    rinv = lax.rsqrt(variance + EPSILON)
    return centred * rinv, rinv


def params(**kw):
    return pltpu.CompilerParams(vmem_limit_bytes=VMEM_LIMIT, **kw)


def cost(flops, moved):
    return pl.CostEstimate(flops=int(flops), bytes_accessed=int(moved), transcendentals=0)


class Plan:
    def __init__(self, mesh):
        self.n = mesh.shape["dp"] * mesh.shape["fsdp"]
        self.bits = self.n.bit_length() - 1
        self.direct = self.n == 1 << self.bits and self.bits == 5 and mesh.shape["fsdp"] == 4
        self.along = (3, 4)
        self.across = (1, 2)

    @staticmethod
    def masks_of(bits):
        found = [0]
        for bit in bits:
            found = found + [m | 1 << bit for m in found]
        return found

    def slot_masks(self):
        return [m ^ k for m in self.masks_of(self.across) for k in self.masks_of(self.along)]

    def swap(self, value, mask):
        return lax.ppermute(value, AXES, [(i, i ^ mask) for i in range(self.n)])

    def spread_stage(self, held, bits):
        return jnp.concatenate([held] + [self.swap(held, m) for m in self.masks_of(bits)[1:]], axis=0)

    def gather(self, piece):
        held = self.spread_stage(self.spread_stage(piece[None], self.along), self.across)
        return held, self.swap(held, 1)

    def scatter_first(self, keep, send, cut):
        got = self.swap(send, 1)
        grid = (2, 2, -1) + keep.shape[1:]
        keep, got = keep.reshape(grid), got.reshape(grid)
        pair = lambda at: add_low(keep[at], [got[at]])
        every, head, tail = slice(None), slice(None, cut), slice(cut, None)
        one = [pair((every, y, every, head)) for y in range(2)]
        two = [pair((x, every, every, tail)) for x in range(2)]
        return one, two

    def scatter_rest(self, one, two, done, beside, late):
        inner = self.masks_of(self.along)
        arriving = self.swap(one[1], 2), self.swap(two[1], 4)
        stay = [add_low(own[0][0], [got[0]]) for own, got in ((one, arriving[0]), (two, arriving[1]))]
        goes = [add_low(own[0][1], [got[1]]) for own, got in ((one, arriving[0]), (two, arriving[1]))]
        goes, done = lax.optimization_barrier((goes, done))
        got = self.swap(goes[0], 4), self.swap(goes[1], 2)
        held = jnp.concatenate([add_low(stay[0], [got[0]]), add_low(stay[1], [got[1]])], axis=1)
        held, late = lax.optimization_barrier((held, late))
        arriving = [self.swap(held[z], m) for z, m in list(enumerate(inner))[1:]]
        arriving[0], beside = lax.optimization_barrier((arriving[0], beside))
        return add_low(held[0], arriving), done, beside, late

    def view(self, held):
        pieces, rows, width = held.shape
        return held.reshape(pieces // 4, 2, 2, 2, rows // 2, width)

    def first_away(self, keep, got):
        k, g = self.view(keep), self.view(got)
        return add_low(k[:, :, 1, 0], [g[:, :, 1, 0]]), add_low(k[:, 1, :, 1], [g[:, 1, :, 1]])

    def second_away(self, keep, got, back):
        k, g = self.view(keep), self.view(got)
        return (
            add_low(k[:, 1, 0, 0], [g[:, 1, 0, 0], back[0][:, 1]]),
            add_low(k[:, 0, 1, 1], [g[:, 0, 1, 1], back[1][:, 1]]),
        )

    def last_sum(self, keep, got, back, again):
        k, g = self.view(keep), self.view(got)
        both = [
            add_low(k[:, 0, 0, half], [g[:, 0, 0, half], back[half][:, 0], again[half]]) for half in range(2)
        ]
        whole = jnp.concatenate(both, axis=1)
        return whole.reshape(-1, whole.shape[-1])

    def along_sum(self, whole):
        line = [[r + 8 * z for z in range(self.n // 8)] for r in range(8)]
        return lax.psum_scatter(whole, AXES, scatter_dimension=0, tiled=True, axis_index_groups=line)


def add_low(first, others):
    total = first.astype(F32)
    for other in others:
        total = total + other.astype(F32)
    return total.astype(first.dtype)


def slot_of(masks, me, piece_pair):
    wanted = piece_pair ^ lax.div(me, 2)
    slot = jnp.int32(0)
    for s, m in enumerate(masks):
        slot = jnp.where(wanted == m // 2, s, slot)
    return slot


def qkv_kernel(masks, ppr, me_ref, x_ref, own_ref, sib_ref, e_ref, m_ref, mixed_ref, n1_ref, w_ref, vec_ref):
    me = me_ref[0]

    @pl.when(pl.program_id(0) == 0)
    def _():
        core = lax.rem(me, 2)
        for s, m in enumerate(masks):
            pair = lax.div(me, 2) ^ (m // 2)
            at = pl.ds(pl.multiple_of(pair * (2 * ppr), 16), 2 * ppr)
            both = [own_ref[s, :ppr, :], sib_ref[s, :ppr, :]]
            for side in range(2):

                @pl.when(core == side)
                def _():
                    w_ref[at, :] = jnp.concatenate([both[side], both[1 - side]], axis=0)

        packed = jnp.concatenate([own_ref[:, ppr, :128], sib_ref[:, ppr, :128]], axis=0)
        for v in range(4):
            vec_ref[v : v + 1, :] = jnp.sum(mm_nn(packed, e_ref[v]) * m_ref[...], axis=0, keepdims=True)

    xhat, rinv = norm_stats(x_ref[...].astype(F32))
    n1 = (xhat * vec_ref[0:1, :] + vec_ref[1:2, :]).astype(BF16)
    n1_ref[...] = n1
    mixed_ref[...] = mm_nt(n1, w_ref[...]).astype(BF16)


def qkv_project(plan, me, tokens, gathered, spread, place, out_cols, rows_block=256):
    rows, width = tokens.shape
    masks = plan.slot_masks()
    full = lambda a: pl.BlockSpec(a.shape, lambda r, *_: (0,) * a.ndim)
    whole = lambda shape: pl.BlockSpec(shape, lambda r, *_: (0,) * len(shape))
    return pl.pallas_call(
        functools.partial(qkv_kernel, masks, out_cols // plan.n),
        grid_spec=pltpu.PrefetchScalarGridSpec(
            num_scalar_prefetch=1,
            grid=(rows // rows_block,),
            in_specs=[
                pl.BlockSpec((rows_block, width), lambda r, *_: (r, 0)),
            ]
            + [full(a) for a in (*gathered, spread, place)],
            out_specs=[
                pl.BlockSpec((rows_block, out_cols), lambda r, *_: (r, 0)),
                pl.BlockSpec((rows_block, width), lambda r, *_: (r, 0)),
                whole((out_cols, width)), whole((8, width)),
            ],
        ),
        out_shape=[
            jax.ShapeDtypeStruct((rows, out_cols), BF16),
            jax.ShapeDtypeStruct((rows, width), BF16),
            jax.ShapeDtypeStruct((out_cols, width), BF16),
            jax.ShapeDtypeStruct((8, width), F32),
        ],
        compiler_params=params(),
        cost_estimate=cost(2 * rows * width * out_cols, 20e6),
        name="qkv_project",
    )(me, tokens, *gathered, spread, place)


def qkv_plain_kernel(x_ref, w_ref, vec_ref, mixed_ref, n1_ref):
    xhat, rinv = norm_stats(x_ref[...].astype(F32))
    n1 = (xhat * vec_ref[0:1, :] + vec_ref[1:2, :]).astype(BF16)
    n1_ref[...] = n1
    mixed_ref[...] = mm_nt(n1, w_ref[...]).astype(BF16)


def qkv_plain(tokens, w_abs, vecs, rows_block=256):
    rows, width = tokens.shape
    out_cols = w_abs.shape[0]
    full = lambda a: pl.BlockSpec(a.shape, lambda r: (0,) * a.ndim)
    return pl.pallas_call(
        qkv_plain_kernel,
        grid=(rows // rows_block,),
        in_specs=[pl.BlockSpec((rows_block, width), lambda r: (r, 0)), full(w_abs), full(vecs)],
        out_specs=[
            pl.BlockSpec((rows_block, out_cols), lambda r: (r, 0)),
            pl.BlockSpec((rows_block, width), lambda r: (r, 0)),
        ],
        out_shape=[
            jax.ShapeDtypeStruct((rows, out_cols), BF16),
            jax.ShapeDtypeStruct((rows, width), BF16),
        ],
        compiler_params=params(),
        name="qkv_plain",
    )(tokens, w_abs, vecs)


def tile_at(i, j):
    return i * (i + 1) // 2 + j

def attend_kernel(maxlen, len_ref, q_ref, k_ref, v_ref, att_ref, attT_ref, inv_ref, keep_ref):
    length = len_ref[pl.program_id(0)]
    q, k = q_ref[...], k_ref[...]
    qT = (q.astype(F32) * HEAD**-0.5).T.astype(BF16)
    vT = v_ref[...].astype(F32).T.astype(BF16)
    same = lax.broadcasted_iota(jnp.int32, (PAIR, PAIR), 0) // HEAD == lax.broadcasted_iota(jnp.int32, (PAIR, PAIR), 1) // HEAD
    same = jnp.where(same, 1.0, 0.0).astype(BF16)
    square = lambda a: jnp.max(mm_nn((a.astype(F32) * a.astype(F32)).astype(BF16), same))
    small = square(q) * square(k) * (1.03 / HEAD) < 70.0**2

    def block(i, plain):
        lo, hi = i * TILE, (i + 1) * TILE
        qpos = lo + lax.broadcasted_iota(jnp.int32, (1, TILE), 1)
        limit = jnp.minimum(qpos, length - 1)
        blank = jnp.zeros((HEAD, TILE), BF16)
        outs = []
        for h in range(2):
            own = qT[h * HEAD : (h + 1) * HEAD, lo:hi]
            own = jnp.concatenate([own, blank] if h == 0 else [blank, own], axis=0)

            def piece(at):
                s = mm_nn(k[at : at + CHUNK], own)
                t = s * s + 1.0
                r = lax.rsqrt(t)
                kpos = at + lax.broadcasted_iota(jnp.int32, (CHUNK, TILE), 0)
                return s, r, t * r, (kpos <= limit if at >= lo else kpos < length)

            top = None
            if not plain:
                for at in range(0, hi, CHUNK):
                    s, r, smooth, allowed = piece(at)
                    here = jnp.max(jnp.where(allowed, smooth, NEGATIVE), axis=0, keepdims=True)
                    top = here if top is None else jnp.maximum(top, here)
            total, weights = None, []
            for at in range(0, hi, CHUNK):
                s, r, smooth, allowed = piece(at)
                e = jnp.exp(smooth) if plain else jnp.exp(jnp.minimum(smooth - top, 0.0))
                e = jnp.where(allowed, e, 0.0)
                part = e.reshape(CHUNK // 8, 8, TILE).sum(axis=0)
                total = part if total is None else total + part
                g = jnp.tanh(s)
                w = g * e
                c = e * (s * r)
                a = e + g * (c - w)
                w = w.astype(BF16)
                weights.append(w)
                tile, row = tile_at(i, at // TILE), at % TILE
                keep_ref[0, h, 0, tile, row : row + CHUNK, :] = w
                keep_ref[0, h, 1, tile, row : row + CHUNK, :] = a.astype(BF16)
                keep_ref[0, h, 2, tile, row : row + CHUNK, :] = c.astype(BF16)
            inv = 1.0 / jnp.sum(total, axis=0, keepdims=True)
            inv_ref[0, h : h + 1, lo:hi] = inv
            outs.append(mm_nn(vT[h * HEAD : (h + 1) * HEAD, :hi], jnp.concatenate(weights, axis=0)) * inv)
        outT = jnp.concatenate(outs, axis=0)
        attT_ref[:, lo:hi] = outT.astype(BF16)
        att_ref[lo:hi, :] = outT.T.astype(BF16)

    @pl.when(small)
    def _():
        for i in range(maxlen // TILE):
            block(i, True)

    @pl.when(jnp.logical_not(small))
    def _():
        for i in range(maxlen // TILE):
            block(i, False)


def attend_forward(mixed, lengths):
    rows, width = mixed.shape[0], mixed.shape[1] // 3
    seqs = lengths.shape[0]
    maxlen, pairs = rows // seqs, width // PAIR
    tiles = tile_at(maxlen // TILE, 0)
    col = lambda part: pl.BlockSpec((maxlen, PAIR), lambda s, p, *_: (s, part * pairs + p))
    return pl.pallas_call(
        functools.partial(attend_kernel, maxlen),
        grid_spec=pltpu.PrefetchScalarGridSpec(
            num_scalar_prefetch=1,
            grid=(seqs, pairs),
            in_specs=[col(0), col(1), col(2)],
            out_specs=[
                col(0),
                pl.BlockSpec((PAIR, maxlen), lambda s, p, *_: (p, s)),
                pl.BlockSpec((1, 8, maxlen), lambda s, p, *_: (s * pairs + p, 0, 0)),
                pl.BlockSpec((1, 2, 3, tiles, TILE, TILE), lambda s, p, *_: (s * pairs + p, 0, 0, 0, 0, 0)),
            ],
        ),
        out_shape=[
            jax.ShapeDtypeStruct((rows, width), BF16),
            jax.ShapeDtypeStruct((width, rows), BF16),
            jax.ShapeDtypeStruct((seqs * pairs, 8, maxlen), F32),
            jax.ShapeDtypeStruct((seqs * pairs, 2, 3, tiles, TILE, TILE), BF16),
        ],
        compiler_params=params(),
        cost_estimate=cost(20e9, 60e6),
        name="attend_forward",
    )(lengths, mixed, mixed, mixed)


def attend_back_kernel(maxlen, q_ref, k_ref, v_ref, ga_ref, attT_ref, inv_ref, keep_ref, d_ref, sum_ref, dqT):
    qs = q_ref[...] * jnp.asarray(HEAD**-0.5, BF16)
    v = v_ref[...]
    kT = k_ref[...].astype(F32).T.astype(BF16)
    gaT = ga_ref[...].astype(F32).T
    prod = gaT * attT_ref[...].astype(F32)
    half = lambda h: slice(h * HEAD, (h + 1) * HEAD)
    inv = [inv_ref[0, h : h + 1, :] for h in range(2)]
    gaT = jnp.concatenate([gaT[half(h)] * inv[h] for h in range(2)], axis=0)
    ga = gaT.T.astype(BF16)
    gaT = gaT.astype(BF16)
    lane = lax.broadcasted_iota(jnp.int32, (maxlen, PAIR), 1)
    blank = jnp.zeros((HEAD, maxlen), BF16)
    nil = jnp.zeros((), BF16)
    heads = []
    for h in range(2):
        mine = (lane < HEAD) if h == 0 else (lane >= HEAD)
        own = gaT[half(h)]
        heads.append(
            (
                jnp.where(mine, ga, nil), jnp.where(mine, qs, nil),
                jnp.concatenate([own, blank] if h == 0 else [blank, own], axis=0), kT[half(h)],
                jnp.sum(prod[half(h)], axis=0, keepdims=True) * inv[h],
            )
        )
    blocks = maxlen // TILE
    for j in range(blocks):
        lo, hi = j * TILE, (j + 1) * TILE
        dv = dk = None
        for h in range(2):
            ga_h, q_h, gaT_h, kT_h, delta = heads[h]
            side = lambda part: jnp.concatenate([keep_ref[0, h, part, tile_at(i, j)] for i in range(j, blocks)], axis=1)
            gw = mm_nn(v[lo:hi], gaT_h[:, lo:])
            ds = (gw * side(1).astype(F32) - side(2).astype(F32) * delta[:, lo:]).astype(BF16)
            dv_h = mm_nn(side(0), ga_h[lo:])
            dk_h = mm_nn(ds, q_h[lo:])
            dv = dv_h if dv is None else dv + dv_h
            dk = dk_h if dk is None else dk + dk_h
            dq_h = mm_nn(kT_h[:, lo:hi], ds)
            if j == 0:
                dqT[half(h), :] = dq_h
            else:
                dqT[half(h), lo:] += dq_h
        d_ref[2, lo:hi, :] = dv.astype(BF16)
        d_ref[1, lo:hi, :] = dk.astype(BF16)
        sums = [jnp.sum(d, axis=0, keepdims=True) for d in (dk, dv)]
        total = sums if j == 0 else [t + d for t, d in zip(total, sums)]
    dq = (dqT[...] * HEAD**-0.5).T
    d_ref[0] = dq.astype(BF16)
    total = [jnp.sum(dq, axis=0, keepdims=True)] + total
    sum_ref[0] = jnp.concatenate(total + [jnp.zeros((5, PAIR), F32)], axis=0)


def attend_backward(mixed, ga, attT, inv, keep, seqs, first, count):
    rows, width = mixed.shape[0], mixed.shape[1] // 3
    maxlen, pairs = rows // seqs, width // PAIR
    col = lambda part: pl.BlockSpec((maxlen, PAIR), lambda s, p: (s, part * pairs + p + first))
    return pl.pallas_call(
        functools.partial(attend_back_kernel, maxlen),
        grid=(seqs, count),
        in_specs=[
            col(0), col(1), col(2), col(0),
            pl.BlockSpec((PAIR, maxlen), lambda s, p: (p + first, s)),
            pl.BlockSpec((1, 8, maxlen), lambda s, p: (s * pairs + p + first, 0, 0)),
            pl.BlockSpec((1,) + keep.shape[1:], lambda s, p: (s * pairs + p + first, 0, 0, 0, 0, 0)),
        ],
        out_specs=[
            pl.BlockSpec((3, maxlen, PAIR), lambda s, p: (0, s, p)),
            pl.BlockSpec((1, 8, PAIR), lambda s, p: (s, 0, p)),
        ],
        out_shape=[
            jax.ShapeDtypeStruct((3, rows, count * PAIR), BF16),
            jax.ShapeDtypeStruct((seqs, 8, count * PAIR), F32),
        ],
        scratch_shapes=[pltpu.VMEM((PAIR, maxlen), F32)],
        compiler_params=params(),
        cost_estimate=cost(5e9 * count, 10e6 * count),
        name="attend_backward",
    )(mixed, mixed, mixed, ga, attT, inv, keep)


def project_kernel(att_ref, x_ref, wp_ref, vec_ref, res_ref, n2_ref, wo_ref):
    pieces, per, _ = wp_ref.shape

    @pl.when(pl.program_id(0) == 0)
    def _():
        for p in range(pieces):
            wo_ref[p * per : (p + 1) * per, :] = wp_ref[p]

    residual = x_ref[...].astype(F32) + mm_nn(att_ref[...], wo_ref[...])
    res_ref[...] = residual
    xhat, rinv = norm_stats(residual)
    n2_ref[...] = (xhat * vec_ref[2:3, :] + vec_ref[3:4, :]).astype(BF16)


def project_out(att, tokens, wo_pieces, at, vecs, rows_block=512):
    rows, width = tokens.shape
    pieces = wo_pieces.shape[0]
    block = pl.BlockSpec((rows_block, width), lambda r: (r, 0))
    full = lambda a: pl.BlockSpec(a.shape, lambda r: (0,) * a.ndim)
    return pl.pallas_call(
        project_kernel,
        grid=(rows // rows_block,),
        in_specs=[
            block, block, pl.BlockSpec((pieces, width // pieces, width), lambda r: (0, at, 0)), full(vecs),
        ],
        out_specs=[block, block, pl.BlockSpec((width, width), lambda r: (0, 0))],
        out_shape=[
            jax.ShapeDtypeStruct((rows, width), F32),
            jax.ShapeDtypeStruct((rows, width), BF16),
            jax.ShapeDtypeStruct((width, width), BF16),
        ],
        compiler_params=params(),
        cost_estimate=cost(2 * rows * width * width, 10e6),
        name="project_out",
    )(att, tokens, wo_pieces, vecs)


def live_grad(cot, lengths_ref, maxlen, first_row):
    rows = cot.shape[0]
    at = first_row + lax.broadcasted_iota(jnp.int32, (rows, 1), 0)
    seq = first_row // maxlen
    return jnp.where(at - seq * maxlen < lengths_ref[seq], cot, 0.0)


def mlp_kernel(units, me_ref, n2_ref, gl_ref, w_ref, act_ref, gn_ref, *gw_refs):
    step = pl.program_id(0)
    rows, width = n2_ref.shape

    pieces = w_ref.shape[0]
    wu = w_ref[:, :units, :].reshape(pieces * units, width)
    wd = w_ref[:, units : 2 * units, :].reshape(pieces * units, width)
    n2, gl = n2_ref[...], gl_ref[...]
    u = mm_nt(n2, wu)
    uu = u * u
    th = jnp.tanh(u * (GELU_A + GELU_B * uu))
    half = 0.5 * u
    act = (half + half * th).astype(BF16)
    slope = 0.5 + 0.5 * th + (half - half * (th * th)) * (GELU_A + (3.0 * GELU_B) * uu)
    act_ref[...] = act
    gp = (mm_nt(gl, wd) * slope).astype(BF16)
    gn = mm_nn(gp, wu)

    @pl.when(step == 0)
    def _():
        gn_ref[...] = gn

    @pl.when(step > 0)
    def _():
        gn_ref[...] += gn

    for at, grad in ((0, mm_tn(gp, n2)), (units, mm_tn(act, gl))):
        grad = grad.astype(BF16)
        if len(gw_refs) == 1:
            gw_refs[0][:, at : at + units, :] = grad.reshape(pieces, units, width)
            continue
        grad = grad.reshape(pieces // 2, 2, units, width)
        core = lax.rem(me_ref[0], 2)
        near = lax.rem(lax.div(me_ref[0], 2), 4)
        for side in range(2):

            @pl.when(core == side)
            def _():
                for place in range(pieces // 2):
                    slot = (place // 4) * 4 + ((place % 4) ^ near)
                    gw_refs[0][slot, at : at + units, :] = grad[place, side]
                    gw_refs[1][slot, at : at + units, :] = grad[place, 1 - side]


def feed_forward(me, n2, gl, w, units, split):
    rows, width = n2.shape
    pieces, held, _ = w.shape
    take = max(1, 768 // units)
    full = lambda: pl.BlockSpec((rows, width), lambda f, *_: (0, 0))
    outs = 2 if split else 1
    grads = [pl.BlockSpec((take // outs, 2 * units, width), lambda f, *_: (f, 0, 0))] * outs
    return pl.pallas_call(
        functools.partial(mlp_kernel, units),
        grid_spec=pltpu.PrefetchScalarGridSpec(
            num_scalar_prefetch=1,
            grid=(pieces // take,),
            in_specs=[
                full(), full(), pl.BlockSpec((take, held, width), lambda f, *_: (f, 0, 0)),
            ],
            out_specs=[pl.BlockSpec((rows, take * units), lambda f, *_: (0, f)), full()] + grads,
        ),
        out_shape=[jax.ShapeDtypeStruct((rows, pieces * units), BF16), jax.ShapeDtypeStruct((rows, width), F32)]
        + [jax.ShapeDtypeStruct((pieces // outs, 2 * units, width), BF16)] * outs,
        compiler_params=params(),
        cost_estimate=cost(10 * rows * width * pieces * units, 40e6),
        name="feed_forward",
    )(me, n2, gl, w)


def finish_kernel(units, act_ref, w_ref, res_ref, out_ref, acc_s):
    step = pl.program_id(0)
    pieces, _, width = w_ref.shape
    part = mm_nn(act_ref[...], w_ref[:, units : 2 * units, :].reshape(pieces * units, width))

    @pl.when(step == 0)
    def _():
        acc_s[...] = part + res_ref[...]

    @pl.when(step > 0)
    def _():
        acc_s[...] += part

    @pl.when(step == pl.num_programs(0) - 1)
    def _():
        out_ref[...] = acc_s[...].astype(BF16)


def finish_output(act, w, residual, units):
    rows, width = residual.shape
    pieces, held, _ = w.shape
    take = max(1, 768 // units)
    full = lambda: pl.BlockSpec((rows, width), lambda f: (0, 0))
    return pl.pallas_call(
        functools.partial(finish_kernel, units),
        grid=(pieces // take,),
        in_specs=[
            pl.BlockSpec((rows, take * units), lambda f: (0, f)),
            pl.BlockSpec((take, held, width), lambda f: (f, 0, 0)), full(),
        ],
        out_specs=full(),
        out_shape=jax.ShapeDtypeStruct((rows, width), BF16),
        scratch_shapes=[pltpu.VMEM((rows, width), F32)],
        compiler_params=params(),
        cost_estimate=cost(2 * rows * width * pieces * units, 20e6),
        name="finish_output",
    )(act, w, residual)


def norm_back(grad, xhat, rinv, gain):
    dh = grad * gain
    first = jnp.mean(dh, axis=-1, keepdims=True)
    second = jnp.mean(dh * xhat, axis=-1, keepdims=True)
    return rinv * (dh - first - xhat * second)


def middle_kernel(maxlen, len_ref, gn_ref, res_ref, cot_ref, att_ref, wo_ref, vec_ref, gres_ref, ga_ref, gwo_ref, gvec_ref, low_s):
    step = pl.program_id(0)
    rows = gn_ref.shape[0]
    gn = gn_ref[...]
    xhat, rinv = norm_stats(res_ref[...])
    gres = live_grad(cot_ref[...], len_ref, maxlen, step * rows) + norm_back(gn, xhat, rinv, vec_ref[2:3, :])
    gres_ref[...] = gres
    low = gres.astype(BF16)
    low_s[pl.ds(pl.multiple_of(step * rows, rows), rows), :] = low
    ga_ref[...] = mm_nt(low, wo_ref[...]).astype(BF16)

    @pl.when(step == 0)
    def _():
        gvec_ref[...] = jnp.zeros_like(gvec_ref)

    gvec_ref[0:1, :] += jnp.sum(gn * xhat, axis=0, keepdims=True)
    gvec_ref[1:2, :] += jnp.sum(gn, axis=0, keepdims=True)

    @pl.when(step == pl.num_programs(0) - 1)
    def _():
        gwo_ref[...] = mm_tn(att_ref[...], low_s[...]).astype(BF16)


def middle_back(lengths, gn, residual, cot, att, wo, vecs):
    rows, width = gn.shape
    rows_block = rows // lengths.shape[0]
    block = pl.BlockSpec((rows_block, width), lambda r, *_: (r, 0))
    full = lambda shape: pl.BlockSpec(shape, lambda r, *_: (0,) * len(shape))
    return pl.pallas_call(
        functools.partial(middle_kernel, rows // lengths.shape[0]),
        grid_spec=pltpu.PrefetchScalarGridSpec(
            num_scalar_prefetch=1,
            grid=(rows // rows_block,),
            in_specs=[block, block, block, full(att.shape), full(wo.shape), full(vecs.shape)],
            out_specs=[block, block, full(wo.shape), full((8, width))],
            scratch_shapes=[pltpu.VMEM((rows, width), BF16)],
        ),
        out_shape=[
            jax.ShapeDtypeStruct((rows, width), F32),
            jax.ShapeDtypeStruct((rows, width), BF16),
            jax.ShapeDtypeStruct(wo.shape, BF16),
            jax.ShapeDtypeStruct((8, width), F32),
        ],
        compiler_params=params(),
        cost_estimate=cost(4 * rows * width * width, 30e6),
        name="middle_back",
    )(lengths, gn, residual, cot, att, wo, vecs)


def qkv_grad_kernel(masks, ppr, opr, me_ref, *refs):
    d1_ref, d2_ref, sum1_ref, sum2_ref, n1_ref, w_ref, gwo_ref, vec_ref, gvec2_ref, e_ref, keep_ref, send_ref, low_s, acc_s = refs
    rows, width = n1_ref.shape
    part = pl.program_id(0)
    n1 = n1_ref[...]
    paired, gshift, at = jnp.zeros((1, width), F32), jnp.zeros((8, width), F32), 0
    for d_ref, sum_ref in ((d1_ref, sum1_ref), (d2_ref, sum2_ref)):
        cols = d_ref.shape[2]
        gw = mm_tn(d_ref[0], n1)
        low_s[pl.ds(pl.multiple_of(part * width + at, PAIR), cols), :] = gw.astype(BF16)
        w = w_ref[at : at + cols, :]
        paired += jnp.sum(gw * w.astype(F32), axis=0, keepdims=True)
        total = jnp.sum(sum_ref[...], axis=0)
        pick = lax.broadcasted_iota(jnp.int32, (8, 1), 0) == part
        total = jnp.sum(jnp.where(pick, total, 0.0), axis=0, keepdims=True)
        high = total.astype(BF16).astype(F32)
        low = jnp.concatenate([high, total - high, jnp.zeros((6, cols), F32)], axis=0)
        gshift += mm_nn(low.astype(BF16), w)
        at += cols

    @pl.when(part == 0)
    def _():
        acc_s[...] = jnp.zeros_like(acc_s)

    acc_s[0:1, :] += paired
    acc_s[1:2, :] += gshift[0:1, :] + gshift[1:2, :]

    @pl.when(part == 2)
    def _():
        qkv_grad_pieces(masks, ppr, opr, me_ref, acc_s, gwo_ref, vec_ref, gvec2_ref, e_ref, keep_ref, send_ref, low_s)


def qkv_grad_pieces(masks, ppr, opr, me_ref, acc_s, gwo_ref, vec_ref, gvec2_ref, e_ref, keep_ref, send_ref, low_s):
    width = acc_s.shape[1]
    paired, gshift = acc_s[0:1, :], acc_s[1:2, :]
    ggain = (paired - vec_ref[1:2, :] * gshift) / vec_ref[0:1, :]
    n = 2 * len(masks)
    owner = lax.broadcasted_iota(jnp.int32, (n, width), 1) // opr == lax.broadcasted_iota(jnp.int32, (n, width), 0)
    packed = jnp.zeros((n, 128), F32)
    for v, row in enumerate((ggain, gshift, gvec2_ref[0:1, :], gvec2_ref[1:2, :])):
        packed += mm_nt(jnp.where(owner, row, 0.0).astype(BF16), e_ref[v])
    me = me_ref[0]
    core = lax.rem(me, 2)
    for pair in range(len(masks)):
        slot = slot_of(masks, me, pair)
        sides = []
        for j in (2 * pair, 2 * pair + 1):
            extra = jnp.concatenate([packed[j : j + 1, :], jnp.zeros((1, width - 128), F32)], axis=1)
            extra = jnp.concatenate([extra, jnp.zeros((7, width), F32)], axis=0)
            sides.append((low_s[j * ppr : (j + 1) * ppr, :], gwo_ref[j * opr : (j + 1) * opr, :], extra.astype(BF16)))
        for side in range(2):

            @pl.when(core == side)
            def _():
                for out, part in ((keep_ref, sides[side]), (send_ref, sides[1 - side])):
                    out[slot] = jnp.concatenate(part, axis=0)


def qkv_grad(plan, me, grads, sums, n1, w_abs, gwo, vecs, gvec2, spread):
    rows, width = n1.shape
    masks = plan.slot_masks()
    ppr, opr = 3 * width // plan.n, width // plan.n
    full = lambda a: pl.BlockSpec(a.shape, lambda p, *_: (0,) * len(a.shape))
    shape = jax.ShapeDtypeStruct((len(masks), ppr + opr + 8, width), BF16)
    return pl.pallas_call(
        functools.partial(qkv_grad_kernel, masks, ppr, opr),
        grid_spec=pltpu.PrefetchScalarGridSpec(
            num_scalar_prefetch=1,
            grid=(3,),
            in_specs=[pl.BlockSpec((1, rows, d.shape[2]), lambda p, *_: (p, 0, 0)) for d in grads]
            + [full(a) for a in (*sums, n1)]
            + [pl.BlockSpec((width, width), lambda p, *_: (p, 0))]
            + [full(a) for a in (gwo, vecs, gvec2, spread)],
            out_specs=[full(shape), full(shape)],
            scratch_shapes=[pltpu.VMEM((3 * width, width), BF16), pltpu.VMEM((8, width), F32)],
        ),
        out_shape=[shape, shape],
        compiler_params=params(),
        cost_estimate=cost(6 * rows * width * width, 25e6),
        name="qkv_grad",
    )(me, *grads, *sums, n1, w_abs, gwo, vecs, gvec2, spread)


def qkv_grad_plain_kernel(d_ref, n1_ref, out_ref):
    out_ref[...] = mm_tn(d_ref[...], n1_ref[...]).astype(BF16)


def qkv_grad_plain(grads, n1):
    rows, width = n1.shape
    vm = pl.BlockSpec(memory_space=pltpu.VMEM)
    found = []
    for part in range(3):
        for d in grads:
            call = pl.pallas_call(
                qkv_grad_plain_kernel,
                in_specs=[vm, vm],
                out_specs=vm,
                out_shape=jax.ShapeDtypeStruct((d.shape[2], width), BF16),
                compiler_params=params(),
                name="qkv_grad_plain",
            )
            found.append(call(d[part], n1))
    return jnp.concatenate(found, axis=0)


def first_kernel(d1_ref, d2_ref, w_ref, x_ref, gres_ref, vec_ref, gtok_ref, gvec_ref):
    width = x_ref.shape[1]
    gn = jnp.zeros(x_ref.shape, F32)
    for part in range(3):
        at = part * width
        for ref in (d1_ref, d2_ref):
            gn += mm_nn(ref[part], w_ref[at : at + ref.shape[2], :])
            at += ref.shape[2]
    xhat, rinv = norm_stats(x_ref[...].astype(F32))
    gtok_ref[...] = gres_ref[...] + norm_back(gn, xhat, rinv, vec_ref[0:1, :])

    @pl.when(pl.program_id(0) == 0)
    def _():
        gvec_ref[...] = jnp.zeros_like(gvec_ref)

    gvec_ref[0:1, :] += jnp.sum(gn * xhat, axis=0, keepdims=True)
    gvec_ref[1:2, :] += jnp.sum(gn, axis=0, keepdims=True)


def first_back(grads, w_abs, tokens, gres, vecs, rows_block=256):
    rows, width = tokens.shape
    block = pl.BlockSpec((rows_block, width), lambda r: (r, 0))
    full = lambda shape: pl.BlockSpec(shape, lambda r: (0,) * len(shape))
    return pl.pallas_call(
        first_kernel,
        grid=(rows // rows_block,),
        in_specs=[pl.BlockSpec((3, rows_block, d.shape[2]), lambda r: (0, r, 0)) for d in grads]
        + [full(w_abs.shape), block, block, full(vecs.shape)],
        out_specs=[block, full((8, width))],
        out_shape=[jax.ShapeDtypeStruct((rows, width), F32), jax.ShapeDtypeStruct((8, width), F32)],
        compiler_params=params(),
        cost_estimate=cost(6 * rows * width * width, 25e6),
        name="first_back",
    )(*grads, w_abs, tokens, gres, vecs)


def body(plan, tokens, lengths, ln1_gain, ln1_shift, w_qkv, w_out, ln2_gain, ln2_shift, w_up, w_down, cot):
    rows, width = tokens.shape
    n = plan.n
    seqs = lengths.shape[0]
    me = lax.axis_index(AXES).astype(jnp.int32)
    me_arr = me[None]
    vec_piece = jnp.stack([ln1_gain, ln1_shift, ln2_gain, ln2_shift])
    per = vec_piece.shape[1]
    qkv_piece = w_qkv.T
    ppr, units = qkv_piece.shape[0], w_down.shape[0]
    ff = units * n

    mlp_piece = jnp.concatenate([w_up.T, w_down, w_out], axis=0)
    mlp_all = lax.all_gather(mlp_piece, AXES, axis=0, tiled=True).reshape(n, -1, width)
    if plan.direct:
        w_ff, ff_units, wo_pieces, wo_at = mlp_all, units, mlp_all, 2 * units // per
    else:
        ff_units = 768
        wo_pieces, wo_at = mlp_all[:, 2 * units :].reshape(1, width, width), 0
        w_ff = mlp_all[:, : 2 * units].reshape(n, 2, units, width).transpose(1, 0, 2, 3)
        w_ff = w_ff.reshape(2, ff // 768, 768, width).transpose(1, 0, 2, 3).reshape(ff // 768, 2 * 768, width)

    maxlen = rows // seqs
    live = (lax.iota(jnp.int32, maxlen)[None, :] < lengths[:, None]).reshape(rows, 1)
    grad_low = jnp.where(live, cot, 0.0).astype(BF16)
    if plan.direct:
        flat = jnp.pad(vec_piece.reshape(1, -1), ((0, 7), (0, width - 4 * per)))
        gathered = plan.gather(jnp.concatenate([qkv_piece, flat], axis=0))
        gathered, grad_low = lax.optimization_barrier((gathered, grad_low))
        slots = jnp.array(plan.slot_masks() + [m ^ 1 for m in plan.slot_masks()], jnp.int32)
        column = jnp.arange(width, dtype=jnp.int32)
        place = ((slots ^ me)[:, None] == (column // per)[None]).astype(F32)
        lane = jnp.arange(128, dtype=jnp.int32)
        spread = jnp.stack([(lane[:, None] == v * per + (column % per)[None]).astype(BF16) for v in range(4)])
        mixed, n1, w_abs, vecs = qkv_project(plan, me_arr, tokens, gathered, spread, place, ppr * n)
    else:
        w_abs = lax.all_gather(qkv_piece, AXES, axis=0, tiled=True)
        vecs = lax.all_gather(vec_piece, AXES, axis=1, tiled=True).astype(F32)
        vecs = jnp.pad(vecs, ((0, 4), (0, 0)))
        mixed, n1 = qkv_plain(tokens, w_abs, vecs)

    att, attT, inv, kept = attend_forward(mixed, lengths)
    residual, n2, wo = project_out(att, tokens, wo_pieces, wo_at, vecs)
    act, gn2, *gw_ff = feed_forward(me_arr, n2, grad_low, w_ff, ff_units, plan.direct)
    if plan.direct:
        got = plan.swap(gw_ff[1], 1)
    else:
        gw_ff = gw_ff[0].reshape(ff // 768, 2, 768, width).transpose(1, 0, 2, 3)
        gw_ff = gw_ff.reshape(2, n, units, width).transpose(1, 0, 2, 3).reshape(-1, width)
        g_ff = lax.psum_scatter(gw_ff, AXES, scatter_dimension=0, tiled=True)
    gres, ga, gwo, gvec2 = middle_back(lengths, gn2, residual, cot, att, wo, vecs)
    pairs = width // PAIR
    late = pairs // 6
    if plan.direct:
        ga, got, keep = lax.optimization_barrier((ga, got, gw_ff[0]))
        away = plan.first_away(keep, got)
        back = (plan.swap(away[0], 2), plan.swap(away[1], 4))
        ga, away = lax.optimization_barrier((ga, away))
    grads, sums = attend_backward(mixed, ga, attT, inv, kept, seqs, 0, pairs - late)
    if plan.direct:
        back, grads, ga, sums = lax.optimization_barrier((back, grads, ga, sums))
        away = plan.second_away(keep, got, back)
        again = (plan.swap(away[0], 4), plan.swap(away[1], 2))
        ga, away = lax.optimization_barrier((ga, away))
    more, late_sums = attend_backward(mixed, ga, attT, inv, kept, seqs, pairs - late, late)
    grads, sums = [grads, more], [sums, late_sums]
    if plan.direct:
        q_keep, q_send = qkv_grad(plan, me_arr, grads, sums, n1, w_abs, gwo, vecs, gvec2, spread)
        again, q_keep, q_send = lax.optimization_barrier((again, q_keep, q_send))
        whole, q_keep = lax.optimization_barrier((plan.last_sum(keep, got, back, again), q_keep))
        g_ff = plan.along_sum(whole)
        summed = plan.scatter_first(q_keep, q_send, 48)
        act, summed = lax.optimization_barrier((act, summed))
        output = finish_output(act, w_ff, residual, ff_units)
        g_attn, output, g_ff, gres = plan.scatter_rest(*summed, output, g_ff, gres)
        g_attn = g_attn.astype(F32)
        g_qkv, g_out = g_attn[:ppr], g_attn[ppr : ppr + per]
        g_vec = g_attn[ppr + per, : 4 * per].reshape(4, per)
    else:
        g_qkv = lax.psum_scatter(qkv_grad_plain(grads, n1), AXES, scatter_dimension=0, tiled=True)
        g_out = lax.psum_scatter(gwo, AXES, scatter_dimension=0, tiled=True)
    gtok, gvec1 = first_back(grads, w_abs, tokens, gres, vecs)
    if not plan.direct:
        output = finish_output(act, w_ff, residual, ff_units)
        gvec = jnp.concatenate([gvec1[:2], gvec2[:2]], axis=0)
        g_vec = lax.psum_scatter(gvec, AXES, scatter_dimension=1, tiled=True)
    g_ff = g_ff.astype(F32)
    return (
        output, gtok, g_vec[0], g_vec[1], g_qkv.astype(F32).T, g_out.astype(F32), g_vec[2], g_vec[3],
        g_ff[:units].T, g_ff[units:],
    )


def solution(mesh):
    both = AXES
    rows2, vec, cols2 = P(both, None), P(both), P(None, both)
    in_specs = (rows2, vec, vec, vec, cols2, rows2, vec, vec, cols2, rows2, rows2)
    out_specs = (rows2, rows2, vec, vec, cols2, rows2, vec, vec, cols2, rows2)
    return jax.shard_map(
        functools.partial(body, Plan(mesh)), mesh=mesh, in_specs=in_specs, out_specs=out_specs, check_vma=False
    )
```

```python
import functools
import math

import jax
import jax.numpy as jnp
from jax import lax
from jax.experimental import pallas as pl
from jax.experimental.pallas import tpu as pltpu
from jax.sharding import PartitionSpec as P

F32 = jnp.float32
BF16 = jnp.bfloat16
HEAD = 64
PAIR = 2 * HEAD
EPSILON = 1e-05
NEGATIVE = -1e30
TILE = 256
CHUNK = 32
AXES = ("dp", "fsdp")
GELU_A = math.sqrt(2.0 / math.pi)
GELU_B = GELU_A * 0.044715


def mm_nn(left, right):
    return jnp.dot(left, right, preferred_element_type=F32)


def mm_nt(left, right):
    return lax.dot_general(left, right, (((1,), (1,)), ((), ())), preferred_element_type=F32)


def mm_tn(left, right):
    return lax.dot_general(left, right, (((0,), (0,)), ((), ())), preferred_element_type=F32)


def norm_stats(values):
    average = jnp.mean(values, axis=-1, keepdims=True)
    centred = values - average
    variance = jnp.mean(centred * centred, axis=-1, keepdims=True)
    rinv = lax.rsqrt(variance + EPSILON)
    return centred * rinv, rinv


def params(mib=56):
    return pltpu.CompilerParams(vmem_limit_bytes=mib << 20)


def cost(flops, moved):
    return pl.CostEstimate(flops=int(flops), bytes_accessed=int(moved), transcendentals=0)


class Plan:
    def __init__(self, mesh):
        self.n = mesh.shape["dp"] * mesh.shape["fsdp"]
        self.bits = self.n.bit_length() - 1
        self.direct = self.n == 1 << self.bits and self.bits == 5 and mesh.shape["fsdp"] == 4
        self.along = (3, 4)
        self.across = (1, 2)

    @staticmethod
    def masks_of(bits):
        found = [0]
        for bit in bits:
            found = found + [m | 1 << bit for m in found]
        return found

    def slot_masks(self):
        return [m ^ k for m in self.masks_of(self.across) for k in self.masks_of(self.along)]

    def swap(self, value, mask):
        return lax.ppermute(value, AXES, [(i, i ^ mask) for i in range(self.n)])

    def spread_stage(self, held, bits):
        return jnp.concatenate([held] + [self.swap(held, m) for m in self.masks_of(bits)[1:]], axis=0)

    def gather(self, piece):
        held = self.spread_stage(self.spread_stage(piece[None], self.along), self.across)
        return held, self.swap(held, 1)

    def scatter_first(self, keep, send, cut):
        got = self.swap(send, 1)
        grid = (2, 2, -1) + keep.shape[1:]
        keep, got = keep.reshape(grid), got.reshape(grid)
        pair = lambda at: add_low(keep[at], [got[at]])
        every, head, tail = slice(None), slice(None, cut), slice(cut, None)
        one = [pair((every, y, every, head)) for y in range(2)]
        two = [pair((x, every, every, tail)) for x in range(2)]
        return one, two

    def scatter_rest(self, one, two, done, beside, late):
        inner = self.masks_of(self.along)
        arriving = self.swap(one[1], 2), self.swap(two[1], 4)
        stay = [add_low(own[0][0], [got[0]]) for own, got in ((one, arriving[0]), (two, arriving[1]))]
        goes = [add_low(own[0][1], [got[1]]) for own, got in ((one, arriving[0]), (two, arriving[1]))]
        goes, done = lax.optimization_barrier((goes, done))
        got = self.swap(goes[0], 4), self.swap(goes[1], 2)
        held = jnp.concatenate([add_low(stay[0], [got[0]]), add_low(stay[1], [got[1]])], axis=1)
        held, late = lax.optimization_barrier((held, late))
        arriving = [self.swap(held[z], m) for z, m in list(enumerate(inner))[1:]]
        arriving[0], beside = lax.optimization_barrier((arriving[0], beside))
        return add_low(held[0], arriving), done, beside, late

    def view(self, held):
        pieces, rows, width = held.shape
        return held.reshape(pieces // 4, 2, 2, 2, rows // 2, width)

    def first_away(self, keep, got):
        k, g = self.view(keep), self.view(got)
        return add_low(k[:, :, 1, 0], [g[:, :, 1, 0]]), add_low(k[:, 1, :, 1], [g[:, 1, :, 1]])

    def second_away(self, keep, got, back):
        k, g = self.view(keep), self.view(got)
        return (
            add_low(k[:, 1, 0, 0], [g[:, 1, 0, 0], back[0][:, 1]]),
            add_low(k[:, 0, 1, 1], [g[:, 0, 1, 1], back[1][:, 1]]),
        )

    def last_sum(self, keep, got, back, again):
        k, g = self.view(keep), self.view(got)
        both = [
            add_low(k[:, 0, 0, half], [g[:, 0, 0, half], back[half][:, 0], again[half]]) for half in range(2)
        ]
        whole = jnp.concatenate(both, axis=1)
        return whole.reshape(-1, whole.shape[-1])

    def along_sum(self, whole):
        line = [[r + 8 * z for z in range(self.n // 8)] for r in range(8)]
        return lax.psum_scatter(whole, AXES, scatter_dimension=0, tiled=True, axis_index_groups=line)


def add_low(first, others):
    total = first.astype(F32)
    for other in others:
        total = total + other.astype(F32)
    return total.astype(first.dtype)


def slot_of(masks, me, piece_pair):
    wanted = piece_pair ^ lax.div(me, 2)
    slot = jnp.int32(0)
    for s, m in enumerate(masks):
        slot = jnp.where(wanted == m // 2, s, slot)
    return slot


def qkv_kernel(masks, ppr, me_ref, x_ref, own_ref, sib_ref, e_ref, m_ref, mixed_ref, n1_ref, w_ref, vec_ref):
    me = me_ref[0]

    @pl.when(pl.program_id(0) == 0)
    def _():
        core = lax.rem(me, 2)
        for s, m in enumerate(masks):
            pair = lax.div(me, 2) ^ (m // 2)
            at = pl.ds(pl.multiple_of(pair * (2 * ppr), 16), 2 * ppr)
            both = [own_ref[s, :ppr, :], sib_ref[s, :ppr, :]]
            for side in range(2):

                @pl.when(core == side)
                def _():
                    w_ref[at, :] = jnp.concatenate([both[side], both[1 - side]], axis=0)

        packed = jnp.concatenate([own_ref[:, ppr, :128], sib_ref[:, ppr, :128]], axis=0)
        for v in range(4):
            vec_ref[v : v + 1, :] = jnp.sum(mm_nn(packed, e_ref[v]) * m_ref[...], axis=0, keepdims=True)

    xhat, rinv = norm_stats(x_ref[...].astype(F32))
    n1 = (xhat * vec_ref[0:1, :] + vec_ref[1:2, :]).astype(BF16)
    n1_ref[...] = n1
    mixed_ref[...] = mm_nt(n1, w_ref[...]).astype(BF16)


def qkv_project(plan, me, tokens, gathered, spread, place, out_cols, rows_block=256):
    rows, width = tokens.shape
    masks = plan.slot_masks()
    full = lambda a: pl.BlockSpec(a.shape, lambda r, *_: (0,) * a.ndim)
    whole = lambda shape: pl.BlockSpec(shape, lambda r, *_: (0,) * len(shape))
    return pl.pallas_call(
        functools.partial(qkv_kernel, masks, out_cols // plan.n),
        grid_spec=pltpu.PrefetchScalarGridSpec(
            num_scalar_prefetch=1,
            grid=(rows // rows_block,),
            in_specs=[
                pl.BlockSpec((rows_block, width), lambda r, *_: (r, 0)),
            ]
            + [full(a) for a in (*gathered, spread, place)],
            out_specs=[
                pl.BlockSpec((rows_block, out_cols), lambda r, *_: (r, 0)),
                pl.BlockSpec((rows_block, width), lambda r, *_: (r, 0)),
                whole((out_cols, width)), whole((8, width)),
            ],
        ),
        out_shape=[
            jax.ShapeDtypeStruct((rows, out_cols), BF16),
            jax.ShapeDtypeStruct((rows, width), BF16),
            jax.ShapeDtypeStruct((out_cols, width), BF16),
            jax.ShapeDtypeStruct((8, width), F32),
        ],
        compiler_params=params(),
        cost_estimate=cost(2 * rows * width * out_cols, 20e6),
        name="qkv_project",
    )(me, tokens, *gathered, spread, place)


def qkv_plain_kernel(x_ref, w_ref, vec_ref, mixed_ref, n1_ref):
    xhat, rinv = norm_stats(x_ref[...].astype(F32))
    n1 = (xhat * vec_ref[0:1, :] + vec_ref[1:2, :]).astype(BF16)
    n1_ref[...] = n1
    mixed_ref[...] = mm_nt(n1, w_ref[...]).astype(BF16)


def qkv_plain(tokens, w_abs, vecs, rows_block=256):
    rows, width = tokens.shape
    out_cols = w_abs.shape[0]
    full = lambda a: pl.BlockSpec(a.shape, lambda r: (0,) * a.ndim)
    return pl.pallas_call(
        qkv_plain_kernel,
        grid=(rows // rows_block,),
        in_specs=[pl.BlockSpec((rows_block, width), lambda r: (r, 0)), full(w_abs), full(vecs)],
        out_specs=[
            pl.BlockSpec((rows_block, out_cols), lambda r: (r, 0)),
            pl.BlockSpec((rows_block, width), lambda r: (r, 0)),
        ],
        out_shape=[
            jax.ShapeDtypeStruct((rows, out_cols), BF16),
            jax.ShapeDtypeStruct((rows, width), BF16),
        ],
        compiler_params=params(),
        name="qkv_plain",
    )(tokens, w_abs, vecs)


def tile_at(i, j):
    return i * (i + 1) // 2 + j

def attend_kernel(maxlen, len_ref, q_ref, k_ref, v_ref, att_ref, attT_ref, inv_ref, keep_ref):
    length = len_ref[pl.program_id(0)]
    q, k = q_ref[...], k_ref[...]
    qT = (q.astype(F32) * HEAD**-0.5).T.astype(BF16)
    vT = v_ref[...].astype(F32).T.astype(BF16)
    same = lax.broadcasted_iota(jnp.int32, (PAIR, PAIR), 0) // HEAD == lax.broadcasted_iota(jnp.int32, (PAIR, PAIR), 1) // HEAD
    same = jnp.where(same, 1.0, 0.0).astype(BF16)
    square = lambda a: jnp.max(mm_nn((a.astype(F32) * a.astype(F32)).astype(BF16), same))
    small = square(q) * square(k) * (1.03 / HEAD) < 70.0**2

    def block(i, plain):
        lo, hi = i * TILE, (i + 1) * TILE
        qpos = lo + lax.broadcasted_iota(jnp.int32, (1, TILE), 1)
        limit = jnp.minimum(qpos, length - 1)
        blank = jnp.zeros((HEAD, TILE), BF16)
        outs = []
        for h in range(2):
            own = qT[h * HEAD : (h + 1) * HEAD, lo:hi]
            own = jnp.concatenate([own, blank] if h == 0 else [blank, own], axis=0)

            def piece(at):
                s = mm_nn(k[at : at + CHUNK], own)
                t = s * s + 1.0
                r = lax.rsqrt(t)
                kpos = at + lax.broadcasted_iota(jnp.int32, (CHUNK, TILE), 0)
                return s, r, t * r, (kpos <= limit if at >= lo else kpos < length)

            top = None
            if not plain:
                for at in range(0, hi, CHUNK):
                    s, r, smooth, allowed = piece(at)
                    here = jnp.max(jnp.where(allowed, smooth, NEGATIVE), axis=0, keepdims=True)
                    top = here if top is None else jnp.maximum(top, here)
            total, weights = None, []
            for at in range(0, hi, CHUNK):
                s, r, smooth, allowed = piece(at)
                e = jnp.exp(smooth) if plain else jnp.exp(jnp.minimum(smooth - top, 0.0))
                e = jnp.where(allowed, e, 0.0)
                part = e.reshape(CHUNK // 8, 8, TILE).sum(axis=0)
                total = part if total is None else total + part
                g = jnp.tanh(s)
                w = g * e
                c = e * (s * r)
                a = e + g * (c - w)
                w = w.astype(BF16)
                weights.append(w)
                tile, row = tile_at(i, at // TILE), at % TILE
                keep_ref[0, h, 0, tile, row : row + CHUNK, :] = w
                keep_ref[0, h, 1, tile, row : row + CHUNK, :] = a.astype(BF16)
                keep_ref[0, h, 2, tile, row : row + CHUNK, :] = c.astype(BF16)
            inv = 1.0 / jnp.sum(total, axis=0, keepdims=True)
            inv_ref[0, h : h + 1, lo:hi] = inv
            outs.append(mm_nn(vT[h * HEAD : (h + 1) * HEAD, :hi], jnp.concatenate(weights, axis=0)) * inv)
        outT = jnp.concatenate(outs, axis=0)
        attT_ref[:, lo:hi] = outT.astype(BF16)
        att_ref[lo:hi, :] = outT.T.astype(BF16)

    @pl.when(small)
    def _():
        for i in range(maxlen // TILE):
            block(i, True)

    @pl.when(jnp.logical_not(small))
    def _():
        for i in range(maxlen // TILE):
            block(i, False)


def attend_forward(mixed, lengths):
    rows, width = mixed.shape[0], mixed.shape[1] // 3
    seqs = lengths.shape[0]
    maxlen, pairs = rows // seqs, width // PAIR
    tiles = tile_at(maxlen // TILE, 0)
    col = lambda part: pl.BlockSpec((maxlen, PAIR), lambda s, p, *_: (s, part * pairs + p))
    return pl.pallas_call(
        functools.partial(attend_kernel, maxlen),
        grid_spec=pltpu.PrefetchScalarGridSpec(
            num_scalar_prefetch=1,
            grid=(seqs, pairs),
            in_specs=[col(0), col(1), col(2)],
            out_specs=[
                col(0),
                pl.BlockSpec((PAIR, maxlen), lambda s, p, *_: (p, s)),
                pl.BlockSpec((1, 8, maxlen), lambda s, p, *_: (s * pairs + p, 0, 0)),
                pl.BlockSpec((1, 2, 3, tiles, TILE, TILE), lambda s, p, *_: (s * pairs + p, 0, 0, 0, 0, 0)),
            ],
        ),
        out_shape=[
            jax.ShapeDtypeStruct((rows, width), BF16),
            jax.ShapeDtypeStruct((width, rows), BF16),
            jax.ShapeDtypeStruct((seqs * pairs, 8, maxlen), F32),
            jax.ShapeDtypeStruct((seqs * pairs, 2, 3, tiles, TILE, TILE), BF16),
        ],
        compiler_params=params(),
        cost_estimate=cost(20e9, 60e6),
        name="attend_forward",
    )(lengths, mixed, mixed, mixed)


def attend_back_kernel(maxlen, q_ref, k_ref, v_ref, ga_ref, attT_ref, inv_ref, keep_ref, d_ref, sum_ref, dqT):
    qs = q_ref[...] * jnp.asarray(HEAD**-0.5, BF16)
    v = v_ref[...]
    kT = k_ref[...].astype(F32).T.astype(BF16)
    gaT = ga_ref[...].astype(F32).T
    prod = gaT * attT_ref[...].astype(F32)
    half = lambda h: slice(h * HEAD, (h + 1) * HEAD)
    inv = [inv_ref[0, h : h + 1, :] for h in range(2)]
    gaT = jnp.concatenate([gaT[half(h)] * inv[h] for h in range(2)], axis=0)
    ga = gaT.T.astype(BF16)
    gaT = gaT.astype(BF16)
    lane = lax.broadcasted_iota(jnp.int32, (maxlen, PAIR), 1)
    blank = jnp.zeros((HEAD, maxlen), BF16)
    nil = jnp.zeros((), BF16)
    heads = []
    for h in range(2):
        mine = (lane < HEAD) if h == 0 else (lane >= HEAD)
        own = gaT[half(h)]
        heads.append(
            (
                jnp.where(mine, ga, nil), jnp.where(mine, qs, nil),
                jnp.concatenate([own, blank] if h == 0 else [blank, own], axis=0), kT[half(h)],
                jnp.sum(prod[half(h)], axis=0, keepdims=True) * inv[h],
            )
        )
    blocks = maxlen // TILE
    for j in range(blocks):
        lo, hi = j * TILE, (j + 1) * TILE
        dv = dk = None
        for h in range(2):
            ga_h, q_h, gaT_h, kT_h, delta = heads[h]
            side = lambda part: jnp.concatenate([keep_ref[0, h, part, tile_at(i, j)] for i in range(j, blocks)], axis=1)
            gw = mm_nn(v[lo:hi], gaT_h[:, lo:])
            ds = (gw * side(1).astype(F32) - side(2).astype(F32) * delta[:, lo:]).astype(BF16)
            dv_h = mm_nn(side(0), ga_h[lo:])
            dk_h = mm_nn(ds, q_h[lo:])
            dv = dv_h if dv is None else dv + dv_h
            dk = dk_h if dk is None else dk + dk_h
            dq_h = mm_nn(kT_h[:, lo:hi], ds)
            if j == 0:
                dqT[half(h), :] = dq_h
            else:
                dqT[half(h), lo:] += dq_h
        d_ref[2, lo:hi, :] = dv.astype(BF16)
        d_ref[1, lo:hi, :] = dk.astype(BF16)
        sums = [jnp.sum(d, axis=0, keepdims=True) for d in (dk, dv)]
        total = sums if j == 0 else [t + d for t, d in zip(total, sums)]
    dq = (dqT[...] * HEAD**-0.5).T
    d_ref[0] = dq.astype(BF16)
    total = [jnp.sum(dq, axis=0, keepdims=True)] + total
    sum_ref[0] = jnp.concatenate(total + [jnp.zeros((5, PAIR), F32)], axis=0)


def attend_backward(mixed, ga, attT, inv, keep, seqs, first, count):
    rows, width = mixed.shape[0], mixed.shape[1] // 3
    maxlen, pairs = rows // seqs, width // PAIR
    col = lambda part: pl.BlockSpec((maxlen, PAIR), lambda s, p: (s, part * pairs + p + first))
    return pl.pallas_call(
        functools.partial(attend_back_kernel, maxlen),
        grid=(seqs, count),
        in_specs=[
            col(0), col(1), col(2), col(0),
            pl.BlockSpec((PAIR, maxlen), lambda s, p: (p + first, s)),
            pl.BlockSpec((1, 8, maxlen), lambda s, p: (s * pairs + p + first, 0, 0)),
            pl.BlockSpec((1,) + keep.shape[1:], lambda s, p: (s * pairs + p + first, 0, 0, 0, 0, 0)),
        ],
        out_specs=[
            pl.BlockSpec((3, maxlen, PAIR), lambda s, p: (0, s, p)),
            pl.BlockSpec((1, 8, PAIR), lambda s, p: (s, 0, p)),
        ],
        out_shape=[
            jax.ShapeDtypeStruct((3, rows, count * PAIR), BF16),
            jax.ShapeDtypeStruct((seqs, 8, count * PAIR), F32),
        ],
        scratch_shapes=[pltpu.VMEM((PAIR, maxlen), F32)],
        compiler_params=params(40),
        cost_estimate=cost(5e9 * count, 10e6 * count),
        name="attend_backward",
    )(mixed, mixed, mixed, ga, attT, inv, keep)


def project_kernel(att_ref, x_ref, wp_ref, vec_ref, res_ref, n2_ref, wo_ref):
    pieces, per, _ = wp_ref.shape

    @pl.when(pl.program_id(0) == 0)
    def _():
        for p in range(pieces):
            wo_ref[p * per : (p + 1) * per, :] = wp_ref[p]

    residual = x_ref[...].astype(F32) + mm_nn(att_ref[...], wo_ref[...])
    res_ref[...] = residual
    xhat, rinv = norm_stats(residual)
    n2_ref[...] = (xhat * vec_ref[2:3, :] + vec_ref[3:4, :]).astype(BF16)


def project_out(att, tokens, wo_pieces, at, vecs, rows_block=512):
    rows, width = tokens.shape
    pieces = wo_pieces.shape[0]
    block = pl.BlockSpec((rows_block, width), lambda r: (r, 0))
    full = lambda a: pl.BlockSpec(a.shape, lambda r: (0,) * a.ndim)
    return pl.pallas_call(
        project_kernel,
        grid=(rows // rows_block,),
        in_specs=[
            block, block, pl.BlockSpec((pieces, width // pieces, width), lambda r: (0, at, 0)), full(vecs),
        ],
        out_specs=[block, block, pl.BlockSpec((width, width), lambda r: (0, 0))],
        out_shape=[
            jax.ShapeDtypeStruct((rows, width), F32),
            jax.ShapeDtypeStruct((rows, width), BF16),
            jax.ShapeDtypeStruct((width, width), BF16),
        ],
        compiler_params=params(),
        cost_estimate=cost(2 * rows * width * width, 10e6),
        name="project_out",
    )(att, tokens, wo_pieces, vecs)


def live_grad(cot, lengths_ref, maxlen, first_row):
    rows = cot.shape[0]
    at = first_row + lax.broadcasted_iota(jnp.int32, (rows, 1), 0)
    seq = first_row // maxlen
    return jnp.where(at - seq * maxlen < lengths_ref[seq], cot, 0.0)


def mlp_kernel(units, me_ref, n2_ref, gl_ref, w_ref, act_ref, gn_ref, *gw_refs):
    step = pl.program_id(0)
    rows, width = n2_ref.shape

    pieces = w_ref.shape[0]
    wu = w_ref[:, :units, :].reshape(pieces * units, width)
    wd = w_ref[:, units : 2 * units, :].reshape(pieces * units, width)
    n2, gl = n2_ref[...], gl_ref[...]
    u = mm_nt(n2, wu)
    uu = u * u
    th = jnp.tanh(u * (GELU_A + GELU_B * uu))
    half = 0.5 * u
    act = (half + half * th).astype(BF16)
    slope = 0.5 + 0.5 * th + (half - half * (th * th)) * (GELU_A + (3.0 * GELU_B) * uu)
    act_ref[...] = act
    gp = (mm_nt(gl, wd) * slope).astype(BF16)
    gn = mm_nn(gp, wu)

    @pl.when(step == 0)
    def _():
        gn_ref[...] = gn

    @pl.when(step > 0)
    def _():
        gn_ref[...] += gn

    for at, grad in ((0, mm_tn(gp, n2)), (units, mm_tn(act, gl))):
        grad = grad.astype(BF16)
        if len(gw_refs) == 1:
            gw_refs[0][:, at : at + units, :] = grad.reshape(pieces, units, width)
            continue
        grad = grad.reshape(pieces // 2, 2, units, width)
        core = lax.rem(me_ref[0], 2)
        near = lax.rem(lax.div(me_ref[0], 2), 4)
        for side in range(2):

            @pl.when(core == side)
            def _():
                for place in range(pieces // 2):
                    slot = (place // 4) * 4 + ((place % 4) ^ near)
                    gw_refs[0][slot, at : at + units, :] = grad[place, side]
                    gw_refs[1][slot, at : at + units, :] = grad[place, 1 - side]


def feed_forward(me, n2, gl, w, units, split):
    rows, width = n2.shape
    pieces, held, _ = w.shape
    take = max(1, 768 // units)
    full = lambda: pl.BlockSpec((rows, width), lambda f, *_: (0, 0))
    outs = 2 if split else 1
    grads = [pl.BlockSpec((take // outs, 2 * units, width), lambda f, *_: (f, 0, 0))] * outs
    return pl.pallas_call(
        functools.partial(mlp_kernel, units),
        grid_spec=pltpu.PrefetchScalarGridSpec(
            num_scalar_prefetch=1,
            grid=(pieces // take,),
            in_specs=[
                full(), full(), pl.BlockSpec((take, held, width), lambda f, *_: (f, 0, 0)),
            ],
            out_specs=[pl.BlockSpec((rows, take * units), lambda f, *_: (0, f)), full()] + grads,
        ),
        out_shape=[jax.ShapeDtypeStruct((rows, pieces * units), BF16), jax.ShapeDtypeStruct((rows, width), F32)]
        + [jax.ShapeDtypeStruct((pieces // outs, 2 * units, width), BF16)] * outs,
        compiler_params=params(),
        cost_estimate=cost(10 * rows * width * pieces * units, 40e6),
        name="feed_forward",
    )(me, n2, gl, w)


def finish_kernel(units, act_ref, w_ref, res_ref, out_ref, acc_s):
    step = pl.program_id(0)
    pieces, _, width = w_ref.shape
    part = mm_nn(act_ref[...], w_ref[:, units : 2 * units, :].reshape(pieces * units, width))

    @pl.when(step == 0)
    def _():
        acc_s[...] = part + res_ref[...]

    @pl.when(step > 0)
    def _():
        acc_s[...] += part

    @pl.when(step == pl.num_programs(0) - 1)
    def _():
        out_ref[...] = acc_s[...].astype(BF16)


def finish_output(act, w, residual, units):
    rows, width = residual.shape
    pieces, held, _ = w.shape
    take = max(1, 768 // units)
    full = lambda: pl.BlockSpec((rows, width), lambda f: (0, 0))
    return pl.pallas_call(
        functools.partial(finish_kernel, units),
        grid=(pieces // take,),
        in_specs=[
            pl.BlockSpec((rows, take * units), lambda f: (0, f)),
            pl.BlockSpec((take, held, width), lambda f: (f, 0, 0)), full(),
        ],
        out_specs=full(),
        out_shape=jax.ShapeDtypeStruct((rows, width), BF16),
        scratch_shapes=[pltpu.VMEM((rows, width), F32)],
        compiler_params=params(),
        cost_estimate=cost(2 * rows * width * pieces * units, 20e6),
        name="finish_output",
    )(act, w, residual)


def norm_back(grad, xhat, rinv, gain):
    dh = grad * gain
    first = jnp.mean(dh, axis=-1, keepdims=True)
    second = jnp.mean(dh * xhat, axis=-1, keepdims=True)
    return rinv * (dh - first - xhat * second)


def middle_kernel(maxlen, len_ref, gn_ref, res_ref, cot_ref, att_ref, wo_ref, vec_ref, gres_ref, ga_ref, gwo_ref, gvec_ref, low_s):
    step = pl.program_id(0)
    rows = gn_ref.shape[0]
    gn = gn_ref[...]
    xhat, rinv = norm_stats(res_ref[...])
    gres = live_grad(cot_ref[...], len_ref, maxlen, step * rows) + norm_back(gn, xhat, rinv, vec_ref[2:3, :])
    gres_ref[...] = gres
    low = gres.astype(BF16)
    low_s[pl.ds(pl.multiple_of(step * rows, rows), rows), :] = low
    ga_ref[...] = mm_nt(low, wo_ref[...]).astype(BF16)

    @pl.when(step == 0)
    def _():
        gvec_ref[...] = jnp.zeros_like(gvec_ref)

    gvec_ref[0:1, :] += jnp.sum(gn * xhat, axis=0, keepdims=True)
    gvec_ref[1:2, :] += jnp.sum(gn, axis=0, keepdims=True)

    @pl.when(step == pl.num_programs(0) - 1)
    def _():
        gwo_ref[...] = mm_tn(att_ref[...], low_s[...]).astype(BF16)


def middle_back(lengths, gn, residual, cot, att, wo, vecs):
    rows, width = gn.shape
    rows_block = rows // lengths.shape[0]
    block = pl.BlockSpec((rows_block, width), lambda r, *_: (r, 0))
    full = lambda shape: pl.BlockSpec(shape, lambda r, *_: (0,) * len(shape))
    return pl.pallas_call(
        functools.partial(middle_kernel, rows // lengths.shape[0]),
        grid_spec=pltpu.PrefetchScalarGridSpec(
            num_scalar_prefetch=1,
            grid=(rows // rows_block,),
            in_specs=[block, block, block, full(att.shape), full(wo.shape), full(vecs.shape)],
            out_specs=[block, block, full(wo.shape), full((8, width))],
            scratch_shapes=[pltpu.VMEM((rows, width), BF16)],
        ),
        out_shape=[
            jax.ShapeDtypeStruct((rows, width), F32),
            jax.ShapeDtypeStruct((rows, width), BF16),
            jax.ShapeDtypeStruct(wo.shape, BF16),
            jax.ShapeDtypeStruct((8, width), F32),
        ],
        compiler_params=params(48),
        cost_estimate=cost(4 * rows * width * width, 30e6),
        name="middle_back",
    )(lengths, gn, residual, cot, att, wo, vecs)


def qkv_grad_kernel(masks, ppr, opr, me_ref, *refs):
    d1_ref, d2_ref, sum1_ref, sum2_ref, n1_ref, w_ref, gwo_ref, vec_ref, gvec2_ref, e_ref, keep_ref, send_ref, low_s, acc_s = refs
    rows, width = n1_ref.shape
    part = pl.program_id(0)
    n1 = n1_ref[...]
    paired, gshift, at = jnp.zeros((1, width), F32), jnp.zeros((8, width), F32), 0
    for d_ref, sum_ref in ((d1_ref, sum1_ref), (d2_ref, sum2_ref)):
        cols = d_ref.shape[2]
        gw = mm_tn(d_ref[0], n1)
        low_s[pl.ds(pl.multiple_of(part * width + at, PAIR), cols), :] = gw.astype(BF16)
        w = w_ref[at : at + cols, :]
        paired += jnp.sum(gw * w.astype(F32), axis=0, keepdims=True)
        total = jnp.sum(sum_ref[...], axis=0)
        pick = lax.broadcasted_iota(jnp.int32, (8, 1), 0) == part
        total = jnp.sum(jnp.where(pick, total, 0.0), axis=0, keepdims=True)
        high = total.astype(BF16).astype(F32)
        low = jnp.concatenate([high, total - high, jnp.zeros((6, cols), F32)], axis=0)
        gshift += mm_nn(low.astype(BF16), w)
        at += cols

    @pl.when(part == 0)
    def _():
        acc_s[...] = jnp.zeros_like(acc_s)

    acc_s[0:1, :] += paired
    acc_s[1:2, :] += gshift[0:1, :] + gshift[1:2, :]

    @pl.when(part == 2)
    def _():
        qkv_grad_pieces(masks, ppr, opr, me_ref, acc_s, gwo_ref, vec_ref, gvec2_ref, e_ref, keep_ref, send_ref, low_s)


def qkv_grad_pieces(masks, ppr, opr, me_ref, acc_s, gwo_ref, vec_ref, gvec2_ref, e_ref, keep_ref, send_ref, low_s):
    width = acc_s.shape[1]
    paired, gshift = acc_s[0:1, :], acc_s[1:2, :]
    ggain = (paired - vec_ref[1:2, :] * gshift) / vec_ref[0:1, :]
    n = 2 * len(masks)
    owner = lax.broadcasted_iota(jnp.int32, (n, width), 1) // opr == lax.broadcasted_iota(jnp.int32, (n, width), 0)
    packed = jnp.zeros((n, 128), F32)
    for v, row in enumerate((ggain, gshift, gvec2_ref[0:1, :], gvec2_ref[1:2, :])):
        packed += mm_nt(jnp.where(owner, row, 0.0).astype(BF16), e_ref[v])
    me = me_ref[0]
    core = lax.rem(me, 2)
    for pair in range(len(masks)):
        slot = slot_of(masks, me, pair)
        sides = []
        for j in (2 * pair, 2 * pair + 1):
            extra = jnp.concatenate([packed[j : j + 1, :], jnp.zeros((1, width - 128), F32)], axis=1)
            extra = jnp.concatenate([extra, jnp.zeros((7, width), F32)], axis=0)
            sides.append((low_s[j * ppr : (j + 1) * ppr, :], gwo_ref[j * opr : (j + 1) * opr, :], extra.astype(BF16)))
        for side in range(2):

            @pl.when(core == side)
            def _():
                for out, part in ((keep_ref, sides[side]), (send_ref, sides[1 - side])):
                    out[slot] = jnp.concatenate(part, axis=0)


def qkv_grad(plan, me, grads, sums, n1, w_abs, gwo, vecs, gvec2, spread):
    rows, width = n1.shape
    masks = plan.slot_masks()
    ppr, opr = 3 * width // plan.n, width // plan.n
    full = lambda a: pl.BlockSpec(a.shape, lambda p, *_: (0,) * len(a.shape))
    shape = jax.ShapeDtypeStruct((len(masks), ppr + opr + 8, width), BF16)
    return pl.pallas_call(
        functools.partial(qkv_grad_kernel, masks, ppr, opr),
        grid_spec=pltpu.PrefetchScalarGridSpec(
            num_scalar_prefetch=1,
            grid=(3,),
            in_specs=[pl.BlockSpec((1, rows, d.shape[2]), lambda p, *_: (p, 0, 0)) for d in grads]
            + [full(a) for a in (*sums, n1)]
            + [pl.BlockSpec((width, width), lambda p, *_: (p, 0))]
            + [full(a) for a in (gwo, vecs, gvec2, spread)],
            out_specs=[full(shape), full(shape)],
            scratch_shapes=[pltpu.VMEM((3 * width, width), BF16), pltpu.VMEM((8, width), F32)],
        ),
        out_shape=[shape, shape],
        compiler_params=params(40),
        cost_estimate=cost(6 * rows * width * width, 25e6),
        name="qkv_grad",
    )(me, *grads, *sums, n1, w_abs, gwo, vecs, gvec2, spread)


def qkv_grad_plain_kernel(d_ref, n1_ref, out_ref):
    out_ref[...] = mm_tn(d_ref[...], n1_ref[...]).astype(BF16)


def qkv_grad_plain(grads, n1):
    rows, width = n1.shape
    vm = pl.BlockSpec(memory_space=pltpu.VMEM)
    found = []
    for part in range(3):
        for d in grads:
            call = pl.pallas_call(
                qkv_grad_plain_kernel,
                in_specs=[vm, vm],
                out_specs=vm,
                out_shape=jax.ShapeDtypeStruct((d.shape[2], width), BF16),
                compiler_params=params(),
                name="qkv_grad_plain",
            )
            found.append(call(d[part], n1))
    return jnp.concatenate(found, axis=0)


def first_kernel(d1_ref, d2_ref, w_ref, x_ref, gres_ref, vec_ref, gtok_ref, gvec_ref):
    width = x_ref.shape[1]
    gn = jnp.zeros(x_ref.shape, F32)
    for part in range(3):
        at = part * width
        for ref in (d1_ref, d2_ref):
            gn += mm_nn(ref[part], w_ref[at : at + ref.shape[2], :])
            at += ref.shape[2]
    xhat, rinv = norm_stats(x_ref[...].astype(F32))
    gtok_ref[...] = gres_ref[...] + norm_back(gn, xhat, rinv, vec_ref[0:1, :])

    @pl.when(pl.program_id(0) == 0)
    def _():
        gvec_ref[...] = jnp.zeros_like(gvec_ref)

    gvec_ref[0:1, :] += jnp.sum(gn * xhat, axis=0, keepdims=True)
    gvec_ref[1:2, :] += jnp.sum(gn, axis=0, keepdims=True)


def first_back(grads, w_abs, tokens, gres, vecs, rows_block=256):
    rows, width = tokens.shape
    block = pl.BlockSpec((rows_block, width), lambda r: (r, 0))
    full = lambda shape: pl.BlockSpec(shape, lambda r: (0,) * len(shape))
    return pl.pallas_call(
        first_kernel,
        grid=(rows // rows_block,),
        in_specs=[pl.BlockSpec((3, rows_block, d.shape[2]), lambda r: (0, r, 0)) for d in grads]
        + [full(w_abs.shape), block, block, full(vecs.shape)],
        out_specs=[block, full((8, width))],
        out_shape=[jax.ShapeDtypeStruct((rows, width), F32), jax.ShapeDtypeStruct((8, width), F32)],
        compiler_params=params(),
        cost_estimate=cost(6 * rows * width * width, 25e6),
        name="first_back",
    )(*grads, w_abs, tokens, gres, vecs)


def body(plan, tokens, lengths, ln1_gain, ln1_shift, w_qkv, w_out, ln2_gain, ln2_shift, w_up, w_down, cot):
    rows, width = tokens.shape
    n = plan.n
    seqs = lengths.shape[0]
    me = lax.axis_index(AXES).astype(jnp.int32)
    me_arr = me[None]
    vec_piece = jnp.stack([ln1_gain, ln1_shift, ln2_gain, ln2_shift])
    per = vec_piece.shape[1]
    qkv_piece = w_qkv.T
    ppr, units = qkv_piece.shape[0], w_down.shape[0]
    ff = units * n

    mlp_piece = jnp.concatenate([w_up.T, w_down, w_out], axis=0)
    mlp_all = lax.all_gather(mlp_piece, AXES, axis=0, tiled=True).reshape(n, -1, width)
    if plan.direct:
        w_ff, ff_units, wo_pieces, wo_at = mlp_all, units, mlp_all, 2 * units // per
    else:
        ff_units = 768
        wo_pieces, wo_at = mlp_all[:, 2 * units :].reshape(1, width, width), 0
        w_ff = mlp_all[:, : 2 * units].reshape(n, 2, units, width).transpose(1, 0, 2, 3)
        w_ff = w_ff.reshape(2, ff // 768, 768, width).transpose(1, 0, 2, 3).reshape(ff // 768, 2 * 768, width)

    maxlen = rows // seqs
    live = (lax.iota(jnp.int32, maxlen)[None, :] < lengths[:, None]).reshape(rows, 1)
    grad_low = jnp.where(live, cot, 0.0).astype(BF16)
    if plan.direct:
        flat = jnp.pad(vec_piece.reshape(1, -1), ((0, 7), (0, width - 4 * per)))
        gathered = plan.gather(jnp.concatenate([qkv_piece, flat], axis=0))
        gathered, grad_low = lax.optimization_barrier((gathered, grad_low))
        slots = jnp.array(plan.slot_masks() + [m ^ 1 for m in plan.slot_masks()], jnp.int32)
        column = jnp.arange(width, dtype=jnp.int32)
        place = ((slots ^ me)[:, None] == (column // per)[None]).astype(F32)
        lane = jnp.arange(128, dtype=jnp.int32)
        spread = jnp.stack([(lane[:, None] == v * per + (column % per)[None]).astype(BF16) for v in range(4)])
        mixed, n1, w_abs, vecs = qkv_project(plan, me_arr, tokens, gathered, spread, place, ppr * n)
    else:
        w_abs = lax.all_gather(qkv_piece, AXES, axis=0, tiled=True)
        vecs = lax.all_gather(vec_piece, AXES, axis=1, tiled=True).astype(F32)
        vecs = jnp.pad(vecs, ((0, 4), (0, 0)))
        mixed, n1 = qkv_plain(tokens, w_abs, vecs)

    att, attT, inv, kept = attend_forward(mixed, lengths)
    residual, n2, wo = project_out(att, tokens, wo_pieces, wo_at, vecs)
    act, gn2, *gw_ff = feed_forward(me_arr, n2, grad_low, w_ff, ff_units, plan.direct)
    if plan.direct:
        got = plan.swap(gw_ff[1], 1)
    else:
        gw_ff = gw_ff[0].reshape(ff // 768, 2, 768, width).transpose(1, 0, 2, 3)
        gw_ff = gw_ff.reshape(2, n, units, width).transpose(1, 0, 2, 3).reshape(-1, width)
        g_ff = lax.psum_scatter(gw_ff, AXES, scatter_dimension=0, tiled=True)
    gres, ga, gwo, gvec2 = middle_back(lengths, gn2, residual, cot, att, wo, vecs)
    pairs = width // PAIR
    late = pairs // 6
    if plan.direct:
        ga, got, keep = lax.optimization_barrier((ga, got, gw_ff[0]))
        away = plan.first_away(keep, got)
        back = (plan.swap(away[0], 2), plan.swap(away[1], 4))
        ga, away = lax.optimization_barrier((ga, away))
    grads, sums = attend_backward(mixed, ga, attT, inv, kept, seqs, 0, pairs - late)
    if plan.direct:
        back, grads, ga, sums = lax.optimization_barrier((back, grads, ga, sums))
        away = plan.second_away(keep, got, back)
        again = (plan.swap(away[0], 4), plan.swap(away[1], 2))
        ga, away = lax.optimization_barrier((ga, away))
    more, late_sums = attend_backward(mixed, ga, attT, inv, kept, seqs, pairs - late, late)
    grads, sums = [grads, more], [sums, late_sums]
    if plan.direct:
        q_keep, q_send = qkv_grad(plan, me_arr, grads, sums, n1, w_abs, gwo, vecs, gvec2, spread)
        again, q_keep, q_send = lax.optimization_barrier((again, q_keep, q_send))
        whole, q_keep = lax.optimization_barrier((plan.last_sum(keep, got, back, again), q_keep))
        g_ff = plan.along_sum(whole)
        summed = plan.scatter_first(q_keep, q_send, 48)
        act, summed = lax.optimization_barrier((act, summed))
        output = finish_output(act, w_ff, residual, ff_units)
        g_attn, output, g_ff, gres = plan.scatter_rest(*summed, output, g_ff, gres)
        g_qkv, g_out = g_attn[:ppr], g_attn[ppr : ppr + per]
        g_vec = g_attn[ppr + per, : 4 * per].astype(F32).reshape(4, per)
    else:
        g_qkv = lax.psum_scatter(qkv_grad_plain(grads, n1), AXES, scatter_dimension=0, tiled=True)
        g_out = lax.psum_scatter(gwo, AXES, scatter_dimension=0, tiled=True)
    gtok, gvec1 = first_back(grads, w_abs, tokens, gres, vecs)
    if not plan.direct:
        output = finish_output(act, w_ff, residual, ff_units)
        gvec = jnp.concatenate([gvec1[:2], gvec2[:2]], axis=0)
        g_vec = lax.psum_scatter(gvec, AXES, scatter_dimension=1, tiled=True)
    return (
        output, gtok, g_vec[0], g_vec[1], g_qkv.astype(F32).T, g_out.astype(F32), g_vec[2], g_vec[3],
        g_ff[:units].astype(F32).T, g_ff[units:].astype(F32),
    )


def solution(mesh):
    both = AXES
    rows2, vec, cols2 = P(both, None), P(both), P(None, both)
    in_specs = (rows2, vec, vec, vec, cols2, rows2, vec, vec, cols2, rows2, rows2)
    out_specs = (rows2, rows2, vec, vec, cols2, rows2, vec, vec, cols2, rows2)
    return jax.shard_map(
        functools.partial(body, Plan(mesh)), mesh=mesh, in_specs=in_specs, out_specs=out_specs, check_vma=False
    )
```

```python
import functools
import math

import jax
import jax.numpy as jnp
from jax import lax
from jax.experimental import pallas as pl
from jax.experimental.pallas import tpu as pltpu
from jax.sharding import PartitionSpec as P

F32 = jnp.float32
BF16 = jnp.bfloat16
HEAD = 64
PAIR = 2 * HEAD
EPSILON = 1e-05
NEGATIVE = -1e30
TILE = 256
CHUNK = 32
AXES = ("dp", "fsdp")
GELU_A = math.sqrt(2.0 / math.pi)
GELU_B = GELU_A * 0.044715


def mm_nn(left, right):
    return jnp.dot(left, right, preferred_element_type=F32)


def mm_nt(left, right):
    return lax.dot_general(left, right, (((1,), (1,)), ((), ())), preferred_element_type=F32)


def mm_tn(left, right):
    return lax.dot_general(left, right, (((0,), (0,)), ((), ())), preferred_element_type=F32)


def norm_stats(values):
    average = jnp.mean(values, axis=-1, keepdims=True)
    centred = values - average
    variance = jnp.mean(centred * centred, axis=-1, keepdims=True)
    rinv = lax.rsqrt(variance + EPSILON)
    return centred * rinv, rinv


def params(mib=56):
    return pltpu.CompilerParams(vmem_limit_bytes=mib << 20)


def cost(flops, moved):
    return pl.CostEstimate(flops=int(flops), bytes_accessed=int(moved), transcendentals=0)


class Plan:
    def __init__(self, mesh):
        self.n = mesh.shape["dp"] * mesh.shape["fsdp"]
        self.bits = self.n.bit_length() - 1
        self.direct = self.n == 1 << self.bits and self.bits == 5 and mesh.shape["fsdp"] == 4
        self.along = (3, 4)
        self.across = (1, 2)

    @staticmethod
    def masks_of(bits):
        found = [0]
        for bit in bits:
            found = found + [m | 1 << bit for m in found]
        return found

    def slot_masks(self):
        return [m ^ k for m in self.masks_of(self.across) for k in self.masks_of(self.along)]

    def swap(self, value, mask):
        return lax.ppermute(value, AXES, [(i, i ^ mask) for i in range(self.n)])

    def spread_stage(self, held, bits):
        return jnp.concatenate([held] + [self.swap(held, m) for m in self.masks_of(bits)[1:]], axis=0)

    def gather(self, piece):
        held = self.spread_stage(self.spread_stage(piece[None], self.along), self.across)
        return held, self.swap(held, 1)

    def scatter_first(self, keep, send, cut):
        got = self.swap(send, 1)
        grid = (2, 2, -1) + keep.shape[1:]
        keep, got = keep.reshape(grid), got.reshape(grid)
        pair = lambda at: add_low(keep[at], [got[at]])
        every, head, tail = slice(None), slice(None, cut), slice(cut, None)
        one = [pair((every, y, every, head)) for y in range(2)]
        two = [pair((x, every, every, tail)) for x in range(2)]
        return one, two

    def scatter_rest(self, one, two, done, beside, late):
        inner = self.masks_of(self.along)
        arriving = self.swap(one[1], 2), self.swap(two[1], 4)
        stay = [add_low(own[0][0], [got[0]]) for own, got in ((one, arriving[0]), (two, arriving[1]))]
        goes = [add_low(own[0][1], [got[1]]) for own, got in ((one, arriving[0]), (two, arriving[1]))]
        goes, done = lax.optimization_barrier((goes, done))
        got = self.swap(goes[0], 4), self.swap(goes[1], 2)
        held = jnp.concatenate([add_low(stay[0], [got[0]]), add_low(stay[1], [got[1]])], axis=1)
        held, late = lax.optimization_barrier((held, late))
        arriving = [self.swap(held[z], m) for z, m in list(enumerate(inner))[1:]]
        arriving[0], beside = lax.optimization_barrier((arriving[0], beside))
        return add_low(held[0], arriving), done, beside, late

    def view(self, held):
        pieces, rows, width = held.shape
        return held.reshape(pieces // 4, 2, 2, 2, rows // 2, width)

    def first_away(self, keep, got):
        k, g = self.view(keep), self.view(got)
        return add_low(k[:, :, 1, 0], [g[:, :, 1, 0]]), add_low(k[:, 1, :, 1], [g[:, 1, :, 1]])

    def second_away(self, keep, got, back):
        k, g = self.view(keep), self.view(got)
        return (
            add_low(k[:, 1, 0, 0], [g[:, 1, 0, 0], back[0][:, 1]]),
            add_low(k[:, 0, 1, 1], [g[:, 0, 1, 1], back[1][:, 1]]),
        )

    def last_sum(self, keep, got, back, again):
        k, g = self.view(keep), self.view(got)
        both = [
            add_low(k[:, 0, 0, half], [g[:, 0, 0, half], back[half][:, 0], again[half]]) for half in range(2)
        ]
        whole = jnp.concatenate(both, axis=1)
        return whole.reshape(-1, whole.shape[-1])

    def along_sum(self, whole):
        line = [[r + 8 * z for z in range(self.n // 8)] for r in range(8)]
        return lax.psum_scatter(whole, AXES, scatter_dimension=0, tiled=True, axis_index_groups=line)


def add_low(first, others):
    total = first.astype(F32)
    for other in others:
        total = total + other.astype(F32)
    return total.astype(first.dtype)


def slot_of(masks, me, piece_pair):
    wanted = piece_pair ^ lax.div(me, 2)
    slot = jnp.int32(0)
    for s, m in enumerate(masks):
        slot = jnp.where(wanted == m // 2, s, slot)
    return slot


def qkv_kernel(masks, ppr, me_ref, x_ref, own_ref, sib_ref, e_ref, m_ref, mixed_ref, n1_ref, w_ref, vec_ref):
    me = me_ref[0]

    @pl.when(pl.program_id(0) == 0)
    def _():
        core = lax.rem(me, 2)
        for s, m in enumerate(masks):
            pair = lax.div(me, 2) ^ (m // 2)
            at = pl.ds(pl.multiple_of(pair * (2 * ppr), 16), 2 * ppr)
            both = [own_ref[s, :ppr, :], sib_ref[s, :ppr, :]]
            for side in range(2):

                @pl.when(core == side)
                def _():
                    w_ref[at, :] = jnp.concatenate([both[side], both[1 - side]], axis=0)

        packed = jnp.concatenate([own_ref[:, ppr, :128], sib_ref[:, ppr, :128]], axis=0)
        for v in range(4):
            vec_ref[v : v + 1, :] = jnp.sum(mm_nn(packed, e_ref[v]) * m_ref[...], axis=0, keepdims=True)

    xhat, rinv = norm_stats(x_ref[...].astype(F32))
    n1 = (xhat * vec_ref[0:1, :] + vec_ref[1:2, :]).astype(BF16)
    n1_ref[...] = n1
    mixed_ref[...] = mm_nt(n1, w_ref[...]).astype(BF16)


def qkv_project(plan, me, tokens, gathered, spread, place, out_cols, rows_block=256):
    rows, width = tokens.shape
    masks = plan.slot_masks()
    full = lambda a: pl.BlockSpec(a.shape, lambda r, *_: (0,) * a.ndim)
    whole = lambda shape: pl.BlockSpec(shape, lambda r, *_: (0,) * len(shape))
    return pl.pallas_call(
        functools.partial(qkv_kernel, masks, out_cols // plan.n),
        grid_spec=pltpu.PrefetchScalarGridSpec(
            num_scalar_prefetch=1,
            grid=(rows // rows_block,),
            in_specs=[
                pl.BlockSpec((rows_block, width), lambda r, *_: (r, 0)),
            ]
            + [full(a) for a in (*gathered, spread, place)],
            out_specs=[
                pl.BlockSpec((rows_block, out_cols), lambda r, *_: (r, 0)),
                pl.BlockSpec((rows_block, width), lambda r, *_: (r, 0)),
                whole((out_cols, width)), whole((8, width)),
            ],
        ),
        out_shape=[
            jax.ShapeDtypeStruct((rows, out_cols), BF16),
            jax.ShapeDtypeStruct((rows, width), BF16),
            jax.ShapeDtypeStruct((out_cols, width), BF16),
            jax.ShapeDtypeStruct((8, width), F32),
        ],
        compiler_params=params(),
        cost_estimate=cost(2 * rows * width * out_cols, 20e6),
        name="qkv_project",
    )(me, tokens, *gathered, spread, place)


def qkv_plain_kernel(x_ref, w_ref, vec_ref, mixed_ref, n1_ref):
    xhat, rinv = norm_stats(x_ref[...].astype(F32))
    n1 = (xhat * vec_ref[0:1, :] + vec_ref[1:2, :]).astype(BF16)
    n1_ref[...] = n1
    mixed_ref[...] = mm_nt(n1, w_ref[...]).astype(BF16)


def qkv_plain(tokens, w_abs, vecs, rows_block=256):
    rows, width = tokens.shape
    out_cols = w_abs.shape[0]
    full = lambda a: pl.BlockSpec(a.shape, lambda r: (0,) * a.ndim)
    return pl.pallas_call(
        qkv_plain_kernel,
        grid=(rows // rows_block,),
        in_specs=[pl.BlockSpec((rows_block, width), lambda r: (r, 0)), full(w_abs), full(vecs)],
        out_specs=[
            pl.BlockSpec((rows_block, out_cols), lambda r: (r, 0)),
            pl.BlockSpec((rows_block, width), lambda r: (r, 0)),
        ],
        out_shape=[
            jax.ShapeDtypeStruct((rows, out_cols), BF16),
            jax.ShapeDtypeStruct((rows, width), BF16),
        ],
        compiler_params=params(),
        name="qkv_plain",
    )(tokens, w_abs, vecs)


def tile_at(i, j):
    return i * (i + 1) // 2 + j

def attend_kernel(maxlen, len_ref, q_ref, k_ref, v_ref, att_ref, attT_ref, inv_ref, keep_ref):
    length = len_ref[pl.program_id(0)]
    q, k = q_ref[...], k_ref[...]
    qT = (q.astype(F32) * HEAD**-0.5).T.astype(BF16)
    vT = v_ref[...].astype(F32).T.astype(BF16)
    same = lax.broadcasted_iota(jnp.int32, (PAIR, PAIR), 0) // HEAD == lax.broadcasted_iota(jnp.int32, (PAIR, PAIR), 1) // HEAD
    same = jnp.where(same, 1.0, 0.0).astype(BF16)
    square = lambda a: jnp.max(mm_nn((a.astype(F32) * a.astype(F32)).astype(BF16), same))
    small = square(q) * square(k) * (1.03 / HEAD) < 70.0**2

    def block(i, plain):
        lo, hi = i * TILE, (i + 1) * TILE
        qpos = lo + lax.broadcasted_iota(jnp.int32, (1, TILE), 1)
        limit = jnp.minimum(qpos, length - 1)
        blank = jnp.zeros((HEAD, TILE), BF16)
        outs = []
        for h in range(2):
            own = qT[h * HEAD : (h + 1) * HEAD, lo:hi]
            own = jnp.concatenate([own, blank] if h == 0 else [blank, own], axis=0)

            def piece(at):
                s = mm_nn(k[at : at + CHUNK], own)
                t = s * s + 1.0
                r = lax.rsqrt(t)
                kpos = at + lax.broadcasted_iota(jnp.int32, (CHUNK, TILE), 0)
                return s, r, t * r, (kpos <= limit if at >= lo else kpos < length)

            top = None
            if not plain:
                for at in range(0, hi, CHUNK):
                    s, r, smooth, allowed = piece(at)
                    here = jnp.max(jnp.where(allowed, smooth, NEGATIVE), axis=0, keepdims=True)
                    top = here if top is None else jnp.maximum(top, here)
            total, weights = None, []
            for at in range(0, hi, CHUNK):
                s, r, smooth, allowed = piece(at)
                e = jnp.exp(smooth) if plain else jnp.exp(jnp.minimum(smooth - top, 0.0))
                e = jnp.where(allowed, e, 0.0)
                part = e.reshape(CHUNK // 8, 8, TILE).sum(axis=0)
                total = part if total is None else total + part
                g = jnp.tanh(s)
                w = g * e
                c = e * (s * r)
                a = e + g * (c - w)
                w = w.astype(BF16)
                weights.append(w)
                tile, row = tile_at(i, at // TILE), at % TILE
                keep_ref[0, h, 0, tile, row : row + CHUNK, :] = w
                keep_ref[0, h, 1, tile, row : row + CHUNK, :] = a.astype(BF16)
                keep_ref[0, h, 2, tile, row : row + CHUNK, :] = c.astype(BF16)
            inv = 1.0 / jnp.sum(total, axis=0, keepdims=True)
            inv_ref[0, h : h + 1, lo:hi] = inv
            outs.append(mm_nn(vT[h * HEAD : (h + 1) * HEAD, :hi], jnp.concatenate(weights, axis=0)) * inv)
        outT = jnp.concatenate(outs, axis=0)
        attT_ref[:, lo:hi] = outT.astype(BF16)
        att_ref[lo:hi, :] = outT.T.astype(BF16)

    @pl.when(small)
    def _():
        for i in range(maxlen // TILE):
            block(i, True)

    @pl.when(jnp.logical_not(small))
    def _():
        for i in range(maxlen // TILE):
            block(i, False)


def attend_forward(mixed, lengths):
    rows, width = mixed.shape[0], mixed.shape[1] // 3
    seqs = lengths.shape[0]
    maxlen, pairs = rows // seqs, width // PAIR
    tiles = tile_at(maxlen // TILE, 0)
    col = lambda part: pl.BlockSpec((maxlen, PAIR), lambda s, p, *_: (s, part * pairs + p))
    return pl.pallas_call(
        functools.partial(attend_kernel, maxlen),
        grid_spec=pltpu.PrefetchScalarGridSpec(
            num_scalar_prefetch=1,
            grid=(seqs, pairs),
            in_specs=[col(0), col(1), col(2)],
            out_specs=[
                col(0),
                pl.BlockSpec((PAIR, maxlen), lambda s, p, *_: (p, s)),
                pl.BlockSpec((1, 8, maxlen), lambda s, p, *_: (s * pairs + p, 0, 0)),
                pl.BlockSpec((1, 2, 3, tiles, TILE, TILE), lambda s, p, *_: (s * pairs + p, 0, 0, 0, 0, 0)),
            ],
        ),
        out_shape=[
            jax.ShapeDtypeStruct((rows, width), BF16),
            jax.ShapeDtypeStruct((width, rows), BF16),
            jax.ShapeDtypeStruct((seqs * pairs, 8, maxlen), F32),
            jax.ShapeDtypeStruct((seqs * pairs, 2, 3, tiles, TILE, TILE), BF16),
        ],
        compiler_params=params(),
        cost_estimate=cost(20e9, 60e6),
        name="attend_forward",
    )(lengths, mixed, mixed, mixed)


def attend_back_kernel(maxlen, q_ref, k_ref, v_ref, ga_ref, attT_ref, inv_ref, keep_ref, d_ref, sum_ref, dqT):
    qs = q_ref[...] * jnp.asarray(HEAD**-0.5, BF16)
    v = v_ref[...]
    kT = k_ref[...].astype(F32).T.astype(BF16)
    gaT = ga_ref[...].astype(F32).T
    prod = gaT * attT_ref[...].astype(F32)
    half = lambda h: slice(h * HEAD, (h + 1) * HEAD)
    inv = [inv_ref[0, h : h + 1, :] for h in range(2)]
    gaT = jnp.concatenate([gaT[half(h)] * inv[h] for h in range(2)], axis=0)
    ga = gaT.T.astype(BF16)
    gaT = gaT.astype(BF16)
    lane = lax.broadcasted_iota(jnp.int32, (maxlen, PAIR), 1)
    blank = jnp.zeros((HEAD, maxlen), BF16)
    nil = jnp.zeros((), BF16)
    heads = []
    for h in range(2):
        mine = (lane < HEAD) if h == 0 else (lane >= HEAD)
        own = gaT[half(h)]
        heads.append(
            (
                jnp.where(mine, ga, nil), jnp.where(mine, qs, nil),
                jnp.concatenate([own, blank] if h == 0 else [blank, own], axis=0), kT[half(h)],
                jnp.sum(prod[half(h)], axis=0, keepdims=True) * inv[h],
            )
        )
    blocks = maxlen // TILE
    for j in range(blocks):
        lo, hi = j * TILE, (j + 1) * TILE
        dv = dk = None
        for h in range(2):
            ga_h, q_h, gaT_h, kT_h, delta = heads[h]
            side = lambda part: jnp.concatenate([keep_ref[0, h, part, tile_at(i, j)] for i in range(j, blocks)], axis=1)
            gw = mm_nn(v[lo:hi], gaT_h[:, lo:])
            ds = (gw * side(1).astype(F32) - side(2).astype(F32) * delta[:, lo:]).astype(BF16)
            dv_h = mm_nn(side(0), ga_h[lo:])
            dk_h = mm_nn(ds, q_h[lo:])
            dv = dv_h if dv is None else dv + dv_h
            dk = dk_h if dk is None else dk + dk_h
            dq_h = mm_nn(kT_h[:, lo:hi], ds)
            if j == 0:
                dqT[half(h), :] = dq_h
            else:
                dqT[half(h), lo:] += dq_h
        d_ref[2, lo:hi, :] = dv.astype(BF16)
        d_ref[1, lo:hi, :] = dk.astype(BF16)
        sums = [jnp.sum(d, axis=0, keepdims=True) for d in (dk, dv)]
        total = sums if j == 0 else [t + d for t, d in zip(total, sums)]
    dq = (dqT[...] * HEAD**-0.5).T
    d_ref[0] = dq.astype(BF16)
    total = [jnp.sum(dq, axis=0, keepdims=True)] + total
    sum_ref[0] = jnp.concatenate(total + [jnp.zeros((5, PAIR), F32)], axis=0)


def attend_backward(mixed, ga, attT, inv, keep, seqs, first, count):
    rows, width = mixed.shape[0], mixed.shape[1] // 3
    maxlen, pairs = rows // seqs, width // PAIR
    col = lambda part: pl.BlockSpec((maxlen, PAIR), lambda s, p: (s, part * pairs + p + first))
    return pl.pallas_call(
        functools.partial(attend_back_kernel, maxlen),
        grid=(seqs, count),
        in_specs=[
            col(0), col(1), col(2), col(0),
            pl.BlockSpec((PAIR, maxlen), lambda s, p: (p + first, s)),
            pl.BlockSpec((1, 8, maxlen), lambda s, p: (s * pairs + p + first, 0, 0)),
            pl.BlockSpec((1,) + keep.shape[1:], lambda s, p: (s * pairs + p + first, 0, 0, 0, 0, 0)),
        ],
        out_specs=[
            pl.BlockSpec((3, maxlen, PAIR), lambda s, p: (0, s, p)),
            pl.BlockSpec((1, 8, PAIR), lambda s, p: (s, 0, p)),
        ],
        out_shape=[
            jax.ShapeDtypeStruct((3, rows, count * PAIR), BF16),
            jax.ShapeDtypeStruct((seqs, 8, count * PAIR), F32),
        ],
        scratch_shapes=[pltpu.VMEM((PAIR, maxlen), F32)],
        compiler_params=params(40),
        cost_estimate=cost(5e9 * count, 10e6 * count),
        name="attend_backward",
    )(mixed, mixed, mixed, ga, attT, inv, keep)


def project_kernel(att_ref, x_ref, wp_ref, vec_ref, res_ref, n2_ref, wo_ref):
    pieces, per, _ = wp_ref.shape

    @pl.when(pl.program_id(0) == 0)
    def _():
        for p in range(pieces):
            wo_ref[p * per : (p + 1) * per, :] = wp_ref[p]

    residual = x_ref[...].astype(F32) + mm_nn(att_ref[...], wo_ref[...])
    res_ref[...] = residual
    xhat, rinv = norm_stats(residual)
    n2_ref[...] = (xhat * vec_ref[2:3, :] + vec_ref[3:4, :]).astype(BF16)


def project_out(att, tokens, wo_pieces, at, vecs, rows_block=512):
    rows, width = tokens.shape
    pieces = wo_pieces.shape[0]
    block = pl.BlockSpec((rows_block, width), lambda r: (r, 0))
    full = lambda a: pl.BlockSpec(a.shape, lambda r: (0,) * a.ndim)
    return pl.pallas_call(
        project_kernel,
        grid=(rows // rows_block,),
        in_specs=[
            block, block, pl.BlockSpec((pieces, width // pieces, width), lambda r: (0, at, 0)), full(vecs),
        ],
        out_specs=[block, block, pl.BlockSpec((width, width), lambda r: (0, 0))],
        out_shape=[
            jax.ShapeDtypeStruct((rows, width), F32),
            jax.ShapeDtypeStruct((rows, width), BF16),
            jax.ShapeDtypeStruct((width, width), BF16),
        ],
        compiler_params=params(),
        cost_estimate=cost(2 * rows * width * width, 10e6),
        name="project_out",
    )(att, tokens, wo_pieces, vecs)


def live_grad(cot, lengths_ref, maxlen, first_row):
    rows = cot.shape[0]
    at = first_row + lax.broadcasted_iota(jnp.int32, (rows, 1), 0)
    seq = first_row // maxlen
    return jnp.where(at - seq * maxlen < lengths_ref[seq], cot, 0.0)


def mlp_kernel(units, me_ref, n2_ref, gl_ref, w_ref, act_ref, gn_ref, *gw_refs):
    step = pl.program_id(0)
    rows, width = n2_ref.shape

    pieces = w_ref.shape[0]
    wu = w_ref[:, :units, :].reshape(pieces * units, width)
    wd = w_ref[:, units : 2 * units, :].reshape(pieces * units, width)
    n2, gl = n2_ref[...], gl_ref[...]
    u = mm_nt(n2, wu)
    uu = u * u
    th = jnp.tanh(u * (GELU_A + GELU_B * uu))
    half = 0.5 * u
    act = (half + half * th).astype(BF16)
    slope = 0.5 + 0.5 * th + (half - half * (th * th)) * (GELU_A + (3.0 * GELU_B) * uu)
    act_ref[...] = act
    gp = (mm_nt(gl, wd) * slope).astype(BF16)
    gn = mm_nn(gp, wu)

    @pl.when(step == 0)
    def _():
        gn_ref[...] = gn

    @pl.when(step > 0)
    def _():
        gn_ref[...] += gn

    for at, grad in ((0, mm_tn(gp, n2)), (units, mm_tn(act, gl))):
        grad = grad.astype(BF16)
        if len(gw_refs) == 1:
            gw_refs[0][:, at : at + units, :] = grad.reshape(pieces, units, width)
            continue
        grad = grad.reshape(pieces // 2, 2, units, width)
        core = lax.rem(me_ref[0], 2)
        near = lax.rem(lax.div(me_ref[0], 2), 4)
        for side in range(2):

            @pl.when(core == side)
            def _():
                for place in range(pieces // 2):
                    slot = (place // 4) * 4 + ((place % 4) ^ near)
                    gw_refs[0][slot, at : at + units, :] = grad[place, side]
                    gw_refs[1][slot, at : at + units, :] = grad[place, 1 - side]


def feed_forward(me, n2, gl, w, units, split):
    rows, width = n2.shape
    pieces, held, _ = w.shape
    take = max(1, 768 // units)
    full = lambda: pl.BlockSpec((rows, width), lambda f, *_: (0, 0))
    outs = 2 if split else 1
    grads = [pl.BlockSpec((take // outs, 2 * units, width), lambda f, *_: (f, 0, 0))] * outs
    return pl.pallas_call(
        functools.partial(mlp_kernel, units),
        grid_spec=pltpu.PrefetchScalarGridSpec(
            num_scalar_prefetch=1,
            grid=(pieces // take,),
            in_specs=[
                full(), full(), pl.BlockSpec((take, held, width), lambda f, *_: (f, 0, 0)),
            ],
            out_specs=[pl.BlockSpec((rows, take * units), lambda f, *_: (0, f)), full()] + grads,
        ),
        out_shape=[jax.ShapeDtypeStruct((rows, pieces * units), BF16), jax.ShapeDtypeStruct((rows, width), F32)]
        + [jax.ShapeDtypeStruct((pieces // outs, 2 * units, width), BF16)] * outs,
        compiler_params=params(50),
        cost_estimate=cost(10 * rows * width * pieces * units, 40e6),
        name="feed_forward",
    )(me, n2, gl, w)


def finish_kernel(units, act_ref, w_ref, res_ref, out_ref, acc_s):
    step = pl.program_id(0)
    pieces, _, width = w_ref.shape
    part = mm_nn(act_ref[...], w_ref[:, units : 2 * units, :].reshape(pieces * units, width))

    @pl.when(step == 0)
    def _():
        acc_s[...] = part + res_ref[...]

    @pl.when(step > 0)
    def _():
        acc_s[...] += part

    @pl.when(step == pl.num_programs(0) - 1)
    def _():
        out_ref[...] = acc_s[...].astype(BF16)


def finish_output(act, w, residual, units):
    rows, width = residual.shape
    pieces, held, _ = w.shape
    take = max(1, 768 // units)
    full = lambda: pl.BlockSpec((rows, width), lambda f: (0, 0))
    return pl.pallas_call(
        functools.partial(finish_kernel, units),
        grid=(pieces // take,),
        in_specs=[
            pl.BlockSpec((rows, take * units), lambda f: (0, f)),
            pl.BlockSpec((take, held, width), lambda f: (f, 0, 0)), full(),
        ],
        out_specs=full(),
        out_shape=jax.ShapeDtypeStruct((rows, width), BF16),
        scratch_shapes=[pltpu.VMEM((rows, width), F32)],
        compiler_params=params(),
        cost_estimate=cost(2 * rows * width * pieces * units, 20e6),
        name="finish_output",
    )(act, w, residual)


def norm_back(grad, xhat, rinv, gain):
    dh = grad * gain
    first = jnp.mean(dh, axis=-1, keepdims=True)
    second = jnp.mean(dh * xhat, axis=-1, keepdims=True)
    return rinv * (dh - first - xhat * second)


def middle_kernel(maxlen, len_ref, gn_ref, res_ref, cot_ref, att_ref, wo_ref, vec_ref, gres_ref, ga_ref, gwo_ref, gvec_ref, low_s):
    step = pl.program_id(0)
    rows = gn_ref.shape[0]
    gn = gn_ref[...]
    xhat, rinv = norm_stats(res_ref[...])
    gres = live_grad(cot_ref[...], len_ref, maxlen, step * rows) + norm_back(gn, xhat, rinv, vec_ref[2:3, :])
    gres_ref[...] = gres
    low = gres.astype(BF16)
    low_s[pl.ds(pl.multiple_of(step * rows, rows), rows), :] = low
    ga_ref[...] = mm_nt(low, wo_ref[...]).astype(BF16)

    @pl.when(step == 0)
    def _():
        gvec_ref[...] = jnp.zeros_like(gvec_ref)

    gvec_ref[0:1, :] += jnp.sum(gn * xhat, axis=0, keepdims=True)
    gvec_ref[1:2, :] += jnp.sum(gn, axis=0, keepdims=True)

    @pl.when(step == pl.num_programs(0) - 1)
    def _():
        gwo_ref[...] = mm_tn(att_ref[...], low_s[...]).astype(BF16)


def middle_back(lengths, gn, residual, cot, att, wo, vecs):
    rows, width = gn.shape
    rows_block = rows // lengths.shape[0]
    block = pl.BlockSpec((rows_block, width), lambda r, *_: (r, 0))
    full = lambda shape: pl.BlockSpec(shape, lambda r, *_: (0,) * len(shape))
    return pl.pallas_call(
        functools.partial(middle_kernel, rows // lengths.shape[0]),
        grid_spec=pltpu.PrefetchScalarGridSpec(
            num_scalar_prefetch=1,
            grid=(rows // rows_block,),
            in_specs=[block, block, block, full(att.shape), full(wo.shape), full(vecs.shape)],
            out_specs=[block, block, full(wo.shape), full((8, width))],
            scratch_shapes=[pltpu.VMEM((rows, width), BF16)],
        ),
        out_shape=[
            jax.ShapeDtypeStruct((rows, width), F32),
            jax.ShapeDtypeStruct((rows, width), BF16),
            jax.ShapeDtypeStruct(wo.shape, BF16),
            jax.ShapeDtypeStruct((8, width), F32),
        ],
        compiler_params=params(48),
        cost_estimate=cost(4 * rows * width * width, 30e6),
        name="middle_back",
    )(lengths, gn, residual, cot, att, wo, vecs)


def qkv_grad_kernel(masks, ppr, opr, me_ref, *refs):
    d1_ref, d2_ref, sum1_ref, sum2_ref, n1_ref, w_ref, gwo_ref, vec_ref, gvec2_ref, e_ref, keep_ref, send_ref, low_s, acc_s = refs
    rows, width = n1_ref.shape
    part = pl.program_id(0)
    n1 = n1_ref[...]
    paired, gshift, at = jnp.zeros((1, width), F32), jnp.zeros((8, width), F32), 0
    for d_ref, sum_ref in ((d1_ref, sum1_ref), (d2_ref, sum2_ref)):
        cols = d_ref.shape[2]
        gw = mm_tn(d_ref[0], n1)
        low_s[pl.ds(pl.multiple_of(part * width + at, PAIR), cols), :] = gw.astype(BF16)
        w = w_ref[at : at + cols, :]
        paired += jnp.sum(gw * w.astype(F32), axis=0, keepdims=True)
        total = jnp.sum(sum_ref[...], axis=0)
        pick = lax.broadcasted_iota(jnp.int32, (8, 1), 0) == part
        total = jnp.sum(jnp.where(pick, total, 0.0), axis=0, keepdims=True)
        high = total.astype(BF16).astype(F32)
        low = jnp.concatenate([high, total - high, jnp.zeros((6, cols), F32)], axis=0)
        gshift += mm_nn(low.astype(BF16), w)
        at += cols

    @pl.when(part == 0)
    def _():
        acc_s[...] = jnp.zeros_like(acc_s)

    acc_s[0:1, :] += paired
    acc_s[1:2, :] += gshift[0:1, :] + gshift[1:2, :]

    @pl.when(part == 2)
    def _():
        qkv_grad_pieces(masks, ppr, opr, me_ref, acc_s, gwo_ref, vec_ref, gvec2_ref, e_ref, keep_ref, send_ref, low_s)


def qkv_grad_pieces(masks, ppr, opr, me_ref, acc_s, gwo_ref, vec_ref, gvec2_ref, e_ref, keep_ref, send_ref, low_s):
    width = acc_s.shape[1]
    paired, gshift = acc_s[0:1, :], acc_s[1:2, :]
    ggain = (paired - vec_ref[1:2, :] * gshift) / vec_ref[0:1, :]
    n = 2 * len(masks)
    owner = lax.broadcasted_iota(jnp.int32, (n, width), 1) // opr == lax.broadcasted_iota(jnp.int32, (n, width), 0)
    packed = jnp.zeros((n, 128), F32)
    for v, row in enumerate((ggain, gshift, gvec2_ref[0:1, :], gvec2_ref[1:2, :])):
        packed += mm_nt(jnp.where(owner, row, 0.0).astype(BF16), e_ref[v])
    me = me_ref[0]
    core = lax.rem(me, 2)
    for pair in range(len(masks)):
        slot = slot_of(masks, me, pair)
        sides = []
        for j in (2 * pair, 2 * pair + 1):
            extra = jnp.concatenate([packed[j : j + 1, :], jnp.zeros((1, width - 128), F32)], axis=1)
            extra = jnp.concatenate([extra, jnp.zeros((7, width), F32)], axis=0)
            sides.append((low_s[j * ppr : (j + 1) * ppr, :], gwo_ref[j * opr : (j + 1) * opr, :], extra.astype(BF16)))
        for side in range(2):

            @pl.when(core == side)
            def _():
                for out, part in ((keep_ref, sides[side]), (send_ref, sides[1 - side])):
                    out[slot] = jnp.concatenate(part, axis=0)


def qkv_grad(plan, me, grads, sums, n1, w_abs, gwo, vecs, gvec2, spread):
    rows, width = n1.shape
    masks = plan.slot_masks()
    ppr, opr = 3 * width // plan.n, width // plan.n
    full = lambda a: pl.BlockSpec(a.shape, lambda p, *_: (0,) * len(a.shape))
    shape = jax.ShapeDtypeStruct((len(masks), ppr + opr + 8, width), BF16)
    return pl.pallas_call(
        functools.partial(qkv_grad_kernel, masks, ppr, opr),
        grid_spec=pltpu.PrefetchScalarGridSpec(
            num_scalar_prefetch=1,
            grid=(3,),
            in_specs=[pl.BlockSpec((1, rows, d.shape[2]), lambda p, *_: (p, 0, 0)) for d in grads]
            + [full(a) for a in (*sums, n1)]
            + [pl.BlockSpec((width, width), lambda p, *_: (p, 0))]
            + [full(a) for a in (gwo, vecs, gvec2, spread)],
            out_specs=[full(shape), full(shape)],
            scratch_shapes=[pltpu.VMEM((3 * width, width), BF16), pltpu.VMEM((8, width), F32)],
        ),
        out_shape=[shape, shape],
        compiler_params=params(40),
        cost_estimate=cost(6 * rows * width * width, 25e6),
        name="qkv_grad",
    )(me, *grads, *sums, n1, w_abs, gwo, vecs, gvec2, spread)


def qkv_grad_plain_kernel(d_ref, n1_ref, out_ref):
    out_ref[...] = mm_tn(d_ref[...], n1_ref[...]).astype(BF16)


def qkv_grad_plain(grads, n1):
    rows, width = n1.shape
    vm = pl.BlockSpec(memory_space=pltpu.VMEM)
    found = []
    for part in range(3):
        for d in grads:
            call = pl.pallas_call(
                qkv_grad_plain_kernel,
                in_specs=[vm, vm],
                out_specs=vm,
                out_shape=jax.ShapeDtypeStruct((d.shape[2], width), BF16),
                compiler_params=params(),
                name="qkv_grad_plain",
            )
            found.append(call(d[part], n1))
    return jnp.concatenate(found, axis=0)


def first_kernel(d1_ref, d2_ref, w_ref, x_ref, gres_ref, vec_ref, gtok_ref, gvec_ref):
    width = x_ref.shape[1]
    gn = jnp.zeros(x_ref.shape, F32)
    for part in range(3):
        at = part * width
        for ref in (d1_ref, d2_ref):
            gn += mm_nn(ref[part], w_ref[at : at + ref.shape[2], :])
            at += ref.shape[2]
    xhat, rinv = norm_stats(x_ref[...].astype(F32))
    gtok_ref[...] = gres_ref[...] + norm_back(gn, xhat, rinv, vec_ref[0:1, :])

    @pl.when(pl.program_id(0) == 0)
    def _():
        gvec_ref[...] = jnp.zeros_like(gvec_ref)

    gvec_ref[0:1, :] += jnp.sum(gn * xhat, axis=0, keepdims=True)
    gvec_ref[1:2, :] += jnp.sum(gn, axis=0, keepdims=True)


def first_back(grads, w_abs, tokens, gres, vecs, rows_block=256):
    rows, width = tokens.shape
    block = pl.BlockSpec((rows_block, width), lambda r: (r, 0))
    full = lambda shape: pl.BlockSpec(shape, lambda r: (0,) * len(shape))
    return pl.pallas_call(
        first_kernel,
        grid=(rows // rows_block,),
        in_specs=[pl.BlockSpec((3, rows_block, d.shape[2]), lambda r: (0, r, 0)) for d in grads]
        + [full(w_abs.shape), block, block, full(vecs.shape)],
        out_specs=[block, full((8, width))],
        out_shape=[jax.ShapeDtypeStruct((rows, width), F32), jax.ShapeDtypeStruct((8, width), F32)],
        compiler_params=params(),
        cost_estimate=cost(6 * rows * width * width, 25e6),
        name="first_back",
    )(*grads, w_abs, tokens, gres, vecs)


def body(plan, tokens, lengths, ln1_gain, ln1_shift, w_qkv, w_out, ln2_gain, ln2_shift, w_up, w_down, cot):
    rows, width = tokens.shape
    n = plan.n
    seqs = lengths.shape[0]
    me = lax.axis_index(AXES).astype(jnp.int32)
    me_arr = me[None]
    vec_piece = jnp.stack([ln1_gain, ln1_shift, ln2_gain, ln2_shift])
    per = vec_piece.shape[1]
    qkv_piece = w_qkv.T
    ppr, units = qkv_piece.shape[0], w_down.shape[0]
    ff = units * n

    mlp_piece = jnp.concatenate([w_up.T, w_down, w_out], axis=0)
    mlp_all = lax.all_gather(mlp_piece, AXES, axis=0, tiled=True).reshape(n, -1, width)
    if plan.direct:
        w_ff, ff_units, wo_pieces, wo_at = mlp_all, units, mlp_all, 2 * units // per
    else:
        ff_units = 768
        wo_pieces, wo_at = mlp_all[:, 2 * units :].reshape(1, width, width), 0
        w_ff = mlp_all[:, : 2 * units].reshape(n, 2, units, width).transpose(1, 0, 2, 3)
        w_ff = w_ff.reshape(2, ff // 768, 768, width).transpose(1, 0, 2, 3).reshape(ff // 768, 2 * 768, width)

    maxlen = rows // seqs
    live = (lax.iota(jnp.int32, maxlen)[None, :] < lengths[:, None]).reshape(rows, 1)
    grad_low = jnp.where(live, cot, 0.0).astype(BF16)
    if plan.direct:
        flat = jnp.pad(vec_piece.reshape(1, -1), ((0, 7), (0, width - 4 * per)))
        gathered = plan.gather(jnp.concatenate([qkv_piece, flat], axis=0))
        gathered, grad_low = lax.optimization_barrier((gathered, grad_low))
        slots = jnp.array(plan.slot_masks() + [m ^ 1 for m in plan.slot_masks()], jnp.int32)
        column = jnp.arange(width, dtype=jnp.int32)
        place = ((slots ^ me)[:, None] == (column // per)[None]).astype(F32)
        lane = jnp.arange(128, dtype=jnp.int32)
        spread = jnp.stack([(lane[:, None] == v * per + (column % per)[None]).astype(BF16) for v in range(4)])
        mixed, n1, w_abs, vecs = qkv_project(plan, me_arr, tokens, gathered, spread, place, ppr * n)
    else:
        w_abs = lax.all_gather(qkv_piece, AXES, axis=0, tiled=True)
        vecs = lax.all_gather(vec_piece, AXES, axis=1, tiled=True).astype(F32)
        vecs = jnp.pad(vecs, ((0, 4), (0, 0)))
        mixed, n1 = qkv_plain(tokens, w_abs, vecs)

    att, attT, inv, kept = attend_forward(mixed, lengths)
    residual, n2, wo = project_out(att, tokens, wo_pieces, wo_at, vecs)
    act, gn2, *gw_ff = feed_forward(me_arr, n2, grad_low, w_ff, ff_units, plan.direct)
    if plan.direct:
        got = plan.swap(gw_ff[1], 1)
    else:
        gw_ff = gw_ff[0].reshape(ff // 768, 2, 768, width).transpose(1, 0, 2, 3)
        gw_ff = gw_ff.reshape(2, n, units, width).transpose(1, 0, 2, 3).reshape(-1, width)
        g_ff = lax.psum_scatter(gw_ff, AXES, scatter_dimension=0, tiled=True)
    gres, ga, gwo, gvec2 = middle_back(lengths, gn2, residual, cot, att, wo, vecs)
    pairs = width // PAIR
    late = pairs // 6
    if plan.direct:
        ga, got, keep = lax.optimization_barrier((ga, got, gw_ff[0]))
        away = plan.first_away(keep, got)
        back = (plan.swap(away[0], 2), plan.swap(away[1], 4))
        ga, away = lax.optimization_barrier((ga, away))
    grads, sums = attend_backward(mixed, ga, attT, inv, kept, seqs, 0, pairs - late)
    if plan.direct:
        back, grads, ga, sums = lax.optimization_barrier((back, grads, ga, sums))
        away = plan.second_away(keep, got, back)
        again = (plan.swap(away[0], 4), plan.swap(away[1], 2))
        ga, away = lax.optimization_barrier((ga, away))
    more, late_sums = attend_backward(mixed, ga, attT, inv, kept, seqs, pairs - late, late)
    grads, sums = [grads, more], [sums, late_sums]
    if plan.direct:
        q_keep, q_send = qkv_grad(plan, me_arr, grads, sums, n1, w_abs, gwo, vecs, gvec2, spread)
        again, q_keep, q_send = lax.optimization_barrier((again, q_keep, q_send))
        whole, q_keep = lax.optimization_barrier((plan.last_sum(keep, got, back, again), q_keep))
        g_ff = plan.along_sum(whole)
        summed = plan.scatter_first(q_keep, q_send, 48)
        act, summed = lax.optimization_barrier((act, summed))
        output = finish_output(act, w_ff, residual, ff_units)
        g_attn, output, g_ff, gres = plan.scatter_rest(*summed, output, g_ff, gres)
        g_qkv, g_out = g_attn[:ppr], g_attn[ppr : ppr + per]
        g_vec = g_attn[ppr + per, : 4 * per].astype(F32).reshape(4, per)
    else:
        g_qkv = lax.psum_scatter(qkv_grad_plain(grads, n1), AXES, scatter_dimension=0, tiled=True)
        g_out = lax.psum_scatter(gwo, AXES, scatter_dimension=0, tiled=True)
    gtok, gvec1 = first_back(grads, w_abs, tokens, gres, vecs)
    if not plan.direct:
        output = finish_output(act, w_ff, residual, ff_units)
        gvec = jnp.concatenate([gvec1[:2], gvec2[:2]], axis=0)
        g_vec = lax.psum_scatter(gvec, AXES, scatter_dimension=1, tiled=True)
    return (
        output, gtok, g_vec[0], g_vec[1], g_qkv.astype(F32).T, g_out.astype(F32), g_vec[2], g_vec[3],
        g_ff[:units].astype(F32).T, g_ff[units:].astype(F32),
    )


def solution(mesh):
    both = AXES
    rows2, vec, cols2 = P(both, None), P(both), P(None, both)
    in_specs = (rows2, vec, vec, vec, cols2, rows2, vec, vec, cols2, rows2, rows2)
    out_specs = (rows2, rows2, vec, vec, cols2, rows2, vec, vec, cols2, rows2)
    return jax.shard_map(
        functools.partial(body, Plan(mesh)), mesh=mesh, in_specs=in_specs, out_specs=out_specs, check_vma=False
    )
```
